32 devices in a mesh: section: 2 (over x), expert: 8 (over z, core), dp: 2 (over y).
Axes of the slice: x: 2, y: 2, z: 4, core: 2. Of those that a mesh axis runs over, the one named last changes fastest.
Arguments:
- tokens: bfloat16 [2, 2048, 3584], P('section', ('expert', 'dp')), may hold values from -6 to 6
- grad_out: bfloat16 [2, 2048, 3584], P('section', ('expert', 'dp')), may hold values from -6 to 6
- expert_ids: int32 [2, 2048, 2], P('section', ('expert', 'dp')), may hold values from 0 to 3, all different within a row; in each aligned block of 128 rows (0 to 127, 128 to 255, ..., all dimensions but the last counted through in order) at most 65 rows name the same one
- gate_values: float32 [2, 2048, 2], P('section', ('expert', 'dp')), may hold values from 0.1 to 1
- w_in: bfloat16 [2, 8, 1792, 1024], P('section', 'expert', None, 'dp'), may hold values from -0.09375 to 0.09375
- w_out_t: bfloat16 [2, 8, 1792, 1024], P('section', 'expert', None, 'dp'), may hold values from -0.1875 to 0.1875
Outputs:
- handed_grad: bfloat16 [2, 2048, 3584], P('section', ('expert', 'dp'))
The draws below stay inside these ranges and needn't reach their ends.
Inputs may be any that keep to these rules, and one draw needn't show every extreme that they name: `expert_ids`: each token names 2 different experts; in each aligned block of 128 tokens (the tokens of one device) no expert is named more than 65 times, a bound that some block reaches.
All inputs are finite; a program needn't handle non-finite values.
Results may differ from the reference program's by a relative error of at most 0.0051.
Values may be sent and summed in bfloat16 or wider, within the bound.
No kernel may reach another device: no remote copies, remote signals or barrier semaphores. Data moves between devices by JAX's collectives and lax.ppermute only.
A program may use at most 128 MiB of HBM per device.

```python
import math
import jax
import jax.numpy as jnp
import numpy as np
from jax import lax

D = 3584
FF = 1024
TOP = 2
TOK_DEV = 128
EXPERTS = 4
CAP = 65
TOKENS = 2048
N_SECTION = 2


def block_scale(own_key, dims, cuts, least, top_value):
    def one(dim, blocks):
        steps = jax.random.uniform(jax.random.fold_in(jax.random.fold_in(own_key, 6), dim), (blocks,), jnp.float32, least / len(cuts), top_value / len(cuts))
        return jnp.repeat(jnp.exp(steps), dims[dim] // blocks).reshape((-1,) + (1,) * (len(dims) - dim - 1))

    loudness = one(*cuts[0])
    for cut in cuts[1:]:
        loudness = loudness * one(*cut)
    return loudness


def deal_out(key, own, number, rows, number_of, top, limit, slope):
    ranking = jax.random.permutation(key, number_of)
    heavy_load, common = shares(number_of, rows * top, limit, slope, True), shares(number_of, rows * top, limit, slope, False)
    places = jnp.arange(number_of)

    def named(tallies, turn):
        used = int((tallies > 0).sum())
        fixed = max(1, used // 4)
        passed = fixed + (places - fixed + turn * (used - fixed)) % max(1, number_of - fixed)
        return jnp.zeros((number_of,), jnp.int32).at[ranking[jnp.where(places < fixed, places, passed)]].set(jnp.asarray(tallies, jnp.int32))

    tallies = jnp.where(number % 4 == 0, named(heavy_load, number // 4), named(common, number - number // 4 - 1))
    mixed = jax.random.permutation(jax.random.fold_in(own, 3), number_of)
    source_of, sink = mixed[0:number_of // 2 * 2:2], mixed[1:number_of // 2 * 2:2]
    room = jnp.minimum(tallies[source_of] - 1, limit - tallies[sink]) // 2
    room = jnp.where((source_of == ranking[0]) | (sink == ranking[0]) | (tallies[sink] == 0), 0, jnp.maximum(room, 0))
    passed = jax.random.randint(jax.random.fold_in(own, 4), (number_of // 2,), 0, 1 << 20) % (room + 1)
    tallies = tallies.at[source_of].add(-passed).at[sink].add(passed)
    members = jnp.searchsorted(jnp.cumsum(tallies), jnp.arange(rows * top), side="right").astype(jnp.int32)
    grid = members.reshape(top, rows).T
    grid = grid[jax.random.permutation(jax.random.fold_in(own, 1), rows)]
    turn = jax.random.randint(jax.random.fold_in(own, 2), (rows, 1), 0, top)
    return jnp.take_along_axis(grid, (jnp.arange(top)[None, :] + turn) % top, axis=1)


def shares(number_of, total, most, skew, full):
    weights = [(1 << 20) // math.isqrt(grade ** skew) + 1 for grade in range(1, number_of + 1)]
    largest = most if full else min(most, max(-(-total // number_of), total * weights[0] // sum(weights)))
    least = 1 if total - largest >= number_of - 1 else 0
    counts, spare = [largest] + [least] * (number_of - 1), total - largest - least * (number_of - 1)
    while spare > 0:
        candidates = [i for i in range(1, number_of) if counts[i] < largest] or [i for i in range(1, number_of) if counts[i] < most]
        whole, left = sum([weights[i] for i in candidates]), spare
        for i in candidates:
            addition = min(most - counts[i], max(1, left * weights[i] // whole), spare)
            counts[i] = counts[i] + addition
            spare = spare - addition
    return np.array(counts)


def gaussian(own_key, extent, deviation, most, shards=(), kind=jnp.bfloat16):
    drawn = jax.random.normal(own_key, extent, jnp.float32) * deviation
    if len(shards) > 0:
        drawn = block_scale(own_key, extent, shards, -0.22, 0.18) * drawn
    return jnp.clip(drawn, min=-most, max=most).astype(kind)


def setup_inputs(seed: int = 0) -> dict:
    splits = jax.random.split(jax.random.key(seed), 7)
    tokens = gaussian(splits[0], (N_SECTION, TOKENS, D), 1.0, 6.0, ((0, 2), (1, 16)))
    grad_out = gaussian(splits[1], (N_SECTION, TOKENS, D), 1.0, 6.0, ((0, 2), (1, 16)))
    expert_ids_keys = jax.random.split(jax.random.fold_in(splits[2], 1), N_SECTION * TOKENS // TOK_DEV)
    expert_ids_turns = jax.random.permutation(jax.random.fold_in(splits[2], 3), N_SECTION * TOKENS // TOK_DEV)
    expert_ids = jax.vmap(lambda own, number: deal_out(jax.random.fold_in(splits[2], 2), own, number, TOK_DEV, EXPERTS, TOP, CAP, 1))(expert_ids_keys, expert_ids_turns).reshape((N_SECTION, TOKENS, TOP))
    gate_values = jnp.clip(0.1 + 0.9 * jax.random.uniform(splits[3], (N_SECTION, TOKENS, TOP), jnp.float32) ** block_scale(splits[3], (N_SECTION, TOKENS, TOP), ((0, 2), (1, 16)), -0.2, 0.2), 0.1, 1.0)
    w_in = gaussian(splits[4], (N_SECTION, 2 * EXPERTS, D // 2, FF), D ** -0.5, 0.09375, ((0, 2), (1, 8), (3, 2)))
    w_out_t = gaussian(splits[5], (N_SECTION, 2 * EXPERTS, D // 2, FF), FF ** -0.5, 0.1875, ((0, 2), (1, 8), (3, 2)))
    return {"tokens": tokens, "grad_out": grad_out, "expert_ids": expert_ids, "gate_values": gate_values, "w_in": w_in, "w_out_t": w_out_t}


def rounded(value):
    return lax.optimization_barrier(value.astype(jnp.bfloat16)).astype(jnp.float32)

def silu_slope(pre):
    sig = jax.nn.sigmoid(pre)
    return sig * (1.0 + pre * (1.0 - sig))

def section_grad(tokens, grad_out, expert_ids, gate_values, w_in, w_out_t):
    flat_ids = expert_ids.reshape(-1).astype(jnp.int32)
    total_rows = flat_ids.shape[0]
    per_block = TOK_DEV * TOP
    blocks = total_rows // per_block
    onehot = (flat_ids[:, None] == jnp.arange(EXPERTS, dtype=jnp.int32)[None, :]).astype(jnp.int32)
    onehot = onehot.reshape(blocks, per_block, EXPERTS)
    before = jnp.cumsum(onehot, axis=1) - onehot
    rank = lax.optimization_barrier(jnp.sum(before * onehot, axis=2)).reshape(-1).astype(jnp.int32)
    block_of = jnp.arange(total_rows, dtype=jnp.int32) // per_block
    table = jnp.full((EXPERTS, blocks * CAP), -1, jnp.int32)
    table = table.at[flat_ids, block_of * CAP + rank].set(jnp.arange(total_rows, dtype=jnp.int32))
    half = D // 2
    w_pairs = w_in.reshape(EXPERTS, D, FF)
    v_pairs = w_out_t.reshape(EXPERTS, D, FF)
    grad32 = grad_out.astype(jnp.float32)
    gate_flat = gate_values.reshape(-1)

    def one_expert(total, inputs):
        slots, w_one, v_one = inputs
        valid = slots >= 0
        row_index = jnp.where(valid, slots, 0).astype(jnp.int32)
        token_index = (row_index // TOP).astype(jnp.int32)
        gate = jnp.where(valid, gate_flat[row_index], 0.0)
        x_rows = tokens[token_index].astype(jnp.float32)
        g_rows = rounded(gate[:, None] * grad32[token_index])
        w32 = w_one.astype(jnp.float32)
        v32 = v_one.astype(jnp.float32)
        pre = rounded(x_rows[:, :half] @ w32[:half]) + rounded(x_rows[:, half:] @ w32[half:])
        hid = rounded(g_rows[:, :half] @ v32[:half]) + rounded(g_rows[:, half:] @ v32[half:])
        act = rounded(hid * silu_slope(pre))
        back = rounded(act @ w32.T) * valid[:, None].astype(jnp.float32)
        return (total.at[token_index].add(back), None)
    start = jnp.zeros(tokens.shape, jnp.float32)
    total, _ = lax.scan(one_expert, start, (table, w_pairs, v_pairs))
    return (grad32 + total).astype(jnp.bfloat16)

def reference(tokens, grad_out, expert_ids, gate_values, w_in, w_out_t):
    first = section_grad(tokens[0], grad_out[0], expert_ids[0], gate_values[0], w_in[0], w_out_t[0])
    second = section_grad(tokens[1], grad_out[1], expert_ids[1], gate_values[1], w_in[1], w_out_t[1])
    return jnp.stack([second, first])
```

```python
import functools

import jax
import jax.numpy as jnp
from jax import lax
from jax.experimental import pallas as pl
from jax.experimental.pallas import tpu as pltpu
from jax.sharding import PartitionSpec as P

LANES = 128
TILE = 256
F32 = jnp.float32
BF16 = jnp.bfloat16
MIB = 1 << 20


def slots_of(tok_dev, top, experts):
    capacity = min(tok_dev, max(2, tok_dev * top // experts + 1))
    if capacity % 16 == 1 and capacity > 1:
        return capacity - 1, 1
    return -(-capacity // 16) * 16, 0


def fold_columns(pieces, base):
    return -(-pieces // base) * LANES


def fold(ext_ref, row, pieces, first, base):
    for k in range(pieces):
        at = first + k
        column = at // base * LANES
        ext_ref[at % base : at % base + 1, column : column + LANES] = row[:, k * LANES : (k + 1) * LANES]


def unfold(row_ref, at_row, ext, pieces, first, base):
    for k in range(pieces):
        at = first + k
        column = at // base * LANES
        row_ref[at_row : at_row + 1, k * LANES : (k + 1) * LANES] = ext[
            at % base : at % base + 1, column : column + LANES
        ]


def slot_row(ids, expert):
    tokens = ids.shape[1]
    hit = jnp.where(ids == expert, 1.0, 0.0).astype(F32)
    mask = jnp.sum(hit, axis=0, keepdims=True)
    earlier = lax.broadcasted_iota(jnp.int32, (tokens, tokens), 0) < lax.broadcasted_iota(
        jnp.int32, (tokens, tokens), 1
    )
    before = jnp.dot(
        jnp.broadcast_to(mask, (16, tokens)).astype(BF16),
        jnp.where(earlier, 1.0, 0.0).astype(BF16),
        preferred_element_type=F32,
    )[0:1]
    return jnp.where(mask > 0.5, before, -1.0)


def dispatch_kernel(dists, base, extra, ids_ref, gates_ref, tok_ref, grad_ref, *refs):
    outs, ext_ref = refs[: len(dists)], refs[len(dists)]
    here = lax.axis_index("expert") // 2
    ids, gates = ids_ref[...], gates_ref[...]
    tokens, width = tok_ref.shape
    pieces = width // LANES
    rows = base + 16 * extra
    for dist, out in zip(dists, outs):
        expert = here ^ dist
        slot = slot_row(ids, expert)
        gate = jnp.sum(jnp.where(ids == expert, gates, 0.0), axis=0, keepdims=True)
        picks = lax.broadcasted_iota(jnp.int32, (rows, tokens), 0).astype(F32) == slot
        onehot = jnp.where(picks, 1.0, 0.0).astype(BF16)
        scale = jnp.sum(jnp.where(picks, gate, 0.0), axis=1, keepdims=True)
        if extra:
            ext_ref[...] = jnp.zeros_like(ext_ref)
        for at in range(0, width, 512):
            cols = slice(at, at + 512)
            x = jnp.dot(onehot, tok_ref[:, cols], preferred_element_type=F32)
            g = jnp.dot(onehot, grad_ref[:, cols], preferred_element_type=F32) * scale
            out[:, cols] = x[:base].astype(BF16)
            out[:, width + at : width + at + 512] = g[:base].astype(BF16)
            if extra:
                fold(ext_ref, x[base : base + 1], 4, at // LANES, base)
                fold(ext_ref, g[base : base + 1], 4, pieces + at // LANES, base)
        if extra:
            out[:, 2 * width :] = ext_ref[...].astype(BF16)


def dispatch(dists, base, extra, ids_t, gates_t, tok, grad):
    tokens, width = tok.shape
    ext = fold_columns(2 * width // LANES, base)
    cols = 2 * width + extra * ext
    vmem = pl.BlockSpec(memory_space=pltpu.VMEM)
    return pl.pallas_call(
        functools.partial(dispatch_kernel, dists, base, extra),
        out_shape=[jax.ShapeDtypeStruct((base, cols), BF16) for _ in dists],
        in_specs=[vmem] * 4,
        out_specs=[vmem] * len(dists),
        scratch_shapes=[pltpu.VMEM((base, ext), F32)],
        compiler_params=pltpu.CompilerParams(vmem_limit_bytes=24 * MIB),
        cost_estimate=pl.CostEstimate(
            flops=4 * len(dists) * (base + 16) * tokens * width,
            bytes_accessed=4 * tokens * width + 2 * len(dists) * base * cols,
            transcendentals=0,
        ),
        name="dispatch",
    )(ids_t, gates_t, tok, grad)


def silu_slope(pre):
    sig = jax.nn.sigmoid(pre)
    return sig * (1.0 + pre * (1.0 - sig))


def expert_kernel(n, base, extra, shards, *refs):
    msgs, refs = refs[:n], refs[n:]
    w_shards, v_shards, refs = refs[:shards], refs[shards : 2 * shards], refs[2 * shards :]
    outs, refs = refs[:n], refs[n:]
    w, v, x, g, slope, act, ext, row32, ext32, sem_x, sem_g, sem_e, sem_w, sem_v = refs
    width, ff = w.shape
    parts = shards // 2
    half, fh = width // 2, ff // parts
    pieces = width // LANES
    full = n * base
    core = lax.axis_index("expert") % 2

    def start(src, dst, sem):
        copy = pltpu.make_async_copy(src, dst, sem)
        copy.start()
        return copy

    x_in, g_in, e_in = [], [], []
    for i in range(n):
        rows = pl.ds(i * base, base)
        x_in.append(start(msgs[i].at[:, pl.ds(0, width)], x.at[rows, :], sem_x.at[i]))
        if extra:
            e_in.append(start(msgs[i].at[:, pl.ds(2 * width, ext.shape[2])], ext.at[i], sem_e.at[i]))

    def shards_in(given, whole, sems):
        copies = []
        for y in range(parts):
            for c in range(2):
                at = pl.multiple_of((core if c == 0 else 1 - core) * half, half)
                copies.append(
                    start(given[2 * y + c], whole.at[pl.ds(at, half), pl.ds(y * fh, fh)], sems.at[2 * y + c])
                )
        return copies

    w_in = shards_in(w_shards, w, sem_w)
    for i in range(n):
        g_in.append(start(msgs[i].at[:, pl.ds(width, width)], g.at[pl.ds(i * base, base), :], sem_g.at[i]))
    v_in = shards_in(v_shards, v, sem_v)

    def put_extra(rows_ref, first):
        row32[...] = jnp.zeros_like(row32)
        for i in range(n):
            unfold(row32, i, ext[i].astype(F32), pieces, first, base)
        rows_ref[full:, :] = row32[...].astype(BF16)

    for copy in x_in + e_in:
        copy.wait()
    if extra:
        put_extra(x, 0)
    for y in range(parts):
        for copy in w_in[2 * y : 2 * y + 2]:
            copy.wait()
        for at in range(y * fh, (y + 1) * fh, TILE):
            cols = slice(at, at + TILE)
            slope[:, cols] = silu_slope(jnp.dot(x[...], w[:, cols], preferred_element_type=F32))
    for copy in g_in:
        copy.wait()
    if extra:
        put_extra(g, pieces)
    for y in range(parts):
        for copy in v_in[2 * y : 2 * y + 2]:
            copy.wait()
        for at in range(y * fh, (y + 1) * fh, TILE):
            cols = slice(at, at + TILE)
            hid = jnp.dot(g[...], v[:, cols], preferred_element_type=F32)
            act[:, cols] = (hid * slope[:, cols]).astype(BF16)
    if extra:
        ext32[...] = jnp.zeros_like(ext32)
    for at in range(0, width, TILE):
        back = lax.dot_general(
            act[...], w[at : at + TILE, :], (((1,), (1,)), ((), ())), preferred_element_type=F32
        )
        for i in range(n):
            outs[i][:, at : at + TILE] = back[i * base : (i + 1) * base].astype(BF16)
            if extra:
                fold(ext32.at[i], back[full + i : full + i + 1], TILE // LANES, at // LANES, base)
    if extra:
        for i in range(n):
            outs[i][:, width:] = ext32[i].astype(BF16)


def expert(msgs, base, extra, w_shards, v_shards):
    n = len(msgs)
    half, fh = w_shards[0].shape
    shards = len(w_shards)
    width, ff = 2 * half, shards // 2 * fh
    rows = n * base + -(-n * extra // 16) * 16
    ext = fold_columns(2 * width // LANES, base)
    back_ext = fold_columns(width // LANES, base)
    cols = width + extra * back_ext
    anywhere, vmem = pl.BlockSpec(memory_space=pl.ANY), pl.BlockSpec(memory_space=pltpu.VMEM)
    spare = max(16, rows - n * base)
    return pl.pallas_call(
        functools.partial(expert_kernel, n, base, extra, shards),
        out_shape=[jax.ShapeDtypeStruct((base, cols), BF16) for _ in msgs],
        in_specs=[anywhere] * (n + 2 * shards),
        out_specs=[vmem] * n,
        scratch_shapes=[
            pltpu.VMEM((width, ff), BF16),
            pltpu.VMEM((width, ff), BF16),
            pltpu.VMEM((rows, width), BF16),
            pltpu.VMEM((rows, width), BF16),
            pltpu.VMEM((rows, ff), F32),
            pltpu.VMEM((rows, ff), BF16),
            pltpu.VMEM((n, base, ext), BF16),
            pltpu.VMEM((spare, width), F32),
            pltpu.VMEM((n, base, back_ext), F32),
            pltpu.SemaphoreType.DMA((n,)),
            pltpu.SemaphoreType.DMA((n,)),
            pltpu.SemaphoreType.DMA((n,)),
            pltpu.SemaphoreType.DMA((shards,)),
            pltpu.SemaphoreType.DMA((shards,)),
        ],
        compiler_params=pltpu.CompilerParams(vmem_limit_bytes=40 * MIB),
        cost_estimate=pl.CostEstimate(
            flops=6 * rows * width * ff,
            bytes_accessed=4 * width * ff + 6 * rows * width,
            transcendentals=rows * ff,
        ),
        name="expert",
    )(*msgs, *w_shards, *v_shards)


def combine_kernel(dists, base, extra, ids_ref, grad_ref, *refs):
    n = len(dists)
    msgs, (out, rows, ext, row32, sem_b, sem_e) = refs[:n], refs[n:]
    tokens, width = grad_ref.shape
    pieces = width // LANES
    full = n * base
    here = lax.axis_index("expert") // 2
    copies = []
    for i in range(n):
        copies.append(
            pltpu.make_async_copy(msgs[i].at[:, pl.ds(0, width)], rows.at[pl.ds(i * base, base), :], sem_b.at[i])
        )
        if extra:
            copies.append(
                pltpu.make_async_copy(msgs[i].at[:, pl.ds(width, ext.shape[2])], ext.at[i], sem_e.at[i])
            )
    for copy in copies:
        copy.start()
    ids = ids_ref[...]
    places = []
    overflow = jnp.zeros((tokens, 16), F32)
    for i, dist in enumerate(dists):
        slot = jnp.transpose(jnp.broadcast_to(slot_row(ids, here ^ dist), (LANES, tokens)))
        slot = slot[:, 0:1]
        at = lax.broadcasted_iota(jnp.int32, (tokens, base), 1).astype(F32)
        places.append(jnp.where(at == slot, 1.0, 0.0).astype(BF16))
        if extra:
            mine = lax.broadcasted_iota(jnp.int32, (tokens, 16), 1) == i
            overflow = overflow + jnp.where(mine & (slot == float(base)), 1.0, 0.0)
    for copy in copies:
        copy.wait()
    if extra:
        row32[...] = jnp.zeros_like(row32)
        for i in range(n):
            unfold(row32, i, ext[i].astype(F32), pieces, 0, base)
        rows[full:, :] = row32[...].astype(BF16)
    overflow = overflow.astype(BF16)
    for at in range(0, width, 512):
        cols = slice(at, at + 512)
        total = grad_ref[:, cols].astype(F32)
        for i in range(n):
            total = total + jnp.dot(
                places[i], rows[i * base : (i + 1) * base, cols], preferred_element_type=F32
            )
        if extra:
            total = total + jnp.dot(overflow, rows[full:, cols], preferred_element_type=F32)
        out[:, cols] = total.astype(BF16)


def combine(dists, base, extra, ids_t, grad, msgs):
    n = len(dists)
    tokens, width = grad.shape
    rows = n * base + 16 * extra
    ext = fold_columns(width // LANES, base)
    anywhere, vmem = pl.BlockSpec(memory_space=pl.ANY), pl.BlockSpec(memory_space=pltpu.VMEM)
    return pl.pallas_call(
        functools.partial(combine_kernel, dists, base, extra),
        out_shape=jax.ShapeDtypeStruct((tokens, width), BF16),
        in_specs=[vmem, vmem] + [anywhere] * n,
        out_specs=vmem,
        scratch_shapes=[
            pltpu.VMEM((rows, width), BF16),
            pltpu.VMEM((n, base, ext), BF16),
            pltpu.VMEM((16, width), F32),
            pltpu.SemaphoreType.DMA((n,)),
            pltpu.SemaphoreType.DMA((n,)),
        ],
        compiler_params=pltpu.CompilerParams(vmem_limit_bytes=24 * MIB),
        cost_estimate=pl.CostEstimate(
            flops=2 * rows * tokens * width,
            bytes_accessed=2 * rows * width + 4 * tokens * width,
            transcendentals=0,
        ),
        name="combine",
    )(ids_t, grad, *msgs)


def swap(value, axis, apart):
    return lax.ppermute(value, axis, [(i, i ^ apart) for i in range(lax.axis_size(axis))])


def swap_back(value, apart):
    sections, places = lax.axis_size("section"), lax.axis_size("expert")
    pairs = [
        (s * places + i, (s ^ 1) * places + (i ^ apart)) for s in range(sections) for i in range(places)
    ]
    return lax.ppermute(value, ("section", "expert"), pairs)


def groups_of(experts):
    if experts == 4:
        return [[2], [3], [1, 0]]
    order = list(range(experts - 1, -1, -1))
    size = -(-experts // 4)
    return [order[i : i + size] for i in range(0, experts, size)]


def body(tokens, grad_out, expert_ids, gate_values, w_in, w_out_t):
    tok, grad = tokens[0], grad_out[0]
    ids_t, gates_t = expert_ids[0].T, gate_values[0].T
    experts = lax.axis_size("expert") // 2
    base, extra = slots_of(tok.shape[0], ids_t.shape[0], experts)
    groups = groups_of(experts)
    w_own, v_own = w_in[0, 0], w_out_t[0, 0]
    w_columns = [w_own] + [swap(w_own, "dp", apart) for apart in range(1, lax.axis_size("dp"))]
    v_columns = [v_own] + [swap(v_own, "dp", apart) for apart in range(1, lax.axis_size("dp"))]
    sent = [dispatch(group, base, extra, ids_t, gates_t, tok, grad) for group in groups]
    got = [
        [swap(msg, "expert", 2 * dist) if dist else msg for dist, msg in zip(group, msgs)]
        for group, msgs in zip(groups, sent)
    ]
    w_shards = [shard for own in w_columns for shard in (own, swap(own, "expert", 1))]
    v_shards = [shard for own in v_columns for shard in (own, swap(own, "expert", 1))]
    other_grad, other_ids = swap(grad, "section", 1), swap(ids_t, "section", 1)
    dists, returned = [], []
    for group, msgs in zip(groups, got):
        backs = expert(msgs, base, extra, w_shards, v_shards)
        dists += group
        returned += [swap_back(back, 2 * dist) for dist, back in zip(group, backs)]
    return combine(dists, base, extra, other_ids, other_grad, returned)[None]


def solution(mesh):
    rows = P("section", ("expert", "dp"), None)
    weights = P("section", "expert", None, "dp")
    return jax.shard_map(
        body,
        mesh=mesh,
        in_specs=(rows, rows, rows, rows, weights, weights),
        out_specs=rows,
        check_vma=False,
    )
```

```python
import functools

import jax
import jax.numpy as jnp
from jax import lax
from jax.experimental import pallas as pl
from jax.experimental.pallas import tpu as pltpu
from jax.sharding import PartitionSpec as P

LANES = 128
TILE = 256
F32 = jnp.float32
BF16 = jnp.bfloat16
MIB = 1 << 20


def slots_of(tok_dev, top, experts):
    capacity = min(tok_dev, max(2, tok_dev * top // experts + 1))
    if capacity % 16 == 1 and capacity > 1:
        return capacity - 1, 1
    return -(-capacity // 16) * 16, 0


def fold_columns(pieces, base):
    return -(-pieces // base) * LANES


def fold(ext_ref, row, pieces, first, base):
    for k in range(pieces):
        at = first + k
        column = at // base * LANES
        ext_ref[at % base : at % base + 1, column : column + LANES] = row[:, k * LANES : (k + 1) * LANES]


def unfold(row_ref, at_row, ext, pieces, first, base):
    for k in range(pieces):
        at = first + k
        column = at // base * LANES
        row_ref[at_row : at_row + 1, k * LANES : (k + 1) * LANES] = ext[
            at % base : at % base + 1, column : column + LANES
        ]


def slot_row(ids, expert):
    tokens = ids.shape[1]
    hit = jnp.where(ids == expert, 1.0, 0.0).astype(F32)
    mask = jnp.sum(hit, axis=0, keepdims=True)
    earlier = lax.broadcasted_iota(jnp.int32, (tokens, tokens), 0) < lax.broadcasted_iota(
        jnp.int32, (tokens, tokens), 1
    )
    before = jnp.dot(
        jnp.broadcast_to(mask, (16, tokens)).astype(BF16),
        jnp.where(earlier, 1.0, 0.0).astype(BF16),
        preferred_element_type=F32,
    )[0:1]
    return jnp.where(mask > 0.5, before, -1.0)


def dispatch_kernel(dists, base, extra, ids_ref, gates_ref, tok_ref, grad_ref, *refs):
    outs, ext_ref = refs[: len(dists)], refs[len(dists)]
    here = lax.axis_index("expert") // 2
    ids, gates = ids_ref[...], gates_ref[...]
    tokens, width = tok_ref.shape
    pieces = width // LANES
    rows = base + 16 * extra
    for dist, out in zip(dists, outs):
        expert = here ^ dist
        slot = slot_row(ids, expert)
        gate = jnp.sum(jnp.where(ids == expert, gates, 0.0), axis=0, keepdims=True)
        picks = lax.broadcasted_iota(jnp.int32, (rows, tokens), 0).astype(F32) == slot
        onehot = jnp.where(picks, 1.0, 0.0).astype(BF16)
        scale = jnp.sum(jnp.where(picks, gate, 0.0), axis=1, keepdims=True)
        if extra:
            ext_ref[...] = jnp.zeros_like(ext_ref)
        for at in range(0, width, 512):
            cols = slice(at, at + 512)
            x = jnp.dot(onehot, tok_ref[:, cols], preferred_element_type=F32)
            g = jnp.dot(onehot, grad_ref[:, cols], preferred_element_type=F32) * scale
            out[:, cols] = x[:base].astype(BF16)
            out[:, width + at : width + at + 512] = g[:base].astype(BF16)
            if extra:
                fold(ext_ref, x[base : base + 1], 4, at // LANES, base)
                fold(ext_ref, g[base : base + 1], 4, pieces + at // LANES, base)
        if extra:
            out[:, 2 * width :] = ext_ref[...].astype(BF16)


def dispatch(dists, base, extra, ids_t, gates_t, tok, grad):
    tokens, width = tok.shape
    ext = fold_columns(2 * width // LANES, base)
    cols = 2 * width + extra * ext
    vmem = pl.BlockSpec(memory_space=pltpu.VMEM)
    return pl.pallas_call(
        functools.partial(dispatch_kernel, dists, base, extra),
        out_shape=[jax.ShapeDtypeStruct((base, cols), BF16) for _ in dists],
        in_specs=[vmem] * 4,
        out_specs=[vmem] * len(dists),
        scratch_shapes=[pltpu.VMEM((base, ext), F32)],
        compiler_params=pltpu.CompilerParams(vmem_limit_bytes=60 * MIB),
        cost_estimate=pl.CostEstimate(
            flops=4 * len(dists) * (base + 16) * tokens * width,
            bytes_accessed=4 * tokens * width + 2 * len(dists) * base * cols,
            transcendentals=0,
        ),
        name="dispatch",
    )(ids_t, gates_t, tok, grad)


def silu_slope(pre):
    sig = jax.nn.sigmoid(pre)
    return sig * (1.0 + pre * (1.0 - sig))


def begin(src, dst, sem):
    copy = pltpu.make_async_copy(src, dst, sem)
    copy.start()
    return copy


def begin_weights(pieces, layout, whole, sems):
    half = whole.shape[0] // 2
    core = lax.axis_index("expert") % 2
    copies = {}
    for i, (piece, (block, other, row, columns)) in enumerate(zip(pieces, layout)):
        at = pl.multiple_of((1 - core if other else core) * half + row, 16)
        rows = pl.ds(at, piece.shape[0])
        dst = whole.at[rows, pl.ds(block * columns, columns)]
        copies.setdefault(block, []).append(begin(piece, dst, sems.at[i]))
    return copies


def begin_rows(msgs, rows, ext, start, sems, ext_sems):
    base = msgs[0].shape[0]
    width = rows.shape[1]
    copies = []
    for i, msg in enumerate(msgs):
        copies.append(begin(msg.at[:, pl.ds(start, width)], rows.at[pl.ds(i * base, base), :], sems.at[i]))
        if ext is not None:
            copies.append(begin(msg.at[:, pl.ds(2 * width, ext.shape[2])], ext.at[i], ext_sems.at[i]))
    return copies


def finish(copies):
    for copy in copies:
        copy.wait()


def put_extra(rows, row32, ext, n, base, first):
    row32[...] = jnp.zeros_like(row32)
    for i in range(n):
        unfold(row32, i, ext[i].astype(F32), rows.shape[1] // LANES, first, base)
    rows[n * base :, :] = row32[...].astype(BF16)


def expert_kernel(n, base, extra, stage, w_layout, v_layout, *refs):
    msgs, refs = refs[:n], refs[n:]
    w_pieces, refs = refs[: len(w_layout)], refs[len(w_layout) :]
    v_pieces, refs = refs[: len(v_layout)], refs[len(v_layout) :]
    if stage == "late":
        slope, partial, refs = refs[0], refs[1], refs[2:]
        outs, refs = refs[:n], refs[n:]
    elif stage == "early":
        slope_late, partial_out, slope, refs = refs[0], refs[1], refs[2], refs[3:]
    else:
        outs, slope, refs = refs[:n], refs[n], refs[n + 1 :]
    w, v, x, g, act, ext, row32, ext32, sem_x, sem_g, sem_e, sem_w, sem_v = refs
    width = w.shape[0]
    half_ff = w_layout[0][3]
    pieces = width // LANES
    full = n * base
    x_in = []
    if stage != "late":
        x_in = begin_rows(msgs, x, ext if extra else None, 0, sem_x, sem_e)
    w_in = begin_weights(w_pieces, w_layout, w, sem_w)
    g_in = begin_rows(msgs, g, ext if extra and stage == "late" else None, width, sem_g, sem_e)
    v_in = begin_weights(v_pieces, v_layout, v, sem_v)
    if stage != "late":
        finish(x_in)
        if extra:
            put_extra(x, row32, ext, n, base, 0)
        for block in sorted(w_in):
            finish(w_in[block])
            for at in range(block * half_ff, (block + 1) * half_ff, TILE):
                value = silu_slope(jnp.dot(x[...], w[:, at : at + TILE], preferred_element_type=F32))
                if stage == "early" and block > 0:
                    slope_late[:, at - half_ff : at - half_ff + TILE] = value
                else:
                    slope[:, at : at + TILE] = value
    finish(g_in)
    if extra:
        put_extra(g, row32, ext, n, base, pieces)
    for block in sorted(v_in):
        finish(v_in[block])
        for at in range(block * half_ff, (block + 1) * half_ff, TILE):
            hid = jnp.dot(g[...], v[:, at : at + TILE], preferred_element_type=F32)
            act[:, at : at + TILE] = (hid * slope[:, at : at + TILE]).astype(BF16)
    if stage == "late":
        for block in sorted(w_in):
            finish(w_in[block])
    if extra and stage != "early":
        ext32[...] = jnp.zeros_like(ext32)
    hidden = act.shape[1]
    for at in range(0, width, TILE):
        cols = slice(at, at + TILE)
        back = lax.dot_general(
            act[...], w[cols, :hidden], (((1,), (1,)), ((), ())), preferred_element_type=F32
        )
        if stage == "early":
            partial_out[:, cols] = back
            continue
        if stage == "late":
            back = back + partial[:, cols]
        for i in range(n):
            outs[i][:, cols] = back[i * base : (i + 1) * base].astype(BF16)
            if extra:
                fold(ext32.at[i], back[full + i : full + i + 1], TILE // LANES, at // LANES, base)
    if extra and stage != "early":
        for i in range(n):
            outs[i][:, width:] = ext32[i].astype(BF16)


def expert(msgs, base, extra, w_columns, v_columns, stage="whole", carried=()):
    n = len(msgs)

    def flat(columns):
        arrays, layout = [], []
        for block, cores in enumerate(columns):
            for other, pieces in enumerate(cores):
                row = 0
                for piece in pieces:
                    arrays.append(piece)
                    layout.append((block, other, row, piece.shape[1]))
                    row += piece.shape[0]
        return arrays, layout, row

    w_pieces, w_layout, half = flat(w_columns)
    v_pieces, v_layout, _ = flat(v_columns)
    width, block_ff = 2 * half, w_layout[0][3]
    w_ff, v_ff = len(w_columns) * block_ff, len(v_columns) * block_ff
    rows = n * base + -(-n * extra // 16) * 16
    ext = fold_columns(2 * width // LANES, base)
    back_ext = fold_columns(width // LANES, base)
    cols = width + extra * back_ext
    anywhere, vmem = pl.BlockSpec(memory_space=pl.ANY), pl.BlockSpec(memory_space=pltpu.VMEM)
    spare = max(16, rows - n * base)
    own_slope = [] if stage == "late" else [pltpu.VMEM((rows, v_ff), F32)]
    if stage == "early":
        out_shape = [
            jax.ShapeDtypeStruct((rows, w_ff - block_ff), F32),
            jax.ShapeDtypeStruct((rows, width), F32),
        ]
    else:
        out_shape = [jax.ShapeDtypeStruct((base, cols), BF16) for _ in msgs]
    return pl.pallas_call(
        functools.partial(expert_kernel, n, base, extra, stage, w_layout, v_layout),
        out_shape=out_shape,
        in_specs=[anywhere] * (n + len(w_pieces) + len(v_pieces)) + [vmem] * len(carried),
        out_specs=[vmem] * len(out_shape),
        scratch_shapes=own_slope
        + [
            pltpu.VMEM((width, w_ff), BF16),
            pltpu.VMEM((width, v_ff), BF16),
            pltpu.VMEM((rows, width), BF16),
            pltpu.VMEM((rows, width), BF16),
            pltpu.VMEM((rows, v_ff), BF16),
            pltpu.VMEM((n, base, ext), BF16),
            pltpu.VMEM((spare, width), F32),
            pltpu.VMEM((n, base, back_ext), F32),
            pltpu.SemaphoreType.DMA((n,)),
            pltpu.SemaphoreType.DMA((n,)),
            pltpu.SemaphoreType.DMA((n,)),
            pltpu.SemaphoreType.DMA((len(w_pieces),)),
            pltpu.SemaphoreType.DMA((len(v_pieces),)),
        ],
        compiler_params=pltpu.CompilerParams(vmem_limit_bytes=24 * MIB),
        cost_estimate=pl.CostEstimate(
            flops=2 * rows * width * (w_ff + 2 * v_ff),
            bytes_accessed=2 * width * (w_ff + v_ff) + 6 * rows * width,
            transcendentals=rows * w_ff,
        ),
        name="expert_" + stage,
    )(*msgs, *w_pieces, *v_pieces, *carried)


def combine_kernel(dists, base, extra, ids_ref, grad_ref, *refs):
    n = len(dists)
    msgs, (out, rows, ext, row32, sem_b, sem_e) = refs[:n], refs[n:]
    tokens, width = grad_ref.shape
    pieces = width // LANES
    full = n * base
    here = lax.axis_index("expert") // 2
    copies = []
    for i in range(n):
        copies.append(
            pltpu.make_async_copy(msgs[i].at[:, pl.ds(0, width)], rows.at[pl.ds(i * base, base), :], sem_b.at[i])
        )
        if extra:
            copies.append(
                pltpu.make_async_copy(msgs[i].at[:, pl.ds(width, ext.shape[2])], ext.at[i], sem_e.at[i])
            )
    for copy in copies:
        copy.start()
    ids = ids_ref[...]
    places = []
    overflow = jnp.zeros((tokens, 16), F32)
    for i, dist in enumerate(dists):
        slot = jnp.transpose(jnp.broadcast_to(slot_row(ids, here ^ dist), (LANES, tokens)))
        slot = slot[:, 0:1]
        at = lax.broadcasted_iota(jnp.int32, (tokens, base), 1).astype(F32)
        places.append(jnp.where(at == slot, 1.0, 0.0).astype(BF16))
        if extra:
            mine = lax.broadcasted_iota(jnp.int32, (tokens, 16), 1) == i
            overflow = overflow + jnp.where(mine & (slot == float(base)), 1.0, 0.0)
    for copy in copies:
        copy.wait()
    if extra:
        row32[...] = jnp.zeros_like(row32)
        for i in range(n):
            unfold(row32, i, ext[i].astype(F32), pieces, 0, base)
        rows[full:, :] = row32[...].astype(BF16)
    overflow = overflow.astype(BF16)
    for at in range(0, width, 512):
        cols = slice(at, at + 512)
        total = grad_ref[:, cols].astype(F32)
        for i in range(n):
            total = total + jnp.dot(
                places[i], rows[i * base : (i + 1) * base, cols], preferred_element_type=F32
            )
        if extra:
            total = total + jnp.dot(overflow, rows[full:, cols], preferred_element_type=F32)
        out[:, cols] = total.astype(BF16)


def combine(dists, base, extra, ids_t, grad, msgs):
    n = len(dists)
    tokens, width = grad.shape
    rows = n * base + 16 * extra
    ext = fold_columns(width // LANES, base)
    anywhere, vmem = pl.BlockSpec(memory_space=pl.ANY), pl.BlockSpec(memory_space=pltpu.VMEM)
    return pl.pallas_call(
        functools.partial(combine_kernel, dists, base, extra),
        out_shape=jax.ShapeDtypeStruct((tokens, width), BF16),
        in_specs=[vmem, vmem] + [anywhere] * n,
        out_specs=vmem,
        scratch_shapes=[
            pltpu.VMEM((rows, width), BF16),
            pltpu.VMEM((n, base, ext), BF16),
            pltpu.VMEM((16, width), F32),
            pltpu.SemaphoreType.DMA((n,)),
            pltpu.SemaphoreType.DMA((n,)),
        ],
        compiler_params=pltpu.CompilerParams(vmem_limit_bytes=24 * MIB),
        cost_estimate=pl.CostEstimate(
            flops=2 * rows * tokens * width,
            bytes_accessed=2 * rows * width + 4 * tokens * width,
            transcendentals=0,
        ),
        name="combine",
    )(ids_t, grad, *msgs)


def swap(value, axis, apart):
    return lax.ppermute(value, axis, [(i, i ^ apart) for i in range(lax.axis_size(axis))])


def swap_back(value, apart):
    sections, places = lax.axis_size("section"), lax.axis_size("expert")
    pairs = [
        (s * places + i, (s ^ 1) * places + (i ^ apart)) for s in range(sections) for i in range(places)
    ]
    return lax.ppermute(value, ("section", "expert"), pairs)


def after(*values):
    return lax.optimization_barrier(values)


def groups_of(experts):
    if experts == 4:
        return [[2], [3], [1, 0]], [[2, 0], [3, 1]]
    order = list(range(experts - 1, -1, -1))
    size = -(-experts // 4)
    groups = [order[i : i + size] for i in range(0, experts, size)]
    return groups, groups


def body(tokens, grad_out, expert_ids, gate_values, w_in, w_out_t):
    tok, grad = tokens[0], grad_out[0]
    ids_t, gates_t = expert_ids[0].T, gate_values[0].T
    experts = lax.axis_size("expert") // 2
    base, extra = slots_of(tok.shape[0], ids_t.shape[0], experts)
    sends, works = groups_of(experts)
    others = range(1, lax.axis_size("dp"))
    w_own, v_own = w_in[0, 0], w_out_t[0, 0]
    sent = [dispatch(group, base, extra, ids_t, gates_t, tok, grad) for group in sends]
    sent[0], w_own, v_own = after(sent[0], w_own, v_own)
    w_far = [swap(w_own, "dp", apart) for apart in others]
    v_far = [swap(v_own, "dp", apart) for apart in others]
    got = {}
    for group, msgs in zip(sends, sent):
        for dist, msg in zip(group, msgs):
            got[dist] = swap(msg, "expert", 2 * dist) if dist else msg
    first, rest = sends[0], [dist for group in sends[1:] for dist in group]

    w_other, v_other = [swap(w_own, "expert", 1)], [swap(v_own, "expert", 1)]
    w_far, heads, sent, w_other, v_other = after(w_far, [got[dist] for dist in first], sent, w_other, v_other)
    got.update(zip(first, heads))
    w_other += [swap(block, "expert", 1) for block in w_far]
    w_columns = [[[block], [other]] for block, other in zip([w_own] + w_far, w_other)]
    v_columns = [[[v_own], [v_other[0]]]]
    carried = expert([got[dist] for dist in works[0]], base, extra, w_columns, v_columns, "early")
    grad, ids_t, w_other = after(grad, ids_t, w_other)
    other_grad, other_ids = swap(grad, "section", 1), swap(ids_t, "section", 1)
    v_far, tails, other_grad, other_ids, carried = after(
        v_far, [got[dist] for dist in rest], other_grad, other_ids, carried
    )
    got.update(zip(rest, tails))
    v_columns += [[[block], [swap(block, "expert", 1)]] for block in v_far]

    dists, returned = [], []
    for i, group in enumerate(works):
        msgs = [got[dist] for dist in group]
        if i == 0:
            backs = expert(msgs, base, extra, w_columns[1:], v_columns[1:], "late", carried)
            backs, got = after(backs, got)
        else:
            backs = expert(msgs, base, extra, w_columns, v_columns)
        dists += group
        returned += [swap_back(back, 2 * dist) for dist, back in zip(group, backs)]
    return combine(dists, base, extra, other_ids, other_grad, returned)[None]


def solution(mesh):
    rows = P("section", ("expert", "dp"), None)
    weights = P("section", "expert", None, "dp")
    return jax.shard_map(
        body,
        mesh=mesh,
        in_specs=(rows, rows, rows, rows, weights, weights),
        out_specs=rows,
        check_vma=False,
    )
```

```python
import functools

import jax
import jax.numpy as jnp
from jax import lax
from jax.experimental import pallas as pl
from jax.experimental.pallas import tpu as pltpu
from jax.sharding import PartitionSpec as P

LANES = 128
TILE = 256
F32 = jnp.float32
BF16 = jnp.bfloat16
MIB = 1 << 20
CHUNK = 512
PARTS = 4
LIMIT = 57
CUTS = 3


def slots_of(tok_dev, top, experts):
    capacity = min(tok_dev, max(2, tok_dev * top // experts + 1))
    if capacity % 16 == 1 and capacity > 1:
        return capacity - 1, 1
    return -(-capacity // 16) * 16, 0


def fold_columns(pieces, base):
    return -(-(pieces + 1) // base) * LANES


def place_of(piece, base):
    return piece % base, piece // base * LANES


def fold(ext_ref, row, pieces, first, base):
    for k in range(pieces):
        at, column = place_of(first + k, base)
        ext_ref[at : at + 1, column : column + LANES] = row[:, k * LANES : (k + 1) * LANES]


def unfold(row_ref, at_row, ext, pieces, first, base):
    for k in range(pieces):
        at, column = place_of(first + k, base)
        row_ref[at_row : at_row + 1, k * LANES : (k + 1) * LANES] = ext[at : at + 1, column : column + LANES]


def slot_row(ids, expert):
    tokens = ids.shape[1]
    hit = jnp.where(ids == expert, 1.0, 0.0).astype(F32)
    mask = jnp.sum(hit, axis=0, keepdims=True)
    earlier = lax.broadcasted_iota(jnp.int32, (tokens, tokens), 0) < lax.broadcasted_iota(
        jnp.int32, (tokens, tokens), 1
    )
    before = jnp.dot(
        jnp.broadcast_to(mask, (16, tokens)).astype(BF16),
        jnp.where(earlier, 1.0, 0.0).astype(BF16),
        preferred_element_type=F32,
    )[0:1]
    return jnp.where(mask > 0.5, before, -1.0)


def begin(src, dst, sem):
    copy = pltpu.make_async_copy(src, dst, sem)
    copy.start()
    return copy


def finish(copies):
    for copy in copies:
        copy.wait()


def dispatch_kernel(dists, base, extra, ids_hbm, gates_hbm, tok_hbm, grad_hbm, *refs):
    n = len(dists)
    outs, refs = refs[:n], refs[n:]
    ids_ref, gates_ref, tok_ref, grad_ref, msg_ref, ext_ref, sem_i, sem_t, sem_g, sem_o = refs
    here = lax.axis_index("expert") // 2
    tokens, width = tok_ref.shape
    pieces = width // LANES
    rows = base + 16 * extra
    step = tokens // PARTS
    parts = [pl.ds(i * step, step) for i in range(PARTS)]
    small = [begin(ids_hbm, ids_ref, sem_i.at[0]), begin(gates_hbm, gates_ref, sem_i.at[1])]
    tok_in = [begin(tok_hbm.at[p, :], tok_ref.at[p, :], sem_t.at[i]) for i, p in enumerate(parts)]
    grad_in = [begin(grad_hbm.at[p, :], grad_ref.at[p, :], sem_g.at[i]) for i, p in enumerate(parts)]
    finish(small)
    ids, gates = ids_ref[...], gates_ref[...]
    onehots, scales = [], []
    for dist in dists:
        slot = slot_row(ids, here ^ dist)
        gate = jnp.sum(jnp.where(ids == (here ^ dist), gates, 0.0), axis=0, keepdims=True)
        picks = lax.broadcasted_iota(jnp.int32, (rows, tokens), 0).astype(F32) == slot
        onehots.append(jnp.where(picks, 1.0, 0.0).astype(BF16))
        scales.append(jnp.sum(jnp.where(picks, gate, 0.0), axis=1, keepdims=True))
    ext_ref[...] = jnp.zeros_like(ext_ref)
    count = lax.broadcasted_iota(jnp.int32, (16, tokens), 1) + 1
    for d in range(n):
        holders = lax.dot_general(
            count.astype(F32).astype(BF16), onehots[d], (((1,), (1,)), ((), ())), preferred_element_type=F32
        )
        at, column = place_of(2 * pieces * extra, base)
        ext_ref[d, at : at + 1, column : column + rows] = holders[0:1]
    sent = []
    for part, copies in enumerate((tok_in, grad_in)):
        finish(copies)
        for d in range(n):
            for at in range(0, width, CHUNK):
                value = jnp.dot(
                    onehots[d],
                    (grad_ref if part else tok_ref)[:, at : at + CHUNK],
                    preferred_element_type=F32,
                )
                if part:
                    value = value * scales[d]
                msg_ref[d, :, part * width + at : part * width + at + CHUNK] = value[:base].astype(BF16)
                if extra:
                    first = part * pieces + at // LANES
                    fold(ext_ref.at[d], value[base : base + 1], CHUNK // LANES, first, base)
            stop = (part + 1) * width
            if part:
                msg_ref[d, :, stop:] = ext_ref[d].astype(BF16)
                stop = msg_ref.shape[2]
            cols = pl.ds(part * width, stop - part * width)
            sent.append(begin(msg_ref.at[d, :, cols], outs[d].at[:, cols], sem_o.at[d, part]))
    finish(sent)


def dispatch(dists, base, extra, ids_t, gates_t, tok, grad, limit):
    tokens, width = tok.shape
    n, ext = len(dists), fold_columns(2 * width // LANES * extra, base)
    cols = 2 * width + ext
    anywhere = pl.BlockSpec(memory_space=pl.ANY)
    return pl.pallas_call(
        functools.partial(dispatch_kernel, dists, base, extra),
        out_shape=[jax.ShapeDtypeStruct((base, cols), BF16) for _ in dists],
        in_specs=[anywhere] * 4,
        out_specs=[anywhere] * n,
        scratch_shapes=[
            pltpu.VMEM(ids_t.shape, jnp.int32),
            pltpu.VMEM(gates_t.shape, F32),
            pltpu.VMEM((tokens, width), BF16),
            pltpu.VMEM((tokens, width), BF16),
            pltpu.VMEM((n, base, cols), BF16),
            pltpu.VMEM((n, base, ext), F32),
            pltpu.SemaphoreType.DMA((2,)),
            pltpu.SemaphoreType.DMA((PARTS,)),
            pltpu.SemaphoreType.DMA((PARTS,)),
            pltpu.SemaphoreType.DMA((n, 2)),
        ],
        compiler_params=pltpu.CompilerParams(vmem_limit_bytes=limit * MIB),
        cost_estimate=pl.CostEstimate(
            flops=4 * n * (base + 16) * tokens * width,
            bytes_accessed=4 * tokens * width + 2 * n * base * cols,
            transcendentals=0,
        ),
        name="dispatch",
    )(ids_t, gates_t, tok, grad)


def silu_slope(pre):
    sig = jax.nn.sigmoid(pre)
    return sig * (1.0 + pre * (1.0 - sig))


def begin_weights(pieces, layout, whole, sems):
    half = whole.shape[0] // 2
    core = lax.axis_index("expert") % 2
    copies = {}
    for i, (piece, (block, other, row, columns)) in enumerate(zip(pieces, layout)):
        at = pl.multiple_of((1 - core if other else core) * half + row, 16)
        rows = pl.ds(at, piece.shape[0])
        dst = whole.at[rows, pl.ds(block * columns, columns)]
        copies.setdefault(block, []).append(begin(piece, dst, sems.at[i]))
    return copies


def begin_rows(msgs, rows, ext, start, sems, ext_sems):
    base = msgs[0].shape[0]
    width = rows.shape[1]
    copies = []
    for i, msg in enumerate(msgs):
        copies.append(begin(msg.at[:, pl.ds(start, width)], rows.at[pl.ds(i * base, base), :], sems.at[i]))
        if ext is not None:
            copies.append(begin(msg.at[:, pl.ds(2 * width, ext.shape[2])], ext.at[i], ext_sems.at[i]))
    return copies


def put_extra(rows, row32, ext, n, base, first):
    row32[...] = jnp.zeros_like(row32)
    for i in range(n):
        unfold(row32, i, ext[i].astype(F32), rows.shape[1] // LANES, first, base)
    rows[n * base :, :] = row32[...].astype(BF16)


def expert_kernel(n, base, extra, stage, w_layout, v_layout, *refs):
    msgs, refs = refs[:n], refs[n:]
    w_pieces, refs = refs[: len(w_layout)], refs[len(w_layout) :]
    v_pieces, refs = refs[: len(v_layout)], refs[len(v_layout) :]
    if stage == "late":
        slope, partial, refs = refs[0], refs[1], refs[2:]
        outs, refs = refs[:n], refs[n:]
    elif stage == "early":
        slope_late, partial_out, slope, refs = refs[0], refs[1], refs[2], refs[3:]
    else:
        outs, slope, refs = refs[:n], refs[n], refs[n + 1 :]
    w, v, x, g, act, ext, row32, ext32, sem_x, sem_g, sem_e, sem_w, sem_v = refs
    width = w.shape[0]
    half_ff = w_layout[0][3]
    pieces = width // LANES
    full = n * base
    x_in = []
    if stage != "late":
        x_in = begin_rows(msgs, x, ext, 0, sem_x, sem_e)
    w_in = begin_weights(w_pieces, w_layout, w, sem_w)
    g_in = begin_rows(msgs, g, ext if stage == "late" else None, width, sem_g, sem_e)
    v_in = begin_weights(v_pieces, v_layout, v, sem_v)
    if stage != "late":
        finish(x_in)
        if extra:
            put_extra(x, row32, ext, n, base, 0)
        for block in sorted(w_in):
            finish(w_in[block])
            for at in range(block * half_ff, (block + 1) * half_ff, TILE):
                value = silu_slope(jnp.dot(x[...], w[:, at : at + TILE], preferred_element_type=F32))
                if stage == "early" and block > 0:
                    slope_late[:, at - half_ff : at - half_ff + TILE] = value
                else:
                    slope[:, at : at + TILE] = value
    finish(g_in)
    if extra:
        put_extra(g, row32, ext, n, base, pieces)
    for block in sorted(v_in):
        finish(v_in[block])
        for at in range(block * half_ff, (block + 1) * half_ff, TILE):
            hid = jnp.dot(g[...], v[:, at : at + TILE], preferred_element_type=F32)
            act[:, at : at + TILE] = (hid * slope[:, at : at + TILE]).astype(BF16)
    if stage == "late":
        for block in sorted(w_in):
            finish(w_in[block])
    if stage != "early":
        ext32[...] = jnp.zeros_like(ext32)
        (at, column), (to, to_column) = place_of(2 * pieces * extra, base), place_of(pieces * extra, base)
        for i in range(n):
            holders = ext[i].astype(F32)[at : at + 1, column : column + LANES]
            ext32[i, to : to + 1, to_column : to_column + LANES] = holders
    hidden = act.shape[1]
    for at in range(0, width, TILE):
        cols = slice(at, at + TILE)
        back = lax.dot_general(
            act[...], w[cols, :hidden], (((1,), (1,)), ((), ())), preferred_element_type=F32
        )
        if stage == "early":
            partial_out[:, cols] = back
            continue
        if stage == "late":
            back = back + partial[:, cols]
        for i in range(n):
            outs[i][:, cols] = back[i * base : (i + 1) * base].astype(BF16)
            if extra:
                fold(ext32.at[i], back[full + i : full + i + 1], TILE // LANES, at // LANES, base)
    if stage != "early":
        for i in range(n):
            outs[i][:, width:] = ext32[i].astype(BF16)


def expert(msgs, base, extra, w_columns, v_columns, stage="whole", carried=()):
    n = len(msgs)

    def flat(columns):
        arrays, layout = [], []
        for block, cores in enumerate(columns):
            for other, pieces in enumerate(cores):
                row = 0
                for piece in pieces:
                    arrays.append(piece)
                    layout.append((block, other, row, piece.shape[1]))
                    row += piece.shape[0]
        return arrays, layout, row

    w_pieces, w_layout, half = flat(w_columns)
    v_pieces, v_layout, _ = flat(v_columns)
    width, block_ff = 2 * half, w_layout[0][3]
    w_ff, v_ff = len(w_columns) * block_ff, len(v_columns) * block_ff
    rows = n * base + -(-n * extra // 16) * 16
    ext = fold_columns(2 * width // LANES * extra, base)
    back_ext = fold_columns(width // LANES * extra, base)
    cols = width + back_ext
    anywhere, vmem = pl.BlockSpec(memory_space=pl.ANY), pl.BlockSpec(memory_space=pltpu.VMEM)
    spare = max(16, rows - n * base)
    own_slope = [] if stage == "late" else [pltpu.VMEM((rows, v_ff), F32)]
    if stage == "early":
        out_shape = [
            jax.ShapeDtypeStruct((rows, w_ff - block_ff), F32),
            jax.ShapeDtypeStruct((rows, width), F32),
        ]
    else:
        out_shape = [jax.ShapeDtypeStruct((base, cols), BF16) for _ in msgs]
    return pl.pallas_call(
        functools.partial(expert_kernel, n, base, extra, stage, w_layout, v_layout),
        out_shape=out_shape,
        in_specs=[anywhere] * (n + len(w_pieces) + len(v_pieces)) + [vmem] * len(carried),
        out_specs=[vmem] * len(out_shape),
        scratch_shapes=own_slope
        + [
            pltpu.VMEM((width, w_ff), BF16),
            pltpu.VMEM((width, v_ff), BF16),
            pltpu.VMEM((rows, width), BF16),
            pltpu.VMEM((rows, width), BF16),
            pltpu.VMEM((rows, v_ff), BF16),
            pltpu.VMEM((n, base, ext), BF16),
            pltpu.VMEM((spare, width), F32),
            pltpu.VMEM((n, base, back_ext), F32),
            pltpu.SemaphoreType.DMA((n,)),
            pltpu.SemaphoreType.DMA((n,)),
            pltpu.SemaphoreType.DMA((n,)),
            pltpu.SemaphoreType.DMA((len(w_pieces),)),
            pltpu.SemaphoreType.DMA((len(v_pieces),)),
        ],
        compiler_params=pltpu.CompilerParams(vmem_limit_bytes=24 * MIB),
        cost_estimate=pl.CostEstimate(
            flops=0 if stage == "early" else 2 * rows * width * (w_ff + 2 * v_ff),
            bytes_accessed=0 if stage == "early" else 2 * width * (w_ff + v_ff) + 6 * rows * width,
            transcendentals=0 if stage == "early" else rows * w_ff,
        ),
        name="expert_" + stage,
    )(*msgs, *w_pieces, *v_pieces, *carried)


def add_kernel(n, extra, start_ref, *refs):
    msgs, (out, rows, ext, row32, places, sem_b, sem_e) = refs[:n], refs[n:]
    tokens, width = start_ref.shape
    base = ext.shape[1]
    pieces = width // LANES
    copies = []
    for i, msg in enumerate(msgs):
        copies.append(begin(msg.at[:, pl.ds(width, ext.shape[2])], ext.at[i], sem_e.at[i]))
    rows_in = [
        begin(msg.at[:, pl.ds(0, width)], rows.at[pl.ds(i * base, base), :], sem_b.at[i])
        for i, msg in enumerate(msgs)
    ]
    finish(copies)
    folded = jnp.zeros((tokens, 16), F32)
    at, column = place_of(pieces * extra, base)
    for i in range(n):
        holders = ext[i].astype(F32)[at : at + 1, column : column + LANES]
        token = lax.broadcasted_iota(jnp.int32, (tokens, LANES), 0) + 1
        place = jnp.where(holders == token.astype(F32), 1.0, 0.0)
        places[:, i * base : (i + 1) * base] = place[:, :base].astype(BF16)
        if extra:
            mine = lax.broadcasted_iota(jnp.int32, (tokens, 16), 1) == i
            folded = folded + jnp.where(mine, place[:, base : base + 1], 0.0)
    if extra:
        places[:, n * base :] = folded.astype(BF16)
        put_extra(rows, row32, ext, n, base, 0)
    finish(rows_in)
    place = places[...]
    for at in range(0, width, CHUNK):
        cols = slice(at, at + CHUNK)
        back = jnp.dot(place, rows[:, cols], preferred_element_type=F32)
        out[:, cols] = (start_ref[:, cols].astype(F32) + back).astype(out.dtype)


def add_returned(start, msgs, extra, kind, name):
    tokens, width = start.shape
    n, base = len(msgs), msgs[0].shape[0]
    slots = n * base + 16 * extra
    anywhere, vmem = pl.BlockSpec(memory_space=pl.ANY), pl.BlockSpec(memory_space=pltpu.VMEM)
    return pl.pallas_call(
        functools.partial(add_kernel, n, extra),
        out_shape=jax.ShapeDtypeStruct((tokens, width), kind),
        in_specs=[vmem] + [anywhere] * n,
        out_specs=vmem,
        scratch_shapes=[
            pltpu.VMEM((slots, width), BF16),
            pltpu.VMEM((n, base, msgs[0].shape[1] - width), BF16),
            pltpu.VMEM((16, width), F32),
            pltpu.VMEM((tokens, slots), BF16),
            pltpu.SemaphoreType.DMA((n,)),
            pltpu.SemaphoreType.DMA((n,)),
        ],
        compiler_params=pltpu.CompilerParams(vmem_limit_bytes=24 * MIB),
        cost_estimate=pl.CostEstimate(
            flops=2 * slots * tokens * width,
            bytes_accessed=2 * slots * width + 6 * tokens * width,
            transcendentals=0,
        ),
        name=name,
    )(start, *msgs)


def swap(value, axis, apart):
    return lax.ppermute(value, axis, [(i, i ^ apart) for i in range(lax.axis_size(axis))])


def swap_back(value, apart):
    sections, places = lax.axis_size("section"), lax.axis_size("expert")
    pairs = [
        (s * places + i, (s ^ 1) * places + (i ^ apart)) for s in range(sections) for i in range(places)
    ]
    return lax.ppermute(value, ("section", "expert"), pairs)


def after(*values):
    return lax.optimization_barrier(values)


def cut(weight):
    step = -(-weight.shape[0] // (16 * CUTS)) * 16
    return [weight[at : at + step] for at in range(0, weight.shape[0], step)]


def groups_of(experts):
    if experts == 4:
        return [[2], [1, 0], [3]], [[2, 0], [3, 1]]
    order = list(range(experts - 1, -1, -1))
    size = -(-experts // 4)
    groups = [order[i : i + size] for i in range(0, experts, size)]
    return groups, groups


def body(tokens, grad_out, expert_ids, gate_values, w_in, w_out_t):
    tok, grad = tokens[0], grad_out[0]
    ids_t, gates_t = expert_ids[0].T, gate_values[0].T
    experts = lax.axis_size("expert") // 2
    base, extra = slots_of(tok.shape[0], ids_t.shape[0], experts)
    sends, works = groups_of(experts)
    others = range(1, lax.axis_size("dp"))
    w_own, v_own = w_in[0, 0], w_out_t[0, 0]
    sent = [
        dispatch(group, base, extra, ids_t, gates_t, tok, grad, 24 if i else LIMIT)
        for i, group in enumerate(sends)
    ]
    w_far = [swap(w_own, "dp", apart) for apart in others]
    w_other, v_other = swap(w_own, "expert", 1), swap(v_own, "expert", 1)
    other_grad = swap(grad, "section", 1)
    v_late, w_other, v_other = after(v_own, w_other, v_other)
    v_far = [swap(v_late, "dp", apart) for apart in others]
    sent[-1], other_grad = after(sent[-1], other_grad)
    got = {}
    for group, msgs in zip(sends, sent):
        for dist, msg in zip(group, msgs):
            got[dist] = swap(msg, "expert", 2 * dist) if dist else msg
    first, last = [dist for group in sends[:-1] for dist in group], sends[-1]

    w_far, heads = after(w_far, [got[dist] for dist in first])
    got.update(zip(first, heads))
    w_columns = [[[w_own], [w_other]]]
    w_columns += [[[block], [swap(piece, "expert", 1) for piece in cut(block)]] for block in w_far]
    v_columns = [[[v_own], [v_other]]]
    carried = expert([got[dist] for dist in works[0]], base, extra, w_columns, v_columns, "early")
    v_far, tails, carried = after(v_far, [got[dist] for dist in last], carried)
    got.update(zip(last, tails))
    v_columns += [[[block], [swap(block, "expert", 1)]] for block in v_far]

    total = other_grad
    for i, group in enumerate(works):
        msgs = [got[dist] for dist in group]
        if i == 0:
            backs = expert(msgs, base, extra, w_columns[1:], v_columns[1:], "late", carried)
            backs, got = after(backs, got)
        else:
            backs = expert(msgs, base, extra, w_columns, v_columns)
        returned = [swap_back(back, 2 * dist) for dist, back in zip(group, backs)]
        ends = i == len(works) - 1
        total = add_returned(total, returned, extra, BF16 if ends else F32, "finish" if ends else "settle")
    return total[None]


def solution(mesh):
    rows = P("section", ("expert", "dp"), None)
    weights = P("section", "expert", None, "dp")
    return jax.shard_map(
        body,
        mesh=mesh,
        in_specs=(rows, rows, rows, rows, weights, weights),
        out_specs=rows,
        check_vma=False,
    )
```

```python
import functools

import jax
import jax.numpy as jnp
from jax import lax
from jax.experimental import pallas as pl
from jax.experimental.pallas import tpu as pltpu
from jax.sharding import PartitionSpec as P

LANES = 128
TILE = 256
F32 = jnp.float32
BF16 = jnp.bfloat16
MIB = 1 << 20
CHUNK = 512
PARTS = 4
LIMIT = 57
TAIL = 9
CUTS = 3


def slots_of(tok_dev, top, experts):
    capacity = min(tok_dev, max(2, tok_dev * top // experts + 1))
    if capacity % 16 == 1 and capacity > 1:
        return capacity - 1, 1
    return -(-capacity // 16) * 16, 0


def fold_columns(pieces, base):
    return -(-(pieces + 1) // base) * LANES


def place_of(piece, base):
    return piece % base, piece // base * LANES


def fold(ext_ref, row, pieces, first, base):
    for k in range(pieces):
        at, column = place_of(first + k, base)
        ext_ref[at : at + 1, column : column + LANES] = row[:, k * LANES : (k + 1) * LANES]


def unfold(row_ref, at_row, ext, pieces, first, base):
    for k in range(pieces):
        at, column = place_of(first + k, base)
        row_ref[at_row : at_row + 1, k * LANES : (k + 1) * LANES] = ext[at : at + 1, column : column + LANES]


def slot_row(ids, expert):
    tokens = ids.shape[1]
    hit = jnp.where(ids == expert, 1.0, 0.0).astype(F32)
    mask = jnp.sum(hit, axis=0, keepdims=True)
    earlier = lax.broadcasted_iota(jnp.int32, (tokens, tokens), 0) < lax.broadcasted_iota(
        jnp.int32, (tokens, tokens), 1
    )
    before = jnp.dot(
        jnp.broadcast_to(mask, (16, tokens)).astype(BF16),
        jnp.where(earlier, 1.0, 0.0).astype(BF16),
        preferred_element_type=F32,
    )[0:1]
    return jnp.where(mask > 0.5, before, -1.0)


def begin(src, dst, sem):
    copy = pltpu.make_async_copy(src, dst, sem)
    copy.start()
    return copy


def finish(copies):
    for copy in copies:
        copy.wait()


def dispatch_kernel(dists, base, extra, split, ids_hbm, gates_hbm, tok_hbm, grad_hbm, *refs):
    n = len(dists)
    outs, refs = refs[: n * len(split)], refs[n * len(split) :]
    ids_ref, gates_ref, tok_ref, grad_ref, msg_ref, ext_ref, sem_i, sem_t, sem_g, sem_o = refs
    here = lax.axis_index("expert") // 2
    tokens, width = tok_ref.shape
    pieces = width // LANES
    rows = base + 16 * extra
    step = tokens // PARTS
    parts = [pl.ds(i * step, step) for i in range(PARTS)]
    small = [begin(ids_hbm, ids_ref, sem_i.at[0]), begin(gates_hbm, gates_ref, sem_i.at[1])]
    tok_in = [begin(tok_hbm.at[p, :], tok_ref.at[p, :], sem_t.at[i]) for i, p in enumerate(parts)]
    grad_in = [begin(grad_hbm.at[p, :], grad_ref.at[p, :], sem_g.at[i]) for i, p in enumerate(parts)]
    finish(small)
    ids, gates = ids_ref[...], gates_ref[...]
    onehots, scales = [], []
    for dist in dists:
        slot = slot_row(ids, here ^ dist)
        gate = jnp.sum(jnp.where(ids == (here ^ dist), gates, 0.0), axis=0, keepdims=True)
        picks = lax.broadcasted_iota(jnp.int32, (rows, tokens), 0).astype(F32) == slot
        onehots.append(jnp.where(picks, 1.0, 0.0).astype(BF16))
        scales.append(jnp.sum(jnp.where(picks, gate, 0.0), axis=1, keepdims=True))
    ext_ref[...] = jnp.zeros_like(ext_ref)
    count = lax.broadcasted_iota(jnp.int32, (16, tokens), 1) + 1
    for d in range(n):
        holders = lax.dot_general(
            count.astype(F32).astype(BF16), onehots[d], (((1,), (1,)), ((), ())), preferred_element_type=F32
        )
        at, column = place_of(2 * pieces * extra, base)
        ext_ref[d, at : at + 1, column : column + rows] = holders[0:1]
    sent = []
    for part, copies in enumerate((tok_in, grad_in)):
        finish(copies)
        for d in range(n):
            for at in range(0, width, CHUNK):
                value = jnp.dot(
                    onehots[d],
                    (grad_ref if part else tok_ref)[:, at : at + CHUNK],
                    preferred_element_type=F32,
                )
                if part:
                    value = value * scales[d]
                msg_ref[d, :, part * width + at : part * width + at + CHUNK] = value[:base].astype(BF16)
                if extra:
                    first = part * pieces + at // LANES
                    fold(ext_ref.at[d], value[base : base + 1], CHUNK // LANES, first, base)
            stop = (part + 1) * width
            if part:
                msg_ref[d, :, stop:] = ext_ref[d].astype(BF16)
                stop = msg_ref.shape[2]
            for i, (start, end) in enumerate(split):
                low, high = max(start, part * width), min(end, stop)
                if low < high:
                    src = msg_ref.at[d, :, pl.ds(low, high - low)]
                    dst = outs[d * len(split) + i].at[:, pl.ds(low - start, high - low)]
                    sent.append(begin(src, dst, sem_o.at[d, part, i]))
    finish(sent)


def dispatch(dists, base, extra, ids_t, gates_t, tok, grad, limit, whole=True):
    tokens, width = tok.shape
    n, ext = len(dists), fold_columns(2 * width // LANES * extra, base)
    cols = 2 * width + ext
    cutoff = 2 * width - TAIL * LANES
    split = [(0, cols)] if whole else [(0, cutoff), (cutoff, cols)]
    anywhere = pl.BlockSpec(memory_space=pl.ANY)
    outs = pl.pallas_call(
        functools.partial(dispatch_kernel, dists, base, extra, split),
        out_shape=[jax.ShapeDtypeStruct((base, end - start), BF16) for _ in dists for start, end in split],
        in_specs=[anywhere] * 4,
        out_specs=[anywhere] * (n * len(split)),
        scratch_shapes=[
            pltpu.VMEM(ids_t.shape, jnp.int32),
            pltpu.VMEM(gates_t.shape, F32),
            pltpu.VMEM((tokens, width), BF16),
            pltpu.VMEM((tokens, width), BF16),
            pltpu.VMEM((n, base, cols), BF16),
            pltpu.VMEM((n, base, ext), F32),
            pltpu.SemaphoreType.DMA((2,)),
            pltpu.SemaphoreType.DMA((PARTS,)),
            pltpu.SemaphoreType.DMA((PARTS,)),
            pltpu.SemaphoreType.DMA((n, 2, len(split))),
        ],
        compiler_params=pltpu.CompilerParams(vmem_limit_bytes=limit * MIB),
        cost_estimate=pl.CostEstimate(
            flops=4 * n * (base + 16) * tokens * width,
            bytes_accessed=4 * tokens * width + 2 * n * base * cols,
            transcendentals=0,
        ),
        name="dispatch",
    )(ids_t, gates_t, tok, grad)
    return [tuple(outs[i : i + len(split)]) for i in range(0, len(outs), len(split))]


def silu_slope(pre):
    sig = jax.nn.sigmoid(pre)
    return sig * (1.0 + pre * (1.0 - sig))


def begin_weights(pieces, layout, whole, sems):
    half = whole.shape[0] // 2
    core = lax.axis_index("expert") % 2
    copies = {}
    for i, (piece, (block, other, row, columns)) in enumerate(zip(pieces, layout)):
        at = pl.multiple_of((1 - core if other else core) * half + row, 16)
        rows = pl.ds(at, piece.shape[0])
        dst = whole.at[rows, pl.ds(block * columns, columns)]
        copies.setdefault(block, []).append(begin(piece, dst, sems.at[i]))
    return copies


def begin_columns(parts, start, dst, sems):
    copies, at = [], 0
    for i, part in enumerate(parts):
        low, high = max(start, at), min(start + dst.shape[1], at + part.shape[1])
        if low < high:
            src = part.at[:, pl.ds(low - at, high - low)]
            copies.append(begin(src, dst.at[:, pl.ds(low - start, high - low)], sems.at[i]))
        at += part.shape[1]
    return copies


def begin_rows(msgs, rows, ext, start, sems, ext_sems):
    base = msgs[0][0].shape[0]
    width = rows.shape[1]
    copies = []
    for i, parts in enumerate(msgs):
        copies += begin_columns(parts, start, rows.at[pl.ds(i * base, base), :], sems.at[i])
        if ext is not None:
            copies += begin_columns(parts, 2 * width, ext.at[i], ext_sems.at[i])
    return copies


def put_extra(rows, row32, ext, n, base, first):
    row32[...] = jnp.zeros_like(row32)
    for i in range(n):
        unfold(row32, i, ext[i].astype(F32), rows.shape[1] // LANES, first, base)
    rows[n * base :, :] = row32[...].astype(BF16)


def expert_kernel(n, base, extra, stage, w_layout, v_layout, lengths, *refs):
    msgs = []
    for length in lengths:
        msgs.append(refs[:length])
        refs = refs[length:]
    w_pieces, refs = refs[: len(w_layout)], refs[len(w_layout) :]
    v_pieces, refs = refs[: len(v_layout)], refs[len(v_layout) :]
    if stage == "late":
        slope, partial, refs = refs[0], refs[1], refs[2:]
        outs, refs = refs[:n], refs[n:]
    elif stage == "early":
        slope_late, partial_out, slope, refs = refs[0], refs[1], refs[2], refs[3:]
    else:
        outs, slope, refs = refs[:n], refs[n], refs[n + 1 :]
    w, v, x, g, act, ext, row32, ext32, sem_x, sem_g, sem_e, sem_w, sem_v = refs
    width = w.shape[0]
    half_ff = w_layout[0][3]
    pieces = width // LANES
    full = n * base
    x_in = []
    if stage != "late":
        x_in = begin_rows(msgs, x, ext, 0, sem_x, sem_e)
    w_in = begin_weights(w_pieces, w_layout, w, sem_w)
    g_in = begin_rows(msgs, g, ext if stage == "late" else None, width, sem_g, sem_e)
    v_in = begin_weights(v_pieces, v_layout, v, sem_v)
    if stage != "late":
        finish(x_in)
        if extra:
            put_extra(x, row32, ext, n, base, 0)
        for block in sorted(w_in):
            finish(w_in[block])
            for at in range(block * half_ff, (block + 1) * half_ff, TILE):
                value = silu_slope(jnp.dot(x[...], w[:, at : at + TILE], preferred_element_type=F32))
                if stage == "early" and block > 0:
                    slope_late[:, at - half_ff : at - half_ff + TILE] = value
                else:
                    slope[:, at : at + TILE] = value
    finish(g_in)
    if extra:
        put_extra(g, row32, ext, n, base, pieces)
    for block in sorted(v_in):
        finish(v_in[block])
        for at in range(block * half_ff, (block + 1) * half_ff, TILE):
            hid = jnp.dot(g[...], v[:, at : at + TILE], preferred_element_type=F32)
            act[:, at : at + TILE] = (hid * slope[:, at : at + TILE]).astype(BF16)
    if stage == "late":
        for block in sorted(w_in):
            finish(w_in[block])
    if stage != "early":
        ext32[...] = jnp.zeros_like(ext32)
        (at, column), (to, to_column) = place_of(2 * pieces * extra, base), place_of(pieces * extra, base)
        for i in range(n):
            holders = ext[i].astype(F32)[at : at + 1, column : column + LANES]
            ext32[i, to : to + 1, to_column : to_column + LANES] = holders
    hidden = act.shape[1]
    for at in range(0, width, TILE):
        cols = slice(at, at + TILE)
        back = lax.dot_general(
            act[...], w[cols, :hidden], (((1,), (1,)), ((), ())), preferred_element_type=F32
        )
        if stage == "early":
            partial_out[:, cols] = back
            continue
        if stage == "late":
            back = back + partial[:, cols]
        for i in range(n):
            outs[i][:, cols] = back[i * base : (i + 1) * base].astype(BF16)
            if extra:
                fold(ext32.at[i], back[full + i : full + i + 1], TILE // LANES, at // LANES, base)
    if stage != "early":
        for i in range(n):
            outs[i][:, width:] = ext32[i].astype(BF16)


def late_kernel(n, base, extra, blocks, w_layout, v_layout, *refs):
    msgs, refs = refs[:n], refs[n:]
    w_pieces, refs = refs[: len(w_layout)], refs[len(w_layout) :]
    v_pieces, refs = refs[: len(v_layout)], refs[len(v_layout) :]
    slope, partial, refs = refs[0], refs[1], refs[2:]
    outs, (g, act, ext, row32, ext32, sem_g, sem_e) = refs[:n], refs[n:]
    width = g.shape[1]
    half, block_ff = width // 2, v_layout[0][3]
    pieces = width // LANES
    full = n * base
    core = lax.axis_index("expert") % 2
    copies = begin_rows([(msg,) for msg in msgs], g, ext, width, sem_g, sem_e)
    finish(copies)
    if extra:
        put_extra(g, row32, ext, n, base, pieces)
    ext32[...] = jnp.zeros_like(ext32)
    (at, column), (to, to_column) = place_of(2 * pieces * extra, base), place_of(pieces * extra, base)
    for i in range(n):
        holders = ext[i].astype(F32)[at : at + 1, column : column + LANES]
        ext32[i, to : to + 1, to_column : to_column + LANES] = holders

    def work(here):
        for block in range(blocks):
            for at in range(0, block_ff, TILE):
                hid = None
                for ref, (of, other, row, _) in zip(v_pieces, v_layout):
                    if of == block:
                        first = (1 - here if other else here) * half + row
                        term = jnp.dot(
                            g[:, first : first + ref.shape[0]],
                            ref[:, at : at + TILE],
                            preferred_element_type=F32,
                        )
                        hid = term if hid is None else hid + term
                cols = slice(block * block_ff + at, block * block_ff + at + TILE)
                act[:, cols] = (hid * slope[:, cols]).astype(BF16)
        places = {}
        for ref, (of, other, row, _) in zip(w_pieces, w_layout):
            for at in range(0, ref.shape[0], TILE):
                size = min(TILE, ref.shape[0] - at)
                first = (1 - here if other else here) * half + row + at
                places.setdefault((first, size), []).append((of, ref, at))
        for (first, size), terms in sorted(places.items()):
            cols = slice(first, first + size)
            back = partial[:, cols]
            for of, ref, at in terms:
                back = back + lax.dot_general(
                    act[:, of * block_ff : (of + 1) * block_ff],
                    ref[at : at + size, :],
                    (((1,), (1,)), ((), ())),
                    preferred_element_type=F32,
                )
            for i in range(n):
                outs[i][:, cols] = back[i * base : (i + 1) * base].astype(BF16)
                if extra:
                    fold(ext32.at[i], back[full + i : full + i + 1], size // LANES, first // LANES, base)

    for here in range(2):
        pl.when(core == here)(functools.partial(work, here))
    for i in range(n):
        outs[i][:, width:] = ext32[i].astype(BF16)


def flat(columns):
    arrays, layout = [], []
    for block, cores in enumerate(columns):
        for other, pieces in enumerate(cores):
            row = 0
            for piece in pieces:
                arrays.append(piece)
                layout.append((block, other, row, piece.shape[1]))
                row += piece.shape[0]
    return arrays, layout, row


def expert_late(msgs, base, extra, w_columns, v_columns, carried):
    n = len(msgs)
    msgs = [message for (message,) in msgs]
    w_pieces, w_layout, half = flat(w_columns)
    v_pieces, v_layout, _ = flat(v_columns)
    width, ff = 2 * half, len(w_columns) * w_layout[0][3]
    rows = n * base + -(-n * extra // 16) * 16
    ext = fold_columns(2 * width // LANES * extra, base)
    back_ext = fold_columns(width // LANES * extra, base)
    anywhere, vmem = pl.BlockSpec(memory_space=pl.ANY), pl.BlockSpec(memory_space=pltpu.VMEM)
    return pl.pallas_call(
        functools.partial(late_kernel, n, base, extra, len(w_columns), w_layout, v_layout),
        out_shape=[jax.ShapeDtypeStruct((base, width + back_ext), BF16) for _ in msgs],
        in_specs=[anywhere] * n + [vmem] * (len(w_pieces) + len(v_pieces) + len(carried)),
        out_specs=[vmem] * n,
        scratch_shapes=[
            pltpu.VMEM((rows, width), BF16),
            pltpu.VMEM((rows, ff), BF16),
            pltpu.VMEM((n, base, ext), BF16),
            pltpu.VMEM((max(16, rows - n * base), width), F32),
            pltpu.VMEM((n, base, back_ext), F32),
            pltpu.SemaphoreType.DMA((n, 1)),
            pltpu.SemaphoreType.DMA((n, 1)),
        ],
        compiler_params=pltpu.CompilerParams(vmem_limit_bytes=24 * MIB),
        cost_estimate=pl.CostEstimate(
            flops=4 * rows * width * ff,
            bytes_accessed=4 * width * ff + 8 * rows * width,
            transcendentals=0,
        ),
        name="expert_late",
    )(*msgs, *w_pieces, *v_pieces, *carried)


def expert(msgs, base, extra, w_columns, v_columns, stage="whole", carried=()):
    n = len(msgs)

    lengths = [len(parts) for parts in msgs]
    most, parts = max(lengths), [part for message in msgs for part in message]
    w_pieces, w_layout, half = flat(w_columns)
    v_pieces, v_layout, _ = flat(v_columns)
    width, block_ff = 2 * half, w_layout[0][3]
    w_ff, v_ff = len(w_columns) * block_ff, len(v_columns) * block_ff
    rows = n * base + -(-n * extra // 16) * 16
    ext = fold_columns(2 * width // LANES * extra, base)
    back_ext = fold_columns(width // LANES * extra, base)
    cols = width + back_ext
    anywhere, vmem = pl.BlockSpec(memory_space=pl.ANY), pl.BlockSpec(memory_space=pltpu.VMEM)
    spare = max(16, rows - n * base)
    own_slope = [] if stage == "late" else [pltpu.VMEM((rows, v_ff), F32)]
    if stage == "early":
        out_shape = [
            jax.ShapeDtypeStruct((rows, w_ff - block_ff), F32),
            jax.ShapeDtypeStruct((rows, width), F32),
        ]
    else:
        out_shape = [jax.ShapeDtypeStruct((base, cols), BF16) for _ in msgs]
    return pl.pallas_call(
        functools.partial(expert_kernel, n, base, extra, stage, w_layout, v_layout, lengths),
        out_shape=out_shape,
        in_specs=[anywhere] * (len(parts) + len(w_pieces) + len(v_pieces)) + [vmem] * len(carried),
        out_specs=[vmem] * len(out_shape),
        scratch_shapes=own_slope
        + [
            pltpu.VMEM((width, w_ff), BF16),
            pltpu.VMEM((width, v_ff), BF16),
            pltpu.VMEM((rows, width), BF16),
            pltpu.VMEM((rows, width), BF16),
            pltpu.VMEM((rows, v_ff), BF16),
            pltpu.VMEM((n, base, ext), BF16),
            pltpu.VMEM((spare, width), F32),
            pltpu.VMEM((n, base, back_ext), F32),
            pltpu.SemaphoreType.DMA((n, most)),
            pltpu.SemaphoreType.DMA((n, most)),
            pltpu.SemaphoreType.DMA((n, most)),
            pltpu.SemaphoreType.DMA((len(w_pieces),)),
            pltpu.SemaphoreType.DMA((len(v_pieces),)),
        ],
        compiler_params=pltpu.CompilerParams(vmem_limit_bytes=24 * MIB),
        cost_estimate=pl.CostEstimate(
            flops=0 if stage == "early" else 2 * rows * width * (w_ff + 2 * v_ff),
            bytes_accessed=0 if stage == "early" else 2 * width * (w_ff + v_ff) + 6 * rows * width,
            transcendentals=0 if stage == "early" else rows * w_ff,
        ),
        name="expert_" + stage,
    )(*parts, *w_pieces, *v_pieces, *carried)


def add_kernel(n, extra, start_ref, *refs):
    msgs, (out, rows, ext, row32, places, sem_b, sem_e) = refs[:n], refs[n:]
    tokens, width = start_ref.shape
    base = ext.shape[1]
    pieces = width // LANES
    copies = []
    for i, msg in enumerate(msgs):
        copies.append(begin(msg.at[:, pl.ds(width, ext.shape[2])], ext.at[i], sem_e.at[i]))
    rows_in = [
        begin(msg.at[:, pl.ds(0, width)], rows.at[pl.ds(i * base, base), :], sem_b.at[i])
        for i, msg in enumerate(msgs)
    ]
    finish(copies)
    folded = jnp.zeros((tokens, 16), F32)
    at, column = place_of(pieces * extra, base)
    for i in range(n):
        holders = ext[i].astype(F32)[at : at + 1, column : column + LANES]
        token = lax.broadcasted_iota(jnp.int32, (tokens, LANES), 0) + 1
        place = jnp.where(holders == token.astype(F32), 1.0, 0.0)
        places[:, i * base : (i + 1) * base] = place[:, :base].astype(BF16)
        if extra:
            mine = lax.broadcasted_iota(jnp.int32, (tokens, 16), 1) == i
            folded = folded + jnp.where(mine, place[:, base : base + 1], 0.0)
    if extra:
        places[:, n * base :] = folded.astype(BF16)
        put_extra(rows, row32, ext, n, base, 0)
    finish(rows_in)
    place = places[...]
    for at in range(0, width, CHUNK):
        cols = slice(at, at + CHUNK)
        back = jnp.dot(place, rows[:, cols], preferred_element_type=F32)
        out[:, cols] = (start_ref[:, cols].astype(F32) + back).astype(out.dtype)


def add_returned(start, msgs, extra, kind, name):
    tokens, width = start.shape
    n, base = len(msgs), msgs[0].shape[0]
    slots = n * base + 16 * extra
    anywhere, vmem = pl.BlockSpec(memory_space=pl.ANY), pl.BlockSpec(memory_space=pltpu.VMEM)
    return pl.pallas_call(
        functools.partial(add_kernel, n, extra),
        out_shape=jax.ShapeDtypeStruct((tokens, width), kind),
        in_specs=[vmem] + [anywhere] * n,
        out_specs=vmem,
        scratch_shapes=[
            pltpu.VMEM((slots, width), BF16),
            pltpu.VMEM((n, base, msgs[0].shape[1] - width), BF16),
            pltpu.VMEM((16, width), F32),
            pltpu.VMEM((tokens, slots), BF16),
            pltpu.SemaphoreType.DMA((n,)),
            pltpu.SemaphoreType.DMA((n,)),
        ],
        compiler_params=pltpu.CompilerParams(vmem_limit_bytes=24 * MIB),
        cost_estimate=pl.CostEstimate(
            flops=2 * slots * tokens * width,
            bytes_accessed=2 * slots * width + 6 * tokens * width,
            transcendentals=0,
        ),
        name=name,
    )(start, *msgs)


def swap(value, axis, apart):
    return lax.ppermute(value, axis, [(i, i ^ apart) for i in range(lax.axis_size(axis))])


def swap_back(value, apart):
    sections, places = lax.axis_size("section"), lax.axis_size("expert")
    pairs = [
        (s * places + i, (s ^ 1) * places + (i ^ apart)) for s in range(sections) for i in range(places)
    ]
    return lax.ppermute(value, ("section", "expert"), pairs)


def after(*values):
    return lax.optimization_barrier(values)


def cut(weight):
    step = -(-weight.shape[0] // (LANES * CUTS)) * LANES
    return [weight[at : at + step] for at in range(0, weight.shape[0], step)]


def groups_of(experts):
    if experts == 4:
        return [[2], [1, 0], [3]], [[2, 0], [3, 1]]
    order = list(range(experts - 1, -1, -1))
    size = -(-experts // 4)
    groups = [order[i : i + size] for i in range(0, experts, size)]
    return groups, groups


def body(tokens, grad_out, expert_ids, gate_values, w_in, w_out_t):
    tok, grad = tokens[0], grad_out[0]
    ids_t, gates_t = expert_ids[0].T, gate_values[0].T
    experts = lax.axis_size("expert") // 2
    base, extra = slots_of(tok.shape[0], ids_t.shape[0], experts)
    sends, works = groups_of(experts)
    others = range(1, lax.axis_size("dp"))
    w_own, v_own = w_in[0, 0], w_out_t[0, 0]
    sent = [
        dispatch(group, base, extra, ids_t, gates_t, tok, grad, 24 if i else LIMIT, i < len(sends) - 1)
        for i, group in enumerate(sends)
    ]
    w_far = [swap(w_own, "dp", apart) for apart in others]
    w_other, v_other = swap(w_own, "expert", 1), swap(v_own, "expert", 1)
    other_grad = swap(grad, "section", 1)
    v_late, w_other, v_other = after(v_own, w_other, v_other)
    v_far = [swap(v_late, "dp", apart) for apart in others]
    sent[-1], other_grad, w_far = after(sent[-1], other_grad, w_far)
    got = {}
    for group, msgs in zip(sends, sent):
        for dist, msg in zip(group, msgs):
            got[dist] = tuple(swap(part, "expert", 2 * dist) for part in msg) if dist else msg
    first, last = [dist for group in sends[:-1] for dist in group], sends[-1]

    w_far, heads = after(w_far, [got[dist] for dist in first])
    got.update(zip(first, heads))
    w_columns = [[[w_own], [w_other]]]
    w_columns += [[[block], [swap(piece, "expert", 1) for piece in cut(block)]] for block in w_far]
    v_columns = [[[v_own], [v_other]]]
    carried = expert([got[dist] for dist in works[0]], base, extra, w_columns, v_columns, "early")
    v_far, tails, carried = after(v_far, [got[dist][0] for dist in last], carried)
    got.update((dist, (tail,) + got[dist][1:]) for dist, tail in zip(last, tails))
    v_columns += [[[block], [swap(block, "expert", 1)]] for block in v_far]

    total = other_grad
    for i, group in enumerate(works):
        msgs = [got[dist] for dist in group]
        if i == 0:
            backs = expert_late(msgs, base, extra, w_columns[1:], v_columns[1:], carried)
            backs, got = after(backs, got)
        else:
            backs = expert(msgs, base, extra, w_columns, v_columns)
        returned = [swap_back(back, 2 * dist) for dist, back in zip(group, backs)]
        ends = i == len(works) - 1
        total = add_returned(total, returned, extra, BF16 if ends else F32, "finish" if ends else "settle")
    return total[None]


def solution(mesh):
    rows = P("section", ("expert", "dp"), None)
    weights = P("section", "expert", None, "dp")
    return jax.shard_map(
        body,
        mesh=mesh,
        in_specs=(rows, rows, rows, rows, weights, weights),
        out_specs=rows,
        check_vma=False,
    )
```

```python
import functools

import jax
import jax.numpy as jnp
from jax import lax
from jax.experimental import pallas as pl
from jax.experimental.pallas import tpu as pltpu
from jax.sharding import PartitionSpec as P

LANES = 128
TILE = 256
F32 = jnp.float32
BF16 = jnp.bfloat16
MIB = 1 << 20
CHUNK = 512
PARTS = 1
LIMIT = 57
TAIL = 5
CUTS = 3


def slots_of(tok_dev, top, experts):
    capacity = min(tok_dev, max(2, tok_dev * top // experts + 1))
    if capacity % 16 == 1 and capacity > 1:
        return capacity - 1, 1
    return -(-capacity // 16) * 16, 0


def fold_columns(pieces, base):
    return -(-(pieces + 1) // base) * LANES


def sides_of(base):
    return 2 if base % 32 == 0 else 1


def back_shape(base, width, extra):
    sides = sides_of(base)
    return base // sides, sides * width + fold_columns(width // LANES * extra, base // sides)


def place_of(piece, base):
    return piece % base, piece // base * LANES


def fold(ext_ref, row, pieces, first, base):
    for k in range(pieces):
        at, column = place_of(first + k, base)
        ext_ref[at : at + 1, column : column + LANES] = row[:, k * LANES : (k + 1) * LANES]


def unfold(row_ref, at_row, ext, pieces, first, base):
    for k in range(pieces):
        at, column = place_of(first + k, base)
        row_ref[at_row : at_row + 1, k * LANES : (k + 1) * LANES] = ext[at : at + 1, column : column + LANES]


def slot_row(ids, expert):
    tokens = ids.shape[1]
    hit = jnp.where(ids == expert, 1.0, 0.0).astype(F32)
    mask = jnp.sum(hit, axis=0, keepdims=True)
    earlier = lax.broadcasted_iota(jnp.int32, (tokens, tokens), 0) < lax.broadcasted_iota(
        jnp.int32, (tokens, tokens), 1
    )
    before = jnp.dot(
        jnp.broadcast_to(mask, (16, tokens)).astype(BF16),
        jnp.where(earlier, 1.0, 0.0).astype(BF16),
        preferred_element_type=F32,
    )[0:1]
    return jnp.where(mask > 0.5, before, -1.0)


def begin(src, dst, sem):
    copy = pltpu.make_async_copy(src, dst, sem)
    copy.start()
    return copy


def finish(copies):
    for copy in copies:
        copy.wait()


def dispatch_kernel(dists, base, extra, split, ids_hbm, gates_hbm, tok_hbm, grad_hbm, *refs):
    n = len(dists)
    outs, refs = refs[: n * len(split)], refs[n * len(split) :]
    ids_ref, gates_ref, tok_ref, grad_ref, msg_ref, ext_ref, sem_i, sem_t, sem_g, sem_o = refs
    here = lax.axis_index("expert") // 2
    tokens, width = tok_ref.shape
    pieces = width // LANES
    rows = base + 16 * extra
    step = tokens // PARTS
    parts = [pl.ds(i * step, step) for i in range(PARTS)]
    small = [begin(ids_hbm, ids_ref, sem_i.at[0]), begin(gates_hbm, gates_ref, sem_i.at[1])]
    tok_in = [begin(tok_hbm.at[p, :], tok_ref.at[p, :], sem_t.at[i]) for i, p in enumerate(parts)]
    grad_in = [begin(grad_hbm.at[p, :], grad_ref.at[p, :], sem_g.at[i]) for i, p in enumerate(parts)]
    finish(small)
    ids, gates = ids_ref[...], gates_ref[...]
    onehots, scales = [], []
    for dist in dists:
        slot = slot_row(ids, here ^ dist)
        gate = jnp.sum(jnp.where(ids == (here ^ dist), gates, 0.0), axis=0, keepdims=True)
        picks = lax.broadcasted_iota(jnp.int32, (rows, tokens), 0).astype(F32) == slot
        onehots.append(jnp.where(picks, 1.0, 0.0).astype(BF16))
        scales.append(jnp.sum(jnp.where(picks, gate, 0.0), axis=1, keepdims=True))
    ext_ref[...] = jnp.zeros_like(ext_ref)
    count = lax.broadcasted_iota(jnp.int32, (16, tokens), 1) + 1
    for d in range(n):
        holders = lax.dot_general(
            count.astype(F32).astype(BF16), onehots[d], (((1,), (1,)), ((), ())), preferred_element_type=F32
        )
        at, column = place_of(2 * pieces * extra, base)
        ext_ref[d, at : at + 1, column : column + rows] = holders[0:1]
    sent = []
    for part, copies in enumerate((tok_in, grad_in)):
        finish(copies)
        for d in range(n):
            for at in range(0, width, CHUNK):
                value = jnp.dot(
                    onehots[d],
                    (grad_ref if part else tok_ref)[:, at : at + CHUNK],
                    preferred_element_type=F32,
                )
                if part:
                    value = value * scales[d]
                msg_ref[d, :, part * width + at : part * width + at + CHUNK] = value[:base].astype(BF16)
                if extra:
                    first = part * pieces + at // LANES
                    fold(ext_ref.at[d], value[base : base + 1], CHUNK // LANES, first, base)
            stop = (part + 1) * width
            if part:
                msg_ref[d, :, stop:] = ext_ref[d].astype(BF16)
                stop = msg_ref.shape[2]
            for i, (start, end) in enumerate(split):
                low, high = max(start, part * width), min(end, stop)
                if low < high:
                    src = msg_ref.at[d, :, pl.ds(low, high - low)]
                    dst = outs[d * len(split) + i].at[:, pl.ds(low - start, high - low)]
                    sent.append(begin(src, dst, sem_o.at[d, part, i]))
    finish(sent)


def dispatch(dists, base, extra, ids_t, gates_t, tok, grad, limit, whole=True):
    tokens, width = tok.shape
    n, ext = len(dists), fold_columns(2 * width // LANES * extra, base)
    cols = 2 * width + ext
    cutoff = 2 * width - TAIL * LANES
    split = [(0, cols)] if whole else [(0, cutoff), (cutoff, cols)]
    anywhere = pl.BlockSpec(memory_space=pl.ANY)
    outs = pl.pallas_call(
        functools.partial(dispatch_kernel, dists, base, extra, split),
        out_shape=[jax.ShapeDtypeStruct((base, end - start), BF16) for _ in dists for start, end in split],
        in_specs=[anywhere] * 4,
        out_specs=[anywhere] * (n * len(split)),
        scratch_shapes=[
            pltpu.VMEM(ids_t.shape, jnp.int32),
            pltpu.VMEM(gates_t.shape, F32),
            pltpu.VMEM((tokens, width), BF16),
            pltpu.VMEM((tokens, width), BF16),
            pltpu.VMEM((n, base, cols), BF16),
            pltpu.VMEM((n, base, ext), F32),
            pltpu.SemaphoreType.DMA((2,)),
            pltpu.SemaphoreType.DMA((PARTS,)),
            pltpu.SemaphoreType.DMA((PARTS,)),
            pltpu.SemaphoreType.DMA((n, 2, len(split))),
        ],
        compiler_params=pltpu.CompilerParams(vmem_limit_bytes=limit * MIB),
        cost_estimate=pl.CostEstimate(
            flops=4 * n * (base + 16) * tokens * width,
            bytes_accessed=4 * tokens * width + 2 * n * base * cols,
            transcendentals=0,
        ),
        name="dispatch",
    )(ids_t, gates_t, tok, grad)
    return [tuple(outs[i : i + len(split)]) for i in range(0, len(outs), len(split))]


def silu_slope(pre):
    sig = jax.nn.sigmoid(pre)
    return sig * (1.0 + pre * (1.0 - sig))


def begin_weights(pieces, layout, whole, sems):
    half = whole.shape[0] // 2
    core = lax.axis_index("expert") % 2
    copies = {}
    for i, (piece, (block, other, row, columns)) in enumerate(zip(pieces, layout)):
        at = pl.multiple_of((1 - core if other else core) * half + row, 16)
        rows = pl.ds(at, piece.shape[0])
        dst = whole.at[rows, pl.ds(block * columns, columns)]
        copies.setdefault(block, []).append(begin(piece, dst, sems.at[i]))
    return copies


def begin_columns(parts, start, dst, sems):
    copies, at = [], 0
    for i, part in enumerate(parts):
        low, high = max(start, at), min(start + dst.shape[1], at + part.shape[1])
        if low < high:
            src = part.at[:, pl.ds(low - at, high - low)]
            copies.append(begin(src, dst.at[:, pl.ds(low - start, high - low)], sems.at[i]))
        at += part.shape[1]
    return copies


def begin_rows(msgs, rows, ext, start, sems, ext_sems):
    base = msgs[0][0].shape[0]
    width = rows.shape[1]
    copies = []
    for i, parts in enumerate(msgs):
        copies += begin_columns(parts, start, rows.at[pl.ds(i * base, base), :], sems.at[i])
        if ext is not None:
            copies += begin_columns(parts, 2 * width, ext.at[i], ext_sems.at[i])
    return copies


def put_extra(rows, row32, ext, n, base, first):
    row32[...] = jnp.zeros_like(row32)
    for i in range(n):
        unfold(row32, i, ext[i].astype(F32), rows.shape[1] // LANES, first, ext.shape[1])
    rows[n * base :, :] = row32[...].astype(BF16)


def put_back(outs, ext32, back, at, size, n, base, extra, width):
    part = outs[0].shape[0]
    for i in range(n):
        for side in range(base // part):
            first = i * base + side * part
            cols = slice(side * width + at, side * width + at + size)
            outs[i][:, cols] = back[first : first + part].astype(BF16)
        if extra:
            row = back[n * base + i : n * base + i + 1]
            fold(ext32.at[i], row, size // LANES, at // LANES, part)


def expert_kernel(n, base, extra, stage, w_layout, v_layout, lengths, *refs):
    msgs = []
    for length in lengths:
        msgs.append(refs[:length])
        refs = refs[length:]
    w_pieces, refs = refs[: len(w_layout)], refs[len(w_layout) :]
    v_pieces, refs = refs[: len(v_layout)], refs[len(v_layout) :]
    if stage == "late":
        slope, partial, refs = refs[0], refs[1], refs[2:]
        outs, refs = refs[:n], refs[n:]
    elif stage == "early":
        slope_late, partial_out, slope, refs = refs[0], refs[1], refs[2], refs[3:]
    else:
        outs, slope, refs = refs[:n], refs[n], refs[n + 1 :]
    w, v, x, g, act, ext, row32, ext32, sem_x, sem_g, sem_e, sem_w, sem_v = refs
    width = w.shape[0]
    half_ff = w_layout[0][3]
    pieces = width // LANES
    full = n * base
    x_in = []
    if stage != "late":
        x_in = begin_rows(msgs, x, ext, 0, sem_x, sem_e)
    w_in = begin_weights(w_pieces, w_layout, w, sem_w)
    g_in = begin_rows(msgs, g, ext if stage == "late" else None, width, sem_g, sem_e)
    v_in = begin_weights(v_pieces, v_layout, v, sem_v)
    if stage != "late":
        finish(x_in)
        if extra:
            put_extra(x, row32, ext, n, base, 0)
        for block in sorted(w_in):
            finish(w_in[block])
            for at in range(block * half_ff, (block + 1) * half_ff, TILE):
                value = silu_slope(jnp.dot(x[...], w[:, at : at + TILE], preferred_element_type=F32))
                if stage == "early" and block > 0:
                    slope_late[:, at - half_ff : at - half_ff + TILE] = value
                else:
                    slope[:, at : at + TILE] = value
    finish(g_in)
    if extra:
        put_extra(g, row32, ext, n, base, pieces)
    for block in sorted(v_in):
        finish(v_in[block])
        for at in range(block * half_ff, (block + 1) * half_ff, TILE):
            hid = jnp.dot(g[...], v[:, at : at + TILE], preferred_element_type=F32)
            act[:, at : at + TILE] = (hid * slope[:, at : at + TILE]).astype(BF16)
    if stage == "late":
        for block in sorted(w_in):
            finish(w_in[block])
    if stage != "early":
        ext32[...] = jnp.zeros_like(ext32)
        at, column = place_of(2 * pieces * extra, base)
        to, to_column = place_of(pieces * extra, ext32.shape[1])
        for i in range(n):
            holders = ext[i].astype(F32)[at : at + 1, column : column + LANES]
            ext32[i, to : to + 1, to_column : to_column + LANES] = holders
    hidden = act.shape[1]
    for at in range(0, width, TILE):
        cols = slice(at, at + TILE)
        back = lax.dot_general(
            act[...], w[cols, :hidden], (((1,), (1,)), ((), ())), preferred_element_type=F32
        )
        if stage == "early":
            partial_out[:, cols] = back
            continue
        if stage == "late":
            back = back + partial[:, cols]
        put_back(outs, ext32, back, at, TILE, n, base, extra, width)
    if stage != "early":
        for i in range(n):
            outs[i][:, sides_of(base) * width :] = ext32[i].astype(BF16)


def late_kernel(n, base, extra, blocks, w_layout, v_layout, *refs):
    msgs, refs = refs[:n], refs[n:]
    w_pieces, refs = refs[: len(w_layout)], refs[len(w_layout) :]
    v_pieces, refs = refs[: len(v_layout)], refs[len(v_layout) :]
    slope, partial, refs = refs[0], refs[1], refs[2:]
    outs, (g, act, ext, row32, ext32, sem_g, sem_e) = refs[:n], refs[n:]
    width = g.shape[1]
    half, block_ff = width // 2, v_layout[0][3]
    pieces = width // LANES
    full = n * base
    core = lax.axis_index("expert") % 2
    copies = begin_rows([(msg,) for msg in msgs], g, ext, width, sem_g, sem_e)
    finish(copies)
    if extra:
        put_extra(g, row32, ext, n, base, pieces)
    ext32[...] = jnp.zeros_like(ext32)
    at, column = place_of(2 * pieces * extra, base)
    to, to_column = place_of(pieces * extra, ext32.shape[1])
    for i in range(n):
        holders = ext[i].astype(F32)[at : at + 1, column : column + LANES]
        ext32[i, to : to + 1, to_column : to_column + LANES] = holders

    def work(here):
        for block in range(blocks):
            for at in range(0, block_ff, TILE):
                hid = None
                for ref, (of, other, row, _) in zip(v_pieces, v_layout):
                    if of == block:
                        first = (1 - here if other else here) * half + row
                        term = jnp.dot(
                            g[:, first : first + ref.shape[0]],
                            ref[:, at : at + TILE],
                            preferred_element_type=F32,
                        )
                        hid = term if hid is None else hid + term
                cols = slice(block * block_ff + at, block * block_ff + at + TILE)
                act[:, cols] = (hid * slope[:, cols]).astype(BF16)
        places = {}
        for ref, (of, other, row, _) in zip(w_pieces, w_layout):
            for at in range(0, ref.shape[0], TILE):
                size = min(TILE, ref.shape[0] - at)
                first = (1 - here if other else here) * half + row + at
                places.setdefault((first, size), []).append((of, ref, at))
        for (first, size), terms in sorted(places.items()):
            cols = slice(first, first + size)
            back = partial[:, cols]
            for of, ref, at in terms:
                back = back + lax.dot_general(
                    act[:, of * block_ff : (of + 1) * block_ff],
                    ref[at : at + size, :],
                    (((1,), (1,)), ((), ())),
                    preferred_element_type=F32,
                )
            put_back(outs, ext32, back, first, size, n, base, extra, width)

    for here in range(2):
        pl.when(core == here)(functools.partial(work, here))
    for i in range(n):
        outs[i][:, sides_of(base) * width :] = ext32[i].astype(BF16)


def flat(columns):
    arrays, layout = [], []
    for block, cores in enumerate(columns):
        for other, pieces in enumerate(cores):
            row = 0
            for piece in pieces:
                arrays.append(piece)
                layout.append((block, other, row, piece.shape[1]))
                row += piece.shape[0]
    return arrays, layout, row


def expert_late(msgs, base, extra, w_columns, v_columns, carried):
    n = len(msgs)
    msgs = [message for (message,) in msgs]
    w_pieces, w_layout, half = flat(w_columns)
    v_pieces, v_layout, _ = flat(v_columns)
    width, ff = 2 * half, len(w_columns) * w_layout[0][3]
    rows = n * base + -(-n * extra // 16) * 16
    ext = fold_columns(2 * width // LANES * extra, base)
    back_rows, back_cols = back_shape(base, width, extra)
    anywhere, vmem = pl.BlockSpec(memory_space=pl.ANY), pl.BlockSpec(memory_space=pltpu.VMEM)
    return pl.pallas_call(
        functools.partial(late_kernel, n, base, extra, len(w_columns), w_layout, v_layout),
        out_shape=[jax.ShapeDtypeStruct((back_rows, back_cols), BF16) for _ in msgs],
        in_specs=[anywhere] * n + [vmem] * (len(w_pieces) + len(v_pieces) + len(carried)),
        out_specs=[vmem] * n,
        scratch_shapes=[
            pltpu.VMEM((rows, width), BF16),
            pltpu.VMEM((rows, ff), BF16),
            pltpu.VMEM((n, base, ext), BF16),
            pltpu.VMEM((max(16, rows - n * base), width), F32),
            pltpu.VMEM((n, back_rows, back_cols - sides_of(base) * width), F32),
            pltpu.SemaphoreType.DMA((n, 1)),
            pltpu.SemaphoreType.DMA((n, 1)),
        ],
        compiler_params=pltpu.CompilerParams(vmem_limit_bytes=24 * MIB),
        cost_estimate=pl.CostEstimate(
            flops=4 * rows * width * ff,
            bytes_accessed=4 * width * ff + 8 * rows * width,
            transcendentals=0,
        ),
        name="expert_late",
    )(*msgs, *w_pieces, *v_pieces, *carried)


def expert(msgs, base, extra, w_columns, v_columns, stage="whole", carried=()):
    n = len(msgs)

    lengths = [len(parts) for parts in msgs]
    most, parts = max(lengths), [part for message in msgs for part in message]
    w_pieces, w_layout, half = flat(w_columns)
    v_pieces, v_layout, _ = flat(v_columns)
    width, block_ff = 2 * half, w_layout[0][3]
    w_ff, v_ff = len(w_columns) * block_ff, len(v_columns) * block_ff
    rows = n * base + -(-n * extra // 16) * 16
    ext = fold_columns(2 * width // LANES * extra, base)
    back_rows, back_cols = back_shape(base, width, extra)
    anywhere, vmem = pl.BlockSpec(memory_space=pl.ANY), pl.BlockSpec(memory_space=pltpu.VMEM)
    spare = max(16, rows - n * base)
    own_slope = [] if stage == "late" else [pltpu.VMEM((rows, v_ff), F32)]
    if stage == "early":
        out_shape = [
            jax.ShapeDtypeStruct((rows, w_ff - block_ff), F32),
            jax.ShapeDtypeStruct((rows, width), F32),
        ]
    else:
        out_shape = [jax.ShapeDtypeStruct((back_rows, back_cols), BF16) for _ in msgs]
    return pl.pallas_call(
        functools.partial(expert_kernel, n, base, extra, stage, w_layout, v_layout, lengths),
        out_shape=out_shape,
        in_specs=[anywhere] * (len(parts) + len(w_pieces) + len(v_pieces)) + [vmem] * len(carried),
        out_specs=[vmem] * len(out_shape),
        scratch_shapes=own_slope
        + [
            pltpu.VMEM((width, w_ff), BF16),
            pltpu.VMEM((width, v_ff), BF16),
            pltpu.VMEM((rows, width), BF16),
            pltpu.VMEM((rows, width), BF16),
            pltpu.VMEM((rows, v_ff), BF16),
            pltpu.VMEM((n, base, ext), BF16),
            pltpu.VMEM((spare, width), F32),
            pltpu.VMEM((n, back_rows, back_cols - sides_of(base) * width), F32),
            pltpu.SemaphoreType.DMA((n, most)),
            pltpu.SemaphoreType.DMA((n, most)),
            pltpu.SemaphoreType.DMA((n, most)),
            pltpu.SemaphoreType.DMA((len(w_pieces),)),
            pltpu.SemaphoreType.DMA((len(v_pieces),)),
        ],
        compiler_params=pltpu.CompilerParams(vmem_limit_bytes=24 * MIB),
        cost_estimate=pl.CostEstimate(
            flops=0 if stage == "early" else 2 * rows * width * (w_ff + 2 * v_ff),
            bytes_accessed=0 if stage == "early" else 2 * width * (w_ff + v_ff) + 6 * rows * width,
            transcendentals=0 if stage == "early" else rows * w_ff,
        ),
        name="expert_" + stage,
    )(*parts, *w_pieces, *v_pieces, *carried)


def add_kernel(n, base, extra, start_ref, *refs):
    msgs, (out_hbm, out, rows, ext, row32, places, sem_b, sem_e, sem_o) = refs[:n], refs[n:]
    tokens, width = start_ref.shape
    pieces = width // LANES
    part, sides = msgs[0].shape[0], sides_of(base)
    ext_in = [
        begin(msg.at[:, pl.ds(sides * width, ext.shape[2])], ext.at[i], sem_e.at[i])
        for i, msg in enumerate(msgs)
    ]
    rows_in = []
    for i, msg in enumerate(msgs):
        for side in range(sides):
            src = msg.at[:, pl.ds(side * width, width)]
            dst = rows.at[pl.ds(i * base + side * part, part), :]
            rows_in.append(begin(src, dst, sem_b.at[i, side]))
    finish(ext_in)
    folded = jnp.zeros((tokens, 16), F32)
    at, column = place_of(pieces * extra, part)
    for i in range(n):
        holders = ext[i].astype(F32)[at : at + 1, column : column + LANES]
        token = lax.broadcasted_iota(jnp.int32, (tokens, LANES), 0) + 1
        place = jnp.where(holders == token.astype(F32), 1.0, 0.0)
        places[:, i * base : (i + 1) * base] = place[:, :base].astype(BF16)
        if extra:
            mine = lax.broadcasted_iota(jnp.int32, (tokens, 16), 1) == i
            folded = folded + jnp.where(mine, place[:, base : base + 1], 0.0)
    if extra:
        places[:, n * base :] = folded.astype(BF16)
        put_extra(rows, row32, ext, n, base, 0)
    place = places[...]
    finish(rows_in)
    step = width // 4
    sent = []
    for h in range(4):
        for at in range(h * step, (h + 1) * step, TILE):
            cols = slice(at, min(at + TILE, (h + 1) * step))
            back = jnp.dot(place, rows[:, cols], preferred_element_type=F32)
            out[:, cols] = (start_ref[:, cols].astype(F32) + back).astype(out.dtype)
        cols = pl.ds(h * step, step)
        sent.append(begin(out.at[:, cols], out_hbm.at[:, cols], sem_o.at[h]))
    finish(sent)


def add_returned(start, msgs, base, extra, kind, name):
    tokens, width = start.shape
    n = len(msgs)
    slots = n * base + 16 * extra
    part, cols = msgs[0].shape
    sides = sides_of(base)
    anywhere, vmem = pl.BlockSpec(memory_space=pl.ANY), pl.BlockSpec(memory_space=pltpu.VMEM)
    return pl.pallas_call(
        functools.partial(add_kernel, n, base, extra),
        out_shape=jax.ShapeDtypeStruct((tokens, width), kind),
        in_specs=[vmem] + [anywhere] * n,
        out_specs=anywhere,
        scratch_shapes=[
            pltpu.VMEM((tokens, width), kind),
            pltpu.VMEM((slots, width), BF16),
            pltpu.VMEM((n, part, cols - sides * width), BF16),
            pltpu.VMEM((16, width), F32),
            pltpu.VMEM((tokens, slots), BF16),
            pltpu.SemaphoreType.DMA((n, sides)),
            pltpu.SemaphoreType.DMA((n,)),
            pltpu.SemaphoreType.DMA((4,)),
        ],
        compiler_params=pltpu.CompilerParams(vmem_limit_bytes=24 * MIB),
        cost_estimate=pl.CostEstimate(
            flops=2 * slots * tokens * width,
            bytes_accessed=2 * slots * width + 6 * tokens * width,
            transcendentals=0,
        ),
        name=name,
    )(start, *msgs)


def swap(value, axis, apart):
    return lax.ppermute(value, axis, [(i, i ^ apart) for i in range(lax.axis_size(axis))])


def swap_back(value, apart):
    sections, places = lax.axis_size("section"), lax.axis_size("expert")
    pairs = [
        (s * places + i, (s ^ 1) * places + (i ^ apart)) for s in range(sections) for i in range(places)
    ]
    return lax.ppermute(value, ("section", "expert"), pairs)


def after(*values):
    return lax.optimization_barrier(values)


def cut(weight):
    step = -(-weight.shape[0] // (LANES * CUTS)) * LANES
    return [weight[at : at + step] for at in range(0, weight.shape[0], step)]


def groups_of(experts):
    if experts == 4:
        return [[2], [1, 0], [3]], [[1, 2], [0, 3]]
    order = list(range(experts - 1, -1, -1))
    size = -(-experts // 4)
    groups = [order[i : i + size] for i in range(0, experts, size)]
    return groups, groups


def body(tokens, grad_out, expert_ids, gate_values, w_in, w_out_t):
    tok, grad = tokens[0], grad_out[0]
    ids_t, gates_t = expert_ids[0].T, gate_values[0].T
    experts = lax.axis_size("expert") // 2
    base, extra = slots_of(tok.shape[0], ids_t.shape[0], experts)
    sends, works = groups_of(experts)
    others = range(1, lax.axis_size("dp"))
    w_own, v_own = w_in[0, 0], w_out_t[0, 0]
    sent = [
        dispatch(group, base, extra, ids_t, gates_t, tok, grad, 24 if i else LIMIT, i < len(sends) - 1)
        for i, group in enumerate(sends)
    ]
    w_far = [swap(w_own, "dp", apart) for apart in others]
    w_other, v_other = swap(w_own, "expert", 1), swap(v_own, "expert", 1)
    other_grad = swap(grad, "section", 1)
    v_late, w_other, v_other = after(v_own, w_other, v_other)
    v_far = [swap(v_late, "dp", apart) for apart in others]
    sent[-1], other_grad, w_far = after(sent[-1], other_grad, w_far)
    got = {}
    for group, msgs in zip(sends, sent):
        for dist, msg in zip(group, msgs):
            got[dist] = tuple(swap(part, "expert", 2 * dist) for part in msg) if dist else msg
    first, last = [dist for group in sends[:-1] for dist in group], sends[-1]

    w_far, heads = after(w_far, [got[dist] for dist in first])
    got.update(zip(first, heads))
    w_columns = [[[w_own], [w_other]]]
    w_columns += [[[block], [swap(piece, "expert", 1) for piece in cut(block)]] for block in w_far]
    v_columns = [[[v_own], [v_other]]]
    carried = expert([got[dist] for dist in works[0]], base, extra, w_columns, v_columns, "early")
    v_far, tails, carried = after(v_far, [got[dist][0] for dist in last], carried)
    got.update((dist, (tail,) + got[dist][1:]) for dist, tail in zip(last, tails))
    v_columns += [[[block], [swap(block, "expert", 1)]] for block in v_far]

    total = other_grad
    for i, group in enumerate(works):
        msgs = [got[dist] for dist in group]
        if i == 0:
            backs = expert_late(msgs, base, extra, w_columns[1:], v_columns[1:], carried)
            backs, got = after(backs, got)
        else:
            backs = expert(msgs, base, extra, w_columns, v_columns)
        returned = [swap_back(back, 2 * dist) for dist, back in zip(group, backs)]
        ends = i == len(works) - 1
        total = add_returned(total, returned, base, extra, BF16 if ends else F32, "finish" if ends else "settle")
    return total[None]


def solution(mesh):
    rows = P("section", ("expert", "dp"), None)
    weights = P("section", "expert", None, "dp")
    return jax.shard_map(
        body,
        mesh=mesh,
        in_specs=(rows, rows, rows, rows, weights, weights),
        out_specs=rows,
        check_vma=False,
    )
```

```python
import functools

import jax
import jax.numpy as jnp
from jax import lax
from jax.experimental import pallas as pl
from jax.experimental.pallas import tpu as pltpu
from jax.sharding import PartitionSpec as P

LANES = 128
TILE = 256
F32 = jnp.float32
BF16 = jnp.bfloat16
MIB = 1 << 20
CHUNK = 512
PARTS = 1
LIMIT = 57
TAIL = 8
CUTS = 3


def slots_of(tok_dev, top, experts):
    capacity = min(tok_dev, max(2, tok_dev * top // experts + 1))
    if capacity % 16 == 1 and capacity > 1:
        return capacity - 1, 1
    return -(-capacity // 16) * 16, 0


def fold_columns(pieces, base):
    return -(-(pieces + 1) // base) * LANES


def sides_of(base):
    return 2 if base % 32 == 0 else 1


def back_shape(base, width, extra):
    sides = sides_of(base)
    return base // sides, sides * width + fold_columns(width // LANES * extra, base // sides)


def place_of(piece, base):
    return piece % base, piece // base * LANES


def fold(ext_ref, row, pieces, first, base):
    for k in range(pieces):
        at, column = place_of(first + k, base)
        ext_ref[at : at + 1, column : column + LANES] = row[:, k * LANES : (k + 1) * LANES]


def unfold(row_ref, at_row, ext, pieces, first, base):
    for k in range(pieces):
        at, column = place_of(first + k, base)
        row_ref[at_row : at_row + 1, k * LANES : (k + 1) * LANES] = ext[at : at + 1, column : column + LANES]


def slot_row(ids, expert):
    tokens = ids.shape[1]
    hit = jnp.where(ids == expert, 1.0, 0.0).astype(F32)
    mask = jnp.sum(hit, axis=0, keepdims=True)
    earlier = lax.broadcasted_iota(jnp.int32, (tokens, tokens), 0) < lax.broadcasted_iota(
        jnp.int32, (tokens, tokens), 1
    )
    before = jnp.dot(
        jnp.broadcast_to(mask, (16, tokens)).astype(BF16),
        jnp.where(earlier, 1.0, 0.0).astype(BF16),
        preferred_element_type=F32,
    )[0:1]
    return jnp.where(mask > 0.5, before, -1.0)


def begin(src, dst, sem):
    copy = pltpu.make_async_copy(src, dst, sem)
    copy.start()
    return copy


def finish(copies):
    for copy in copies:
        copy.wait()


def dispatch_kernel(dists, base, extra, split, ids_hbm, gates_hbm, tok_hbm, grad_hbm, *refs):
    n = len(dists)
    outs, refs = refs[: n * len(split)], refs[n * len(split) :]
    ids_ref, gates_ref, tok_ref, grad_ref, msg_ref, ext_ref, sem_i, sem_t, sem_g, sem_o = refs
    here = lax.axis_index("expert") // 2
    tokens, width = tok_ref.shape
    pieces = width // LANES
    rows = base + 16 * extra
    step = tokens // PARTS
    parts = [pl.ds(i * step, step) for i in range(PARTS)]
    small = [begin(ids_hbm, ids_ref, sem_i.at[0]), begin(gates_hbm, gates_ref, sem_i.at[1])]
    tok_in = [begin(tok_hbm.at[p, :], tok_ref.at[p, :], sem_t.at[i]) for i, p in enumerate(parts)]
    grad_in = [begin(grad_hbm.at[p, :], grad_ref.at[p, :], sem_g.at[i]) for i, p in enumerate(parts)]
    finish(small)
    ids, gates = ids_ref[...], gates_ref[...]
    onehots, scales = [], []
    for dist in dists:
        slot = slot_row(ids, here ^ dist)
        gate = jnp.sum(jnp.where(ids == (here ^ dist), gates, 0.0), axis=0, keepdims=True)
        picks = lax.broadcasted_iota(jnp.int32, (rows, tokens), 0).astype(F32) == slot
        onehots.append(jnp.where(picks, 1.0, 0.0).astype(BF16))
        scales.append(jnp.sum(jnp.where(picks, gate, 0.0), axis=1, keepdims=True))
    ext_ref[...] = jnp.zeros_like(ext_ref)
    count = lax.broadcasted_iota(jnp.int32, (16, tokens), 1) + 1
    for d in range(n):
        holders = lax.dot_general(
            count.astype(F32).astype(BF16), onehots[d], (((1,), (1,)), ((), ())), preferred_element_type=F32
        )
        at, column = place_of(2 * pieces * extra, base)
        ext_ref[d, at : at + 1, column : column + rows] = holders[0:1]
    sent = []
    for part, copies in enumerate((tok_in, grad_in)):
        finish(copies)
        for d in range(n):
            for at in range(0, width, CHUNK):
                value = jnp.dot(
                    onehots[d],
                    (grad_ref if part else tok_ref)[:, at : at + CHUNK],
                    preferred_element_type=F32,
                )
                if part:
                    value = value * scales[d]
                msg_ref[d, :, part * width + at : part * width + at + CHUNK] = value[:base].astype(BF16)
                if extra:
                    first = part * pieces + at // LANES
                    fold(ext_ref.at[d], value[base : base + 1], CHUNK // LANES, first, base)
            stop = (part + 1) * width
            if part:
                msg_ref[d, :, stop:] = ext_ref[d].astype(BF16)
                stop = msg_ref.shape[2]
            for i, (start, end) in enumerate(split):
                low, high = max(start, part * width), min(end, stop)
                if low < high:
                    src = msg_ref.at[d, :, pl.ds(low, high - low)]
                    dst = outs[d * len(split) + i].at[:, pl.ds(low - start, high - low)]
                    sent.append(begin(src, dst, sem_o.at[d, part, i]))
    finish(sent)


def dispatch(dists, base, extra, ids_t, gates_t, tok, grad, limit, whole=True):
    tokens, width = tok.shape
    n, ext = len(dists), fold_columns(2 * width // LANES * extra, base)
    cols = 2 * width + ext
    cutoff = 2 * width - TAIL * LANES
    split = [(0, cols)] if whole else [(0, cutoff), (cutoff, cols)]
    anywhere = pl.BlockSpec(memory_space=pl.ANY)
    outs = pl.pallas_call(
        functools.partial(dispatch_kernel, dists, base, extra, split),
        out_shape=[jax.ShapeDtypeStruct((base, end - start), BF16) for _ in dists for start, end in split],
        in_specs=[anywhere] * 4,
        out_specs=[anywhere] * (n * len(split)),
        scratch_shapes=[
            pltpu.VMEM(ids_t.shape, jnp.int32),
            pltpu.VMEM(gates_t.shape, F32),
            pltpu.VMEM((tokens, width), BF16),
            pltpu.VMEM((tokens, width), BF16),
            pltpu.VMEM((n, base, cols), BF16),
            pltpu.VMEM((n, base, ext), F32),
            pltpu.SemaphoreType.DMA((2,)),
            pltpu.SemaphoreType.DMA((PARTS,)),
            pltpu.SemaphoreType.DMA((PARTS,)),
            pltpu.SemaphoreType.DMA((n, 2, len(split))),
        ],
        compiler_params=pltpu.CompilerParams(vmem_limit_bytes=limit * MIB),
        cost_estimate=pl.CostEstimate(
            flops=4 * n * (base + 16) * tokens * width,
            bytes_accessed=4 * tokens * width + 2 * n * base * cols,
            transcendentals=0,
        ),
        name="dispatch",
    )(ids_t, gates_t, tok, grad)
    return [tuple(outs[i : i + len(split)]) for i in range(0, len(outs), len(split))]


def silu_slope(pre):
    sig = jax.nn.sigmoid(pre)
    return sig * (1.0 + pre * (1.0 - sig))


def begin_weights(pieces, layout, whole, sems):
    half = whole.shape[0] // 2
    core = lax.axis_index("expert") % 2
    copies = {}
    for i, (piece, (block, other, row, columns)) in enumerate(zip(pieces, layout)):
        at = pl.multiple_of((1 - core if other else core) * half + row, 16)
        rows = pl.ds(at, piece.shape[0])
        dst = whole.at[rows, pl.ds(block * columns, columns)]
        copies.setdefault(block, []).append(begin(piece, dst, sems.at[i]))
    return copies


def begin_columns(parts, start, dst, sems):
    copies, at = [], 0
    for i, part in enumerate(parts):
        low, high = max(start, at), min(start + dst.shape[1], at + part.shape[1])
        if low < high:
            src = part.at[:, pl.ds(low - at, high - low)]
            copies.append(begin(src, dst.at[:, pl.ds(low - start, high - low)], sems.at[i]))
        at += part.shape[1]
    return copies


def begin_rows(msgs, rows, ext, start, sems, ext_sems):
    base = msgs[0][0].shape[0]
    width = rows.shape[1]
    copies = []
    for i, parts in enumerate(msgs):
        copies += begin_columns(parts, start, rows.at[pl.ds(i * base, base), :], sems.at[i])
        if ext is not None:
            copies += begin_columns(parts, 2 * width, ext.at[i], ext_sems.at[i])
    return copies


def put_extra(rows, row32, ext, n, base, first):
    row32[...] = jnp.zeros_like(row32)
    for i in range(n):
        unfold(row32, i, ext[i].astype(F32), rows.shape[1] // LANES, first, ext.shape[1])
    rows[n * base :, :] = row32[...].astype(BF16)


def put_back(outs, ext32, back, at, size, n, base, extra, width):
    part = outs[0].shape[0]
    for i in range(n):
        for side in range(base // part):
            first = i * base + side * part
            cols = slice(side * width + at, side * width + at + size)
            outs[i][:, cols] = back[first : first + part].astype(BF16)
        if extra:
            row = back[n * base + i : n * base + i + 1]
            fold(ext32.at[i], row, size // LANES, at // LANES, part)


def expert_kernel(n, base, extra, stage, w_layout, v_layout, lengths, *refs):
    msgs = []
    for length in lengths:
        msgs.append(refs[:length])
        refs = refs[length:]
    w_pieces, refs = refs[: len(w_layout)], refs[len(w_layout) :]
    v_pieces, refs = refs[: len(v_layout)], refs[len(v_layout) :]
    if stage == "late":
        slope, partial, refs = refs[0], refs[1], refs[2:]
        outs, refs = refs[:n], refs[n:]
    elif stage == "early":
        slope_late, partial_out, slope, refs = refs[0], refs[1], refs[2], refs[3:]
    else:
        outs, slope, refs = refs[:n], refs[n], refs[n + 1 :]
    w, v, x, g, act, ext, row32, ext32, sem_x, sem_g, sem_e, sem_w, sem_v = refs
    width = w.shape[0]
    half_ff = w_layout[0][3]
    pieces = width // LANES
    full = n * base
    x_in = []
    if stage != "late":
        x_in = begin_rows(msgs, x, ext, 0, sem_x, sem_e)
    w_in = begin_weights(w_pieces, w_layout, w, sem_w)
    g_in = begin_rows(msgs, g, ext if stage == "late" else None, width, sem_g, sem_e)
    v_in = begin_weights(v_pieces, v_layout, v, sem_v)
    if stage != "late":
        finish(x_in)
        if extra:
            put_extra(x, row32, ext, n, base, 0)
        for block in sorted(w_in):
            finish(w_in[block])
            for at in range(block * half_ff, (block + 1) * half_ff, TILE):
                value = silu_slope(jnp.dot(x[...], w[:, at : at + TILE], preferred_element_type=F32))
                if stage == "early" and block > 0:
                    slope_late[:, at - half_ff : at - half_ff + TILE] = value
                else:
                    slope[:, at : at + TILE] = value
    finish(g_in)
    if extra:
        put_extra(g, row32, ext, n, base, pieces)
    for block in sorted(v_in):
        finish(v_in[block])
        for at in range(block * half_ff, (block + 1) * half_ff, TILE):
            hid = jnp.dot(g[...], v[:, at : at + TILE], preferred_element_type=F32)
            act[:, at : at + TILE] = (hid * slope[:, at : at + TILE]).astype(BF16)
    if stage == "late":
        for block in sorted(w_in):
            finish(w_in[block])
    if stage != "early":
        ext32[...] = jnp.zeros_like(ext32)
        at, column = place_of(2 * pieces * extra, base)
        to, to_column = place_of(pieces * extra, ext32.shape[1])
        for i in range(n):
            holders = ext[i].astype(F32)[at : at + 1, column : column + LANES]
            ext32[i, to : to + 1, to_column : to_column + LANES] = holders
    hidden = act.shape[1]
    for at in range(0, width, TILE):
        cols = slice(at, at + TILE)
        back = lax.dot_general(
            act[...], w[cols, :hidden], (((1,), (1,)), ((), ())), preferred_element_type=F32
        )
        if stage == "early":
            partial_out[:, cols] = back
            continue
        if stage == "late":
            back = back + partial[:, cols]
        put_back(outs, ext32, back, at, TILE, n, base, extra, width)
    if stage != "early":
        for i in range(n):
            outs[i][:, sides_of(base) * width :] = ext32[i].astype(BF16)


def late_kernel(n, base, extra, blocks, w_layout, v_layout, *refs):
    msgs, refs = refs[:n], refs[n:]
    w_pieces, refs = refs[: len(w_layout)], refs[len(w_layout) :]
    v_pieces, refs = refs[: len(v_layout)], refs[len(v_layout) :]
    slope, partial, refs = refs[0], refs[1], refs[2:]
    outs, (g, act, ext, row32, ext32, sem_g, sem_e) = refs[:n], refs[n:]
    width = g.shape[1]
    half, block_ff = width // 2, v_layout[0][3]
    pieces = width // LANES
    full = n * base
    core = lax.axis_index("expert") % 2
    copies = begin_rows([(msg,) for msg in msgs], g, ext, width, sem_g, sem_e)
    finish(copies)
    if extra:
        put_extra(g, row32, ext, n, base, pieces)
    ext32[...] = jnp.zeros_like(ext32)
    at, column = place_of(2 * pieces * extra, base)
    to, to_column = place_of(pieces * extra, ext32.shape[1])
    for i in range(n):
        holders = ext[i].astype(F32)[at : at + 1, column : column + LANES]
        ext32[i, to : to + 1, to_column : to_column + LANES] = holders

    def work(here):
        for block in range(blocks):
            for at in range(0, block_ff, TILE):
                hid = None
                for ref, (of, other, row, _) in zip(v_pieces, v_layout):
                    if of == block:
                        first = (1 - here if other else here) * half + row
                        term = jnp.dot(
                            g[:, first : first + ref.shape[0]],
                            ref[:, at : at + TILE],
                            preferred_element_type=F32,
                        )
                        hid = term if hid is None else hid + term
                cols = slice(block * block_ff + at, block * block_ff + at + TILE)
                act[:, cols] = (hid * slope[:, cols]).astype(BF16)
        places = {}
        for ref, (of, other, row, _) in zip(w_pieces, w_layout):
            for at in range(0, ref.shape[0], TILE):
                size = min(TILE, ref.shape[0] - at)
                first = (1 - here if other else here) * half + row + at
                places.setdefault((first, size), []).append((of, ref, at))
        for (first, size), terms in sorted(places.items()):
            cols = slice(first, first + size)
            back = partial[:, cols]
            for of, ref, at in terms:
                back = back + lax.dot_general(
                    act[:, of * block_ff : (of + 1) * block_ff],
                    ref[at : at + size, :],
                    (((1,), (1,)), ((), ())),
                    preferred_element_type=F32,
                )
            put_back(outs, ext32, back, first, size, n, base, extra, width)

    for here in range(2):
        pl.when(core == here)(functools.partial(work, here))
    for i in range(n):
        outs[i][:, sides_of(base) * width :] = ext32[i].astype(BF16)


def flat(columns):
    arrays, layout = [], []
    for block, cores in enumerate(columns):
        for other, pieces in enumerate(cores):
            row = 0
            for piece in pieces:
                arrays.append(piece)
                layout.append((block, other, row, piece.shape[1]))
                row += piece.shape[0]
    return arrays, layout, row


def expert_late(msgs, base, extra, w_columns, v_columns, carried):
    n = len(msgs)
    msgs = [message for (message,) in msgs]
    w_pieces, w_layout, half = flat(w_columns)
    v_pieces, v_layout, _ = flat(v_columns)
    width, ff = 2 * half, len(w_columns) * w_layout[0][3]
    rows = n * base + -(-n * extra // 16) * 16
    ext = fold_columns(2 * width // LANES * extra, base)
    back_rows, back_cols = back_shape(base, width, extra)
    anywhere, vmem = pl.BlockSpec(memory_space=pl.ANY), pl.BlockSpec(memory_space=pltpu.VMEM)
    return pl.pallas_call(
        functools.partial(late_kernel, n, base, extra, len(w_columns), w_layout, v_layout),
        out_shape=[jax.ShapeDtypeStruct((back_rows, back_cols), BF16) for _ in msgs],
        in_specs=[anywhere] * n + [vmem] * (len(w_pieces) + len(v_pieces) + len(carried)),
        out_specs=[vmem] * n,
        scratch_shapes=[
            pltpu.VMEM((rows, width), BF16),
            pltpu.VMEM((rows, ff), BF16),
            pltpu.VMEM((n, base, ext), BF16),
            pltpu.VMEM((max(16, rows - n * base), width), F32),
            pltpu.VMEM((n, back_rows, back_cols - sides_of(base) * width), F32),
            pltpu.SemaphoreType.DMA((n, 1)),
            pltpu.SemaphoreType.DMA((n, 1)),
        ],
        compiler_params=pltpu.CompilerParams(vmem_limit_bytes=24 * MIB),
        cost_estimate=pl.CostEstimate(
            flops=4 * rows * width * ff,
            bytes_accessed=4 * width * ff + 8 * rows * width,
            transcendentals=0,
        ),
        name="expert_late",
    )(*msgs, *w_pieces, *v_pieces, *carried)


def expert(msgs, base, extra, w_columns, v_columns, stage="whole", carried=()):
    n = len(msgs)

    lengths = [len(parts) for parts in msgs]
    most, parts = max(lengths), [part for message in msgs for part in message]
    w_pieces, w_layout, half = flat(w_columns)
    v_pieces, v_layout, _ = flat(v_columns)
    width, block_ff = 2 * half, w_layout[0][3]
    w_ff, v_ff = len(w_columns) * block_ff, len(v_columns) * block_ff
    rows = n * base + -(-n * extra // 16) * 16
    ext = fold_columns(2 * width // LANES * extra, base)
    back_rows, back_cols = back_shape(base, width, extra)
    anywhere, vmem = pl.BlockSpec(memory_space=pl.ANY), pl.BlockSpec(memory_space=pltpu.VMEM)
    spare = max(16, rows - n * base)
    own_slope = [] if stage == "late" else [pltpu.VMEM((rows, v_ff), F32)]
    if stage == "early":
        out_shape = [
            jax.ShapeDtypeStruct((rows, w_ff - block_ff), F32),
            jax.ShapeDtypeStruct((rows, width), F32),
        ]
    else:
        out_shape = [jax.ShapeDtypeStruct((back_rows, back_cols), BF16) for _ in msgs]
    return pl.pallas_call(
        functools.partial(expert_kernel, n, base, extra, stage, w_layout, v_layout, lengths),
        out_shape=out_shape,
        in_specs=[anywhere] * (len(parts) + len(w_pieces) + len(v_pieces)) + [vmem] * len(carried),
        out_specs=[vmem] * len(out_shape),
        scratch_shapes=own_slope
        + [
            pltpu.VMEM((width, w_ff), BF16),
            pltpu.VMEM((width, v_ff), BF16),
            pltpu.VMEM((rows, width), BF16),
            pltpu.VMEM((rows, width), BF16),
            pltpu.VMEM((rows, v_ff), BF16),
            pltpu.VMEM((n, base, ext), BF16),
            pltpu.VMEM((spare, width), F32),
            pltpu.VMEM((n, back_rows, back_cols - sides_of(base) * width), F32),
            pltpu.SemaphoreType.DMA((n, most)),
            pltpu.SemaphoreType.DMA((n, most)),
            pltpu.SemaphoreType.DMA((n, most)),
            pltpu.SemaphoreType.DMA((len(w_pieces),)),
            pltpu.SemaphoreType.DMA((len(v_pieces),)),
        ],
        compiler_params=pltpu.CompilerParams(vmem_limit_bytes=24 * MIB),
        cost_estimate=pl.CostEstimate(
            flops=0 if stage == "early" else 2 * rows * width * (w_ff + 2 * v_ff),
            bytes_accessed=0 if stage == "early" else 2 * width * (w_ff + v_ff) + 6 * rows * width,
            transcendentals=0 if stage == "early" else rows * w_ff,
        ),
        name="expert_" + stage,
    )(*parts, *w_pieces, *v_pieces, *carried)


def add_kernel(n, base, extra, start_ref, *refs):
    msgs, (out_hbm, out, rows, ext, row32, places, sem_b, sem_e, sem_o) = refs[:n], refs[n:]
    tokens, width = start_ref.shape
    pieces = width // LANES
    part, sides = msgs[0].shape[0], sides_of(base)
    ext_in = [
        begin(msg.at[:, pl.ds(sides * width, ext.shape[2])], ext.at[i], sem_e.at[i])
        for i, msg in enumerate(msgs)
    ]
    rows_in = []
    for i, msg in enumerate(msgs):
        for side in range(sides):
            src = msg.at[:, pl.ds(side * width, width)]
            dst = rows.at[pl.ds(i * base + side * part, part), :]
            rows_in.append(begin(src, dst, sem_b.at[i, side]))
    finish(ext_in)
    folded = jnp.zeros((tokens, 16), F32)
    at, column = place_of(pieces * extra, part)
    for i in range(n):
        holders = ext[i].astype(F32)[at : at + 1, column : column + LANES]
        token = lax.broadcasted_iota(jnp.int32, (tokens, LANES), 0) + 1
        place = jnp.where(holders == token.astype(F32), 1.0, 0.0)
        places[:, i * base : (i + 1) * base] = place[:, :base].astype(BF16)
        if extra:
            mine = lax.broadcasted_iota(jnp.int32, (tokens, 16), 1) == i
            folded = folded + jnp.where(mine, place[:, base : base + 1], 0.0)
    if extra:
        places[:, n * base :] = folded.astype(BF16)
        put_extra(rows, row32, ext, n, base, 0)
    place = places[...]
    finish(rows_in)
    step = width // 4
    sent = []
    for h in range(4):
        for at in range(h * step, (h + 1) * step, TILE):
            cols = slice(at, min(at + TILE, (h + 1) * step))
            back = jnp.dot(place, rows[:, cols], preferred_element_type=F32)
            out[:, cols] = (start_ref[:, cols].astype(F32) + back).astype(out.dtype)
        cols = pl.ds(h * step, step)
        sent.append(begin(out.at[:, cols], out_hbm.at[:, cols], sem_o.at[h]))
    finish(sent)


def add_returned(start, msgs, base, extra, kind, name):
    tokens, width = start.shape
    n = len(msgs)
    slots = n * base + 16 * extra
    part, cols = msgs[0].shape
    sides = sides_of(base)
    anywhere, vmem = pl.BlockSpec(memory_space=pl.ANY), pl.BlockSpec(memory_space=pltpu.VMEM)
    return pl.pallas_call(
        functools.partial(add_kernel, n, base, extra),
        out_shape=jax.ShapeDtypeStruct((tokens, width), kind),
        in_specs=[vmem] + [anywhere] * n,
        out_specs=anywhere,
        scratch_shapes=[
            pltpu.VMEM((tokens, width), kind),
            pltpu.VMEM((slots, width), BF16),
            pltpu.VMEM((n, part, cols - sides * width), BF16),
            pltpu.VMEM((16, width), F32),
            pltpu.VMEM((tokens, slots), BF16),
            pltpu.SemaphoreType.DMA((n, sides)),
            pltpu.SemaphoreType.DMA((n,)),
            pltpu.SemaphoreType.DMA((4,)),
        ],
        compiler_params=pltpu.CompilerParams(vmem_limit_bytes=24 * MIB),
        cost_estimate=pl.CostEstimate(
            flops=2 * slots * tokens * width,
            bytes_accessed=2 * slots * width + 6 * tokens * width,
            transcendentals=0,
        ),
        name=name,
    )(start, *msgs)


def swap(value, axis, apart):
    return lax.ppermute(value, axis, [(i, i ^ apart) for i in range(lax.axis_size(axis))])


def swap_back(value, apart):
    sections, places = lax.axis_size("section"), lax.axis_size("expert")
    pairs = [
        (s * places + i, (s ^ 1) * places + (i ^ apart)) for s in range(sections) for i in range(places)
    ]
    return lax.ppermute(value, ("section", "expert"), pairs)


def after(*values):
    return lax.optimization_barrier(values)


def cut(weight):
    step = -(-weight.shape[0] // (LANES * CUTS)) * LANES
    return [weight[at : at + step] for at in range(0, weight.shape[0], step)]


def groups_of(experts):
    if experts == 4:
        return [[2], [1, 0], [3]], [[1, 2], [0, 3]]
    order = list(range(experts - 1, -1, -1))
    size = -(-experts // 4)
    groups = [order[i : i + size] for i in range(0, experts, size)]
    return groups, groups


def body(tokens, grad_out, expert_ids, gate_values, w_in, w_out_t):
    tok, grad = tokens[0], grad_out[0]
    ids_t, gates_t = expert_ids[0].T, gate_values[0].T
    experts = lax.axis_size("expert") // 2
    base, extra = slots_of(tok.shape[0], ids_t.shape[0], experts)
    sends, works = groups_of(experts)
    others = range(1, lax.axis_size("dp"))
    w_own, v_own = w_in[0, 0], w_out_t[0, 0]
    sent = [
        dispatch(group, base, extra, ids_t, gates_t, tok, grad, 24 if i else LIMIT, i < len(sends) - 1)
        for i, group in enumerate(sends)
    ]
    w_far = [swap(w_own, "dp", apart) for apart in others]
    w_other, v_other = swap(w_own, "expert", 1), swap(v_own, "expert", 1)
    other_grad = swap(grad, "section", 1)
    v_late, w_other, v_other = after(v_own, w_other, v_other)
    v_far = [swap(v_late, "dp", apart) for apart in others]
    sent[-1], other_grad, w_far = after(sent[-1], other_grad, w_far)
    got = {}
    for group, msgs in zip(sends, sent):
        for dist, msg in zip(group, msgs):
            got[dist] = tuple(swap(part, "expert", 2 * dist) for part in msg) if dist else msg
    first, last = [dist for group in sends[:-1] for dist in group], sends[-1]

    w_far, heads = after(w_far, [got[dist] for dist in first])
    got.update(zip(first, heads))
    w_columns = [[[w_own], [w_other]]]
    w_columns += [[[block], [swap(piece, "expert", 1) for piece in cut(block)]] for block in w_far]
    v_columns = [[[v_own], [v_other]]]
    carried = expert([got[dist] for dist in works[0]], base, extra, w_columns, v_columns, "early")
    v_far, tails, carried = after(v_far, [got[dist][0] for dist in last], carried)
    got.update((dist, (tail,) + got[dist][1:]) for dist, tail in zip(last, tails))
    v_columns += [[[block], [swap(block, "expert", 1)]] for block in v_far]

    total = other_grad
    for i, group in enumerate(works):
        msgs = [got[dist] for dist in group]
        if i == 0:
            backs = expert_late(msgs, base, extra, w_columns[1:], v_columns[1:], carried)
            backs, heads = after(backs, {dist: parts[:1] for dist, parts in got.items()})
            got = {dist: heads[dist] + parts[1:] for dist, parts in got.items()}
        else:
            backs = expert(msgs, base, extra, w_columns, v_columns)
        returned = [swap_back(back, 2 * dist) for dist, back in zip(group, backs)]
        ends = i == len(works) - 1
        total = add_returned(total, returned, base, extra, BF16 if ends else F32, "finish" if ends else "settle")
    return total[None]


def solution(mesh):
    rows = P("section", ("expert", "dp"), None)
    weights = P("section", "expert", None, "dp")
    return jax.shard_map(
        body,
        mesh=mesh,
        in_specs=(rows, rows, rows, rows, weights, weights),
        out_specs=rows,
        check_vma=False,
    )
```

```python
import functools

import jax
import jax.numpy as jnp
from jax import lax
from jax.experimental import pallas as pl
from jax.experimental.pallas import tpu as pltpu
from jax.sharding import PartitionSpec as P

LANES = 128
TILE = 256
F32 = jnp.float32
BF16 = jnp.bfloat16
MIB = 1 << 20
CHUNK = 512
PARTS = 1
LIMIT = 57
TAIL = 8
CUTS = 3


def slots_of(tok_dev, top, experts):
    capacity = min(tok_dev, max(2, tok_dev * top // experts + 1))
    if capacity % 16 == 1 and capacity > 1:
        return capacity - 1, 1
    return -(-capacity // 16) * 16, 0


def fold_columns(pieces, base):
    return -(-(pieces + 1) // base) * LANES


def sides_of(base):
    return 2 if base % 32 == 0 else 1


def back_shape(base, width, extra):
    sides = sides_of(base)
    return base // sides, sides * width + fold_columns(width // LANES * extra, base // sides)


def place_of(piece, base):
    return piece % base, piece // base * LANES


def fold(ext_ref, row, pieces, first, base):
    for k in range(pieces):
        at, column = place_of(first + k, base)
        ext_ref[at : at + 1, column : column + LANES] = row[:, k * LANES : (k + 1) * LANES]


def unfold(row_ref, at_row, ext, pieces, first, base):
    for k in range(pieces):
        at, column = place_of(first + k, base)
        row_ref[at_row : at_row + 1, k * LANES : (k + 1) * LANES] = ext[at : at + 1, column : column + LANES]


def slot_row(ids, expert):
    tokens = ids.shape[1]
    hit = jnp.where(ids == expert, 1.0, 0.0).astype(F32)
    mask = jnp.sum(hit, axis=0, keepdims=True)
    earlier = lax.broadcasted_iota(jnp.int32, (tokens, tokens), 0) < lax.broadcasted_iota(
        jnp.int32, (tokens, tokens), 1
    )
    before = jnp.dot(
        jnp.broadcast_to(mask, (16, tokens)).astype(BF16),
        jnp.where(earlier, 1.0, 0.0).astype(BF16),
        preferred_element_type=F32,
    )[0:1]
    return jnp.where(mask > 0.5, before, -1.0)


def begin(src, dst, sem):
    copy = pltpu.make_async_copy(src, dst, sem)
    copy.start()
    return copy


def finish(copies):
    for copy in copies:
        copy.wait()


def dispatch_kernel(dists, base, extra, split, ids_hbm, gates_hbm, tok_hbm, grad_hbm, *refs):
    n = len(dists)
    outs, refs = refs[: n * len(split)], refs[n * len(split) :]
    ids_ref, gates_ref, tok_ref, grad_ref, msg_ref, ext_ref, sem_i, sem_t, sem_g, sem_o = refs
    here = lax.axis_index("expert") // 2
    tokens, width = tok_ref.shape
    pieces = width // LANES
    rows = base + 16 * extra
    step = tokens // PARTS
    parts = [pl.ds(i * step, step) for i in range(PARTS)]
    small = [begin(ids_hbm, ids_ref, sem_i.at[0]), begin(gates_hbm, gates_ref, sem_i.at[1])]
    tok_in = [begin(tok_hbm.at[p, :], tok_ref.at[p, :], sem_t.at[i]) for i, p in enumerate(parts)]
    grad_in = [begin(grad_hbm.at[p, :], grad_ref.at[p, :], sem_g.at[i]) for i, p in enumerate(parts)]
    finish(small)
    ids, gates = ids_ref[...], gates_ref[...]
    onehots, scales = [], []
    for dist in dists:
        slot = slot_row(ids, here ^ dist)
        gate = jnp.sum(jnp.where(ids == (here ^ dist), gates, 0.0), axis=0, keepdims=True)
        picks = lax.broadcasted_iota(jnp.int32, (rows, tokens), 0).astype(F32) == slot
        onehots.append(jnp.where(picks, 1.0, 0.0).astype(BF16))
        scales.append(jnp.sum(jnp.where(picks, gate, 0.0), axis=1, keepdims=True))
    ext_ref[...] = jnp.zeros_like(ext_ref)
    count = lax.broadcasted_iota(jnp.int32, (16, tokens), 1) + 1
    for d in range(n):
        holders = lax.dot_general(
            count.astype(F32).astype(BF16), onehots[d], (((1,), (1,)), ((), ())), preferred_element_type=F32
        )
        at, column = place_of(2 * pieces * extra, base)
        ext_ref[d, at : at + 1, column : column + rows] = holders[0:1]
    sent = []
    for part, copies in enumerate((tok_in, grad_in)):
        finish(copies)
        for d in range(n):
            for at in range(0, width, CHUNK):
                value = jnp.dot(
                    onehots[d],
                    (grad_ref if part else tok_ref)[:, at : at + CHUNK],
                    preferred_element_type=F32,
                )
                if part:
                    value = value * scales[d]
                msg_ref[d, :, part * width + at : part * width + at + CHUNK] = value[:base].astype(BF16)
                if extra:
                    first = part * pieces + at // LANES
                    fold(ext_ref.at[d], value[base : base + 1], CHUNK // LANES, first, base)
            stop = (part + 1) * width
            if part:
                msg_ref[d, :, stop:] = ext_ref[d].astype(BF16)
                stop = msg_ref.shape[2]
            for i, (start, end) in enumerate(split):
                low, high = max(start, part * width), min(end, stop)
                if low < high:
                    src = msg_ref.at[d, :, pl.ds(low, high - low)]
                    dst = outs[d * len(split) + i].at[:, pl.ds(low - start, high - low)]
                    sent.append(begin(src, dst, sem_o.at[d, part, i]))
    finish(sent)


def dispatch(dists, base, extra, ids_t, gates_t, tok, grad, limit, whole=True):
    tokens, width = tok.shape
    n, ext = len(dists), fold_columns(2 * width // LANES * extra, base)
    cols = 2 * width + ext
    cutoff = 2 * width - TAIL * LANES
    split = [(0, cols)] if whole else [(0, cutoff), (cutoff, cols)]
    anywhere = pl.BlockSpec(memory_space=pl.ANY)
    outs = pl.pallas_call(
        functools.partial(dispatch_kernel, dists, base, extra, split),
        out_shape=[jax.ShapeDtypeStruct((base, end - start), BF16) for _ in dists for start, end in split],
        in_specs=[anywhere] * 4,
        out_specs=[anywhere] * (n * len(split)),
        scratch_shapes=[
            pltpu.VMEM(ids_t.shape, jnp.int32),
            pltpu.VMEM(gates_t.shape, F32),
            pltpu.VMEM((tokens, width), BF16),
            pltpu.VMEM((tokens, width), BF16),
            pltpu.VMEM((n, base, cols), BF16),
            pltpu.VMEM((n, base, ext), F32),
            pltpu.SemaphoreType.DMA((2,)),
            pltpu.SemaphoreType.DMA((PARTS,)),
            pltpu.SemaphoreType.DMA((PARTS,)),
            pltpu.SemaphoreType.DMA((n, 2, len(split))),
        ],
        compiler_params=pltpu.CompilerParams(vmem_limit_bytes=limit * MIB),
        cost_estimate=pl.CostEstimate(
            flops=4 * n * (base + 16) * tokens * width,
            bytes_accessed=4 * tokens * width + 2 * n * base * cols,
            transcendentals=0,
        ),
        name="dispatch",
    )(ids_t, gates_t, tok, grad)
    return [tuple(outs[i : i + len(split)]) for i in range(0, len(outs), len(split))]


def silu_slope(pre):
    sig = jax.nn.sigmoid(pre)
    return sig * (1.0 + pre * (1.0 - sig))


def begin_weights(pieces, layout, whole, sems):
    half = whole.shape[0] // 2
    core = lax.axis_index("expert") % 2
    copies = {}
    for i, (piece, (block, other, row, columns)) in enumerate(zip(pieces, layout)):
        at = pl.multiple_of((1 - core if other else core) * half + row, 16)
        rows = pl.ds(at, piece.shape[0])
        dst = whole.at[rows, pl.ds(block * columns, columns)]
        copies.setdefault(block, []).append(begin(piece, dst, sems.at[i]))
    return copies


def begin_columns(parts, start, dst, sems):
    copies, at = [], 0
    for i, part in enumerate(parts):
        low, high = max(start, at), min(start + dst.shape[1], at + part.shape[1])
        if low < high:
            src = part.at[:, pl.ds(low - at, high - low)]
            copies.append(begin(src, dst.at[:, pl.ds(low - start, high - low)], sems.at[i]))
        at += part.shape[1]
    return copies


def begin_rows(msgs, rows, ext, start, sems, ext_sems):
    base = msgs[0][0].shape[0]
    width = rows.shape[1]
    copies = []
    for i, parts in enumerate(msgs):
        copies += begin_columns(parts, start, rows.at[pl.ds(i * base, base), :], sems.at[i])
        if ext is not None:
            copies += begin_columns(parts, 2 * width, ext.at[i], ext_sems.at[i])
    return copies


def put_extra(rows, row32, ext, n, base, first):
    row32[...] = jnp.zeros_like(row32)
    for i in range(n):
        unfold(row32, i, ext[i].astype(F32), rows.shape[1] // LANES, first, ext.shape[1])
    rows[n * base :, :] = row32[...].astype(BF16)


def put_back(outs, ext32, back, at, size, n, base, extra, width):
    part = outs[0].shape[0]
    for i in range(n):
        for side in range(base // part):
            first = i * base + side * part
            cols = slice(side * width + at, side * width + at + size)
            outs[i][:, cols] = back[first : first + part].astype(BF16)
        if extra:
            row = back[n * base + i : n * base + i + 1]
            fold(ext32.at[i], row, size // LANES, at // LANES, part)


def expert_kernel(n, base, extra, stage, w_layout, v_layout, lengths, *refs):
    msgs = []
    for length in lengths:
        msgs.append(refs[:length])
        refs = refs[length:]
    w_pieces, refs = refs[: len(w_layout)], refs[len(w_layout) :]
    v_pieces, refs = refs[: len(v_layout)], refs[len(v_layout) :]
    if stage == "early":
        slope_late, partial_out, refs = refs[0], refs[1], refs[2:]
    else:
        outs, refs = refs[:n], refs[n:]
    g, ext32, slope, w, v, x, act, ext, row32, sem_x, sem_g, sem_e, sem_w, sem_v = refs
    width = w.shape[0]
    half_ff = w_layout[0][3]
    pieces = width // LANES
    full = n * base
    x_in = begin_rows(msgs, x, ext, 0, sem_x, sem_e)
    w_in = begin_weights(w_pieces, w_layout, w, sem_w)
    g_in = begin_rows(msgs, g, None, width, sem_g, sem_e)
    v_in = begin_weights(v_pieces, v_layout, v, sem_v)
    finish(x_in)
    if extra:
        put_extra(x, row32, ext, n, base, 0)
    for block in sorted(w_in):
        finish(w_in[block])
        for at in range(block * half_ff, (block + 1) * half_ff, TILE):
            value = silu_slope(jnp.dot(x[...], w[:, at : at + TILE], preferred_element_type=F32))
            if stage == "early" and block > 0:
                slope_late[:, at - half_ff : at - half_ff + TILE] = value
            else:
                slope[:, at : at + TILE] = value
    finish(g_in)
    if extra:
        put_extra(g, row32, ext, n, base, pieces)
    for block in sorted(v_in):
        finish(v_in[block])
        for at in range(block * half_ff, (block + 1) * half_ff, TILE):
            hid = jnp.dot(g[...], v[:, at : at + TILE], preferred_element_type=F32)
            act[:, at : at + TILE] = (hid * slope[:, at : at + TILE]).astype(BF16)
    ext32[...] = jnp.zeros_like(ext32)
    at, column = place_of(2 * pieces * extra, base)
    to, to_column = place_of(pieces * extra, ext32.shape[1])
    for i in range(n):
        holders = ext[i].astype(F32)[at : at + 1, column : column + LANES]
        ext32[i, to : to + 1, to_column : to_column + LANES] = holders
    hidden = act.shape[1]
    for at in range(0, width, TILE):
        cols = slice(at, at + TILE)
        back = lax.dot_general(
            act[...], w[cols, :hidden], (((1,), (1,)), ((), ())), preferred_element_type=F32
        )
        if stage == "early":
            partial_out[:, cols] = back
            continue
        put_back(outs, ext32, back, at, TILE, n, base, extra, width)
    if stage != "early":
        for i in range(n):
            outs[i][:, sides_of(base) * width :] = ext32[i].astype(BF16)


def middle_kernel(*refs):
    g, v_blocks, out = refs[0], refs[1:-1], refs[-1]
    half, block_ff = v_blocks[0].shape

    def work(here):
        for block, ref in enumerate(v_blocks):
            for at in range(0, block_ff, TILE):
                out[:, block * block_ff + at : block * block_ff + at + TILE] = jnp.dot(
                    g[:, here * half : (here + 1) * half],
                    ref[:, at : at + TILE],
                    preferred_element_type=F32,
                )

    core = lax.axis_index("expert") % 2
    for here in range(2):
        pl.when(core == here)(functools.partial(work, here))


def expert_middle(g, v_blocks):
    rows, (half, block_ff) = g.shape[0], v_blocks[0].shape
    vmem = pl.BlockSpec(memory_space=pltpu.VMEM)
    return pl.pallas_call(
        middle_kernel,
        out_shape=jax.ShapeDtypeStruct((rows, len(v_blocks) * block_ff), F32),
        in_specs=[vmem] * (1 + len(v_blocks)),
        out_specs=vmem,
        compiler_params=pltpu.CompilerParams(vmem_limit_bytes=24 * MIB),
        cost_estimate=pl.CostEstimate(
            flops=2 * rows * half * block_ff * len(v_blocks),
            bytes_accessed=2 * half * block_ff * len(v_blocks),
            transcendentals=0,
        ),
        name="expert_middle",
    )(g, *v_blocks)


def late_kernel(n, base, extra, blocks, w_layout, v_layout, *refs):
    w_pieces, refs = refs[: len(w_layout)], refs[len(w_layout) :]
    v_pieces, refs = refs[: len(v_layout)], refs[len(v_layout) :]
    slope, partial, g, folded, half_hid, refs = refs[0], refs[1], refs[2], refs[3], refs[4], refs[5:]
    outs, (act, ext32) = refs[:n], refs[n:]
    width = g.shape[1]
    half, block_ff = width // 2, v_layout[0][3]
    core = lax.axis_index("expert") % 2
    ext32[...] = folded[...]

    def work(here):
        for block in range(blocks):
            for at in range(0, block_ff, TILE):
                cols = slice(block * block_ff + at, block * block_ff + at + TILE)
                hid = half_hid[:, cols]
                for ref, (of, other, row, _) in zip(v_pieces, v_layout):
                    if of == block:
                        first = (1 - here if other else here) * half + row
                        hid = hid + jnp.dot(
                            g[:, first : first + ref.shape[0]],
                            ref[:, at : at + TILE],
                            preferred_element_type=F32,
                        )
                act[:, cols] = (hid * slope[:, cols]).astype(BF16)
        places = {}
        for ref, (of, other, row, _) in zip(w_pieces, w_layout):
            for at in range(0, ref.shape[0], TILE):
                size = min(TILE, ref.shape[0] - at)
                first = (1 - here if other else here) * half + row + at
                places.setdefault((first, size), []).append((of, ref, at))
        for (first, size), terms in sorted(places.items()):
            cols = slice(first, first + size)
            back = partial[:, cols]
            for of, ref, at in terms:
                back = back + lax.dot_general(
                    act[:, of * block_ff : (of + 1) * block_ff],
                    ref[at : at + size, :],
                    (((1,), (1,)), ((), ())),
                    preferred_element_type=F32,
                )
            put_back(outs, ext32, back, first, size, n, base, extra, width)

    for here in range(2):
        pl.when(core == here)(functools.partial(work, here))
    for i in range(n):
        outs[i][:, sides_of(base) * width :] = ext32[i].astype(BF16)


def flat(columns):
    arrays, layout = [], []
    for block, cores in enumerate(columns):
        for other, pieces in enumerate(cores):
            row = 0
            for piece in pieces:
                arrays.append(piece)
                layout.append((block, other, row, piece.shape[1]))
                row += piece.shape[0]
    return arrays, layout, row


def expert_late(base, extra, w_columns, v_columns, carried):
    w_pieces, w_layout, half = flat(w_columns)
    carried = list(carried) + [expert_middle(carried[2], [own[0] for own, _ in v_columns])]
    v_pieces, v_layout, _ = flat([[[], other] for _, other in v_columns])
    width, ff = 2 * half, len(w_columns) * w_layout[0][3]
    rows, folded = carried[0].shape[0], carried[3].shape
    vmem = pl.BlockSpec(memory_space=pltpu.VMEM)
    back = jax.ShapeDtypeStruct(back_shape(base, width, extra), BF16)
    return pl.pallas_call(
        functools.partial(late_kernel, folded[0], base, extra, len(w_columns), w_layout, v_layout),
        out_shape=[back] * folded[0],
        in_specs=[vmem] * (len(w_pieces) + len(v_pieces) + len(carried)),
        out_specs=[vmem] * folded[0],
        scratch_shapes=[pltpu.VMEM((rows, ff), BF16), pltpu.VMEM(folded, F32)],
        compiler_params=pltpu.CompilerParams(vmem_limit_bytes=24 * MIB),
        cost_estimate=pl.CostEstimate(
            flops=4 * rows * width * ff,
            bytes_accessed=4 * width * ff + 8 * rows * width,
            transcendentals=0,
        ),
        name="expert_late",
    )(*w_pieces, *v_pieces, *carried)


def expert(msgs, base, extra, w_columns, v_columns, stage="whole"):
    n = len(msgs)
    lengths = [len(parts) for parts in msgs]
    most, parts = max(lengths), [part for message in msgs for part in message]
    w_pieces, w_layout, half = flat(w_columns)
    v_pieces, v_layout, _ = flat(v_columns)
    width, block_ff = 2 * half, w_layout[0][3]
    w_ff, v_ff = len(w_columns) * block_ff, len(v_columns) * block_ff
    rows = n * base + -(-n * extra // 16) * 16
    ext = fold_columns(2 * width // LANES * extra, base)
    back_rows, back_cols = back_shape(base, width, extra)
    anywhere, vmem = pl.BlockSpec(memory_space=pl.ANY), pl.BlockSpec(memory_space=pltpu.VMEM)
    spare = max(16, rows - n * base)
    kept = [((rows, width), BF16), ((n, back_rows, back_cols - sides_of(base) * width), F32)]
    if stage == "early":
        results = [((rows, w_ff - block_ff), F32), ((rows, width), F32)] + kept
    else:
        results = [((back_rows, back_cols), BF16)] * n
    return pl.pallas_call(
        functools.partial(expert_kernel, n, base, extra, stage, w_layout, v_layout, lengths),
        out_shape=[jax.ShapeDtypeStruct(*result) for result in results],
        in_specs=[anywhere] * (len(parts) + len(w_pieces) + len(v_pieces)),
        out_specs=[vmem] * len(results),
        scratch_shapes=[pltpu.VMEM(*shape) for shape in (kept if stage != "early" else [])]
        + [
            pltpu.VMEM((rows, v_ff), F32),
            pltpu.VMEM((width, w_ff), BF16),
            pltpu.VMEM((width, v_ff), BF16),
            pltpu.VMEM((rows, width), BF16),
            pltpu.VMEM((rows, v_ff), BF16),
            pltpu.VMEM((n, base, ext), BF16),
            pltpu.VMEM((spare, width), F32),
            pltpu.SemaphoreType.DMA((n, most)),
            pltpu.SemaphoreType.DMA((n, most)),
            pltpu.SemaphoreType.DMA((n, most)),
            pltpu.SemaphoreType.DMA((len(w_pieces),)),
            pltpu.SemaphoreType.DMA((len(v_pieces),)),
        ],
        compiler_params=pltpu.CompilerParams(vmem_limit_bytes=24 * MIB),
        cost_estimate=pl.CostEstimate(
            flops=0 if stage == "early" else 2 * rows * width * (w_ff + 2 * v_ff),
            bytes_accessed=0 if stage == "early" else 2 * width * (w_ff + v_ff) + 6 * rows * width,
            transcendentals=0 if stage == "early" else rows * w_ff,
        ),
        name="expert_" + stage,
    )(*parts, *w_pieces, *v_pieces)


def add_kernel(n, base, extra, start_ref, *refs):
    msgs, (out_hbm, out, rows, ext, row32, places, sem_b, sem_e, sem_o) = refs[:n], refs[n:]
    tokens, width = start_ref.shape
    pieces = width // LANES
    part, sides = msgs[0].shape[0], sides_of(base)
    ext_in = [
        begin(msg.at[:, pl.ds(sides * width, ext.shape[2])], ext.at[i], sem_e.at[i])
        for i, msg in enumerate(msgs)
    ]
    rows_in = []
    for i, msg in enumerate(msgs):
        for side in range(sides):
            src = msg.at[:, pl.ds(side * width, width)]
            dst = rows.at[pl.ds(i * base + side * part, part), :]
            rows_in.append(begin(src, dst, sem_b.at[i, side]))
    finish(ext_in)
    folded = jnp.zeros((tokens, 16), F32)
    at, column = place_of(pieces * extra, part)
    for i in range(n):
        holders = ext[i].astype(F32)[at : at + 1, column : column + LANES]
        token = lax.broadcasted_iota(jnp.int32, (tokens, LANES), 0) + 1
        place = jnp.where(holders == token.astype(F32), 1.0, 0.0)
        places[:, i * base : (i + 1) * base] = place[:, :base].astype(BF16)
        if extra:
            mine = lax.broadcasted_iota(jnp.int32, (tokens, 16), 1) == i
            folded = folded + jnp.where(mine, place[:, base : base + 1], 0.0)
    if extra:
        places[:, n * base :] = folded.astype(BF16)
        put_extra(rows, row32, ext, n, base, 0)
    place = places[...]
    finish(rows_in)
    step = width // 4
    sent = []
    for h in range(4):
        for at in range(h * step, (h + 1) * step, TILE):
            cols = slice(at, min(at + TILE, (h + 1) * step))
            back = jnp.dot(place, rows[:, cols], preferred_element_type=F32)
            out[:, cols] = (start_ref[:, cols].astype(F32) + back).astype(out.dtype)
        cols = pl.ds(h * step, step)
        sent.append(begin(out.at[:, cols], out_hbm.at[:, cols], sem_o.at[h]))
    finish(sent)


def add_returned(start, msgs, base, extra, kind, name):
    tokens, width = start.shape
    n = len(msgs)
    slots = n * base + 16 * extra
    part, cols = msgs[0].shape
    sides = sides_of(base)
    anywhere, vmem = pl.BlockSpec(memory_space=pl.ANY), pl.BlockSpec(memory_space=pltpu.VMEM)
    return pl.pallas_call(
        functools.partial(add_kernel, n, base, extra),
        out_shape=jax.ShapeDtypeStruct((tokens, width), kind),
        in_specs=[vmem] + [anywhere] * n,
        out_specs=anywhere,
        scratch_shapes=[
            pltpu.VMEM((tokens, width), kind),
            pltpu.VMEM((slots, width), BF16),
            pltpu.VMEM((n, part, cols - sides * width), BF16),
            pltpu.VMEM((16, width), F32),
            pltpu.VMEM((tokens, slots), BF16),
            pltpu.SemaphoreType.DMA((n, sides)),
            pltpu.SemaphoreType.DMA((n,)),
            pltpu.SemaphoreType.DMA((4,)),
        ],
        compiler_params=pltpu.CompilerParams(vmem_limit_bytes=24 * MIB),
        cost_estimate=pl.CostEstimate(
            flops=2 * slots * tokens * width,
            bytes_accessed=2 * slots * width + 6 * tokens * width,
            transcendentals=0,
        ),
        name=name,
    )(start, *msgs)


def swap(value, axis, apart):
    return lax.ppermute(value, axis, [(i, i ^ apart) for i in range(lax.axis_size(axis))])


def swap_back(value, apart):
    sections, places = lax.axis_size("section"), lax.axis_size("expert")
    pairs = [
        (s * places + i, (s ^ 1) * places + (i ^ apart)) for s in range(sections) for i in range(places)
    ]
    return lax.ppermute(value, ("section", "expert"), pairs)


def after(*values):
    return lax.optimization_barrier(values)


def cut(weight):
    step = -(-weight.shape[0] // (LANES * CUTS)) * LANES
    return [weight[at : at + step] for at in range(0, weight.shape[0], step)]


def groups_of(experts):
    if experts == 4:
        return [[2], [1, 0], [3]], [[1, 2], [0, 3]]
    order = list(range(experts - 1, -1, -1))
    size = -(-experts // 4)
    groups = [order[i : i + size] for i in range(0, experts, size)]
    return groups, groups


def body(tokens, grad_out, expert_ids, gate_values, w_in, w_out_t):
    tok, grad = tokens[0], grad_out[0]
    ids_t, gates_t = expert_ids[0].T, gate_values[0].T
    experts = lax.axis_size("expert") // 2
    base, extra = slots_of(tok.shape[0], ids_t.shape[0], experts)
    sends, works = groups_of(experts)
    others = range(1, lax.axis_size("dp"))
    w_own, v_own = w_in[0, 0], w_out_t[0, 0]
    sent = [
        dispatch(group, base, extra, ids_t, gates_t, tok, grad, 24 if i else LIMIT, i < len(sends) - 1)
        for i, group in enumerate(sends)
    ]
    w_far = [swap(w_own, "dp", apart) for apart in others]
    w_other, v_other = swap(w_own, "expert", 1), swap(v_own, "expert", 1)
    other_grad = swap(grad, "section", 1)
    v_late, w_other, v_other = after(v_own, w_other, v_other)
    v_far = [swap(v_late, "dp", apart) for apart in others]
    sent[-1], other_grad, w_far = after(sent[-1], other_grad, w_far)
    got = {}
    for group, msgs in zip(sends, sent):
        for dist, msg in zip(group, msgs):
            got[dist] = tuple(swap(part, "expert", 2 * dist) for part in msg) if dist else msg
    first, last = [dist for group in sends[:-1] for dist in group], sends[-1]

    w_far, heads = after(w_far, [got[dist] for dist in first])
    got.update(zip(first, heads))
    w_columns = [[[w_own], [w_other]]]
    w_columns += [[[block], [swap(piece, "expert", 1) for piece in cut(block)]] for block in w_far]
    v_columns = [[[v_own], [v_other]]]
    carried = expert([got[dist] for dist in works[0]], base, extra, w_columns, v_columns, "early")
    v_far, tails, carried = after(v_far, [got[dist][0] for dist in last], carried)
    got.update((dist, (tail,) + got[dist][1:]) for dist, tail in zip(last, tails))
    v_columns += [[[block], [swap(block, "expert", 1)]] for block in v_far]

    total = other_grad
    for i, group in enumerate(works):
        msgs = [got[dist] for dist in group]
        if i == 0:
            backs = expert_late(base, extra, w_columns[1:], v_columns[1:], carried)
            backs, heads = after(backs, {dist: parts[:1] for dist, parts in got.items()})
            got = {dist: heads[dist] + parts[1:] for dist, parts in got.items()}
        else:
            backs = expert(msgs, base, extra, w_columns, v_columns)
        returned = [swap_back(back, 2 * dist) for dist, back in zip(group, backs)]
        ends = i == len(works) - 1
        total = add_returned(total, returned, base, extra, BF16 if ends else F32, "finish" if ends else "settle")
    return total[None]


def solution(mesh):
    rows = P("section", ("expert", "dp"), None)
    weights = P("section", "expert", None, "dp")
    return jax.shard_map(
        body,
        mesh=mesh,
        in_specs=(rows, rows, rows, rows, weights, weights),
        out_specs=rows,
        check_vma=False,
    )
```

```python
import functools

import jax
import jax.numpy as jnp
from jax import lax
from jax.experimental import pallas as pl
from jax.experimental.pallas import tpu as pltpu
from jax.sharding import PartitionSpec as P

LANES = 128
TILE = 256
F32 = jnp.float32
BF16 = jnp.bfloat16
MIB = 1 << 20
CHUNK = 512
PARTS = 1
PIECES = 2
LIMIT = 57
TAIL = 8
CUTS = 3


def slots_of(tok_dev, top, experts):
    capacity = min(tok_dev, max(2, tok_dev * top // experts + 1))
    if capacity % 16 == 1 and capacity > 1:
        return capacity - 1, 1
    return -(-capacity // 16) * 16, 0


def fold_columns(pieces, base):
    return -(-(pieces + 1) // base) * LANES


def sides_of(base):
    return 2 if base % 32 == 0 else 1


def back_shape(base, width, extra):
    sides = sides_of(base)
    return base // sides, sides * width + fold_columns(width // LANES * extra, base // sides)


def place_of(piece, base):
    return piece % base, piece // base * LANES


def fold(ext_ref, row, pieces, first, base):
    for k in range(pieces):
        at, column = place_of(first + k, base)
        ext_ref[at : at + 1, column : column + LANES] = row[:, k * LANES : (k + 1) * LANES]


def unfold(row_ref, at_row, ext, pieces, first, base):
    for k in range(pieces):
        at, column = place_of(first + k, base)
        row_ref[at_row : at_row + 1, k * LANES : (k + 1) * LANES] = ext[at : at + 1, column : column + LANES]


def slot_row(ids, expert):
    tokens = ids.shape[1]
    hit = jnp.where(ids == expert, 1.0, 0.0).astype(F32)
    mask = jnp.sum(hit, axis=0, keepdims=True)
    earlier = lax.broadcasted_iota(jnp.int32, (tokens, tokens), 0) < lax.broadcasted_iota(
        jnp.int32, (tokens, tokens), 1
    )
    before = jnp.dot(
        jnp.broadcast_to(mask, (16, tokens)).astype(BF16),
        jnp.where(earlier, 1.0, 0.0).astype(BF16),
        preferred_element_type=F32,
    )[0:1]
    return jnp.where(mask > 0.5, before, -1.0)


def begin(src, dst, sem):
    copy = pltpu.make_async_copy(src, dst, sem)
    copy.start()
    return copy


def finish(copies):
    for copy in copies:
        copy.wait()


def dispatch_kernel(dists, base, extra, split, ids_hbm, gates_hbm, tok_hbm, grad_hbm, *refs):
    n = len(dists)
    outs, refs = refs[: n * len(split)], refs[n * len(split) :]
    ids_ref, gates_ref, tok_ref, grad_ref, msg_ref, ext_ref, sem_i, sem_t, sem_g, sem_o = refs
    here = lax.axis_index("expert") // 2
    tokens, width = tok_ref.shape
    pieces = width // LANES
    rows = base + 16 * extra
    step = tokens // PARTS
    parts = [pl.ds(i * step, step) for i in range(PARTS)]
    small = [begin(ids_hbm, ids_ref, sem_i.at[0]), begin(gates_hbm, gates_ref, sem_i.at[1])]
    tok_in = [begin(tok_hbm.at[p, :], tok_ref.at[p, :], sem_t.at[i]) for i, p in enumerate(parts)]
    grad_in = [begin(grad_hbm.at[p, :], grad_ref.at[p, :], sem_g.at[i]) for i, p in enumerate(parts)]
    finish(small)
    ids, gates = ids_ref[...], gates_ref[...]
    onehots, scales = [], []
    for dist in dists:
        slot = slot_row(ids, here ^ dist)
        gate = jnp.sum(jnp.where(ids == (here ^ dist), gates, 0.0), axis=0, keepdims=True)
        picks = lax.broadcasted_iota(jnp.int32, (rows, tokens), 0).astype(F32) == slot
        onehots.append(jnp.where(picks, 1.0, 0.0).astype(BF16))
        scales.append(jnp.sum(jnp.where(picks, gate, 0.0), axis=1, keepdims=True))
    ext_ref[...] = jnp.zeros_like(ext_ref)
    count = lax.broadcasted_iota(jnp.int32, (16, tokens), 1) + 1
    for d in range(n):
        holders = lax.dot_general(
            count.astype(F32).astype(BF16), onehots[d], (((1,), (1,)), ((), ())), preferred_element_type=F32
        )
        at, column = place_of(2 * pieces * extra, base)
        ext_ref[d, at : at + 1, column : column + rows] = holders[0:1]
    sent = []
    for part, copies in enumerate((tok_in, grad_in)):
        finish(copies)
        for d in range(n):
            for at in range(0, width, CHUNK):
                value = jnp.dot(
                    onehots[d],
                    (grad_ref if part else tok_ref)[:, at : at + CHUNK],
                    preferred_element_type=F32,
                )
                if part:
                    value = value * scales[d]
                msg_ref[d, :, part * width + at : part * width + at + CHUNK] = value[:base].astype(BF16)
                if extra:
                    first = part * pieces + at // LANES
                    fold(ext_ref.at[d], value[base : base + 1], CHUNK // LANES, first, base)
            stop = (part + 1) * width
            if part:
                msg_ref[d, :, stop:] = ext_ref[d].astype(BF16)
                stop = msg_ref.shape[2]
            for i, (start, end) in enumerate(split):
                low, high = max(start, part * width), min(end, stop)
                if low < high:
                    src = msg_ref.at[d, :, pl.ds(low, high - low)]
                    dst = outs[d * len(split) + i].at[:, pl.ds(low - start, high - low)]
                    sent.append(begin(src, dst, sem_o.at[d, part, i]))
    finish(sent)


def dispatch(dists, base, extra, ids_t, gates_t, tok, grad, limit, whole=True):
    tokens, width = tok.shape
    n, ext = len(dists), fold_columns(2 * width // LANES * extra, base)
    cols = 2 * width + ext
    cutoff = 2 * width - TAIL * LANES
    split = [(0, cols)] if whole else [(0, cutoff), (cutoff, cols)]
    anywhere = pl.BlockSpec(memory_space=pl.ANY)
    outs = pl.pallas_call(
        functools.partial(dispatch_kernel, dists, base, extra, split),
        out_shape=[jax.ShapeDtypeStruct((base, end - start), BF16) for _ in dists for start, end in split],
        in_specs=[anywhere] * 4,
        out_specs=[anywhere] * (n * len(split)),
        scratch_shapes=[
            pltpu.VMEM(ids_t.shape, jnp.int32),
            pltpu.VMEM(gates_t.shape, F32),
            pltpu.VMEM((tokens, width), BF16),
            pltpu.VMEM((tokens, width), BF16),
            pltpu.VMEM((n, base, cols), BF16),
            pltpu.VMEM((n, base, ext), F32),
            pltpu.SemaphoreType.DMA((2,)),
            pltpu.SemaphoreType.DMA((PARTS,)),
            pltpu.SemaphoreType.DMA((PARTS,)),
            pltpu.SemaphoreType.DMA((n, 2, len(split))),
        ],
        compiler_params=pltpu.CompilerParams(vmem_limit_bytes=limit * MIB),
        cost_estimate=pl.CostEstimate(
            flops=4 * n * (base + 16) * tokens * width,
            bytes_accessed=4 * tokens * width + 2 * n * base * cols,
            transcendentals=0,
        ),
        name="dispatch",
    )(ids_t, gates_t, tok, grad)
    return [tuple(outs[i : i + len(split)]) for i in range(0, len(outs), len(split))]


def silu_slope(pre):
    sig = jax.nn.sigmoid(pre)
    return sig * (1.0 + pre * (1.0 - sig))


def begin_weights(pieces, layout, whole, sems):
    half = whole.shape[0] // 2
    core = lax.axis_index("expert") % 2
    copies = {}
    for i, (piece, (block, other, row, columns)) in enumerate(zip(pieces, layout)):
        at = pl.multiple_of((1 - core if other else core) * half + row, 16)
        rows = pl.ds(at, piece.shape[0])
        dst = whole.at[rows, pl.ds(block * columns, columns)]
        copies.setdefault(block, []).append(begin(piece, dst, sems.at[i]))
    return copies


def begin_columns(parts, start, dst, sems):
    copies, at = [], 0
    for i, part in enumerate(parts):
        low, high = max(start, at), min(start + dst.shape[1], at + part.shape[1])
        if low < high:
            src = part.at[:, pl.ds(low - at, high - low)]
            copies.append(begin(src, dst.at[:, pl.ds(low - start, high - low)], sems.at[i]))
        at += part.shape[1]
    return copies


def begin_rows(msgs, rows, ext, start, sems, ext_sems):
    base = msgs[0][0].shape[0]
    width = rows.shape[1]
    copies = []
    for i, parts in enumerate(msgs):
        copies += begin_columns(parts, start, rows.at[pl.ds(i * base, base), :], sems.at[i])
        if ext is not None:
            copies += begin_columns(parts, 2 * width, ext.at[i], ext_sems.at[i])
    return copies


def put_extra(rows, row32, ext, n, base, first):
    row32[...] = jnp.zeros_like(row32)
    for i in range(n):
        unfold(row32, i, ext[i].astype(F32), rows.shape[1] // LANES, first, ext[i].shape[0])
    rows[n * base :, :] = row32[...].astype(BF16)


def put_back(outs, ext32, back, at, size, n, base, extra, width):
    part = outs[0].shape[0]
    for i in range(n):
        for side in range(base // part):
            first = i * base + side * part
            cols = slice(side * width + at, side * width + at + size)
            outs[i][:, cols] = back[first : first + part].astype(BF16)
        if extra:
            row = back[n * base + i : n * base + i + 1]
            fold(ext32.at[i], row, size // LANES, at // LANES, part)


def expert_kernel(n, base, extra, stage, w_layout, v_layout, lengths, *refs):
    msgs = []
    for length in lengths:
        msgs.append(refs[:length])
        refs = refs[length:]
    w_pieces, refs = refs[: len(w_layout)], refs[len(w_layout) :]
    v_pieces, refs = refs[: len(v_layout)], refs[len(v_layout) :]
    if stage == "early":
        slope_late, partial_out, refs = refs[0], refs[1], refs[2:]
    else:
        outs, refs = refs[:n], refs[n:]
    g, ext32, slope, w, v, x, act, ext, row32, sem_x, sem_g, sem_e, sem_w, sem_v = refs
    width = w.shape[0]
    half_ff = w_layout[0][3]
    pieces = width // LANES
    full = n * base
    x_in = begin_rows(msgs, x, ext, 0, sem_x, sem_e)
    w_in = begin_weights(w_pieces, w_layout, w, sem_w)
    g_in = begin_rows(msgs, g, None, width, sem_g, sem_e)
    v_in = begin_weights(v_pieces, v_layout, v, sem_v)
    finish(x_in)
    if extra:
        put_extra(x, row32, ext, n, base, 0)
    for block in sorted(w_in):
        finish(w_in[block])
        for at in range(block * half_ff, (block + 1) * half_ff, TILE):
            value = silu_slope(jnp.dot(x[...], w[:, at : at + TILE], preferred_element_type=F32))
            if stage == "early" and block > 0:
                slope_late[:, at - half_ff : at - half_ff + TILE] = value
            else:
                slope[:, at : at + TILE] = value
    finish(g_in)
    if extra:
        put_extra(g, row32, ext, n, base, pieces)
    for block in sorted(v_in):
        finish(v_in[block])
        for at in range(block * half_ff, (block + 1) * half_ff, TILE):
            hid = jnp.dot(g[...], v[:, at : at + TILE], preferred_element_type=F32)
            act[:, at : at + TILE] = (hid * slope[:, at : at + TILE]).astype(BF16)
    ext32[...] = jnp.zeros_like(ext32)
    at, column = place_of(2 * pieces * extra, base)
    to, to_column = place_of(pieces * extra, ext32.shape[1])
    for i in range(n):
        holders = ext[i].astype(F32)[at : at + 1, column : column + LANES]
        ext32[i, to : to + 1, to_column : to_column + LANES] = holders
    hidden = act.shape[1]
    for at in range(0, width, TILE):
        cols = slice(at, at + TILE)
        back = lax.dot_general(
            act[...], w[cols, :hidden], (((1,), (1,)), ((), ())), preferred_element_type=F32
        )
        if stage == "early":
            partial_out[:, cols] = back
            continue
        put_back(outs, ext32, back, at, TILE, n, base, extra, width)
    if stage != "early":
        for i in range(n):
            outs[i][:, sides_of(base) * width :] = ext32[i].astype(BF16)


def middle_kernel(*refs):
    g, v_blocks, out = refs[0], refs[1:-1], refs[-1]
    half, block_ff = v_blocks[0].shape

    def work(here):
        for block, ref in enumerate(v_blocks):
            for at in range(0, block_ff, TILE):
                out[:, block * block_ff + at : block * block_ff + at + TILE] = jnp.dot(
                    g[:, here * half : (here + 1) * half],
                    ref[:, at : at + TILE],
                    preferred_element_type=F32,
                )

    core = lax.axis_index("expert") % 2
    for here in range(2):
        pl.when(core == here)(functools.partial(work, here))


def expert_middle(g, v_blocks):
    rows, (half, block_ff) = g.shape[0], v_blocks[0].shape
    vmem = pl.BlockSpec(memory_space=pltpu.VMEM)
    return pl.pallas_call(
        middle_kernel,
        out_shape=jax.ShapeDtypeStruct((rows, len(v_blocks) * block_ff), F32),
        in_specs=[vmem] * (1 + len(v_blocks)),
        out_specs=vmem,
        compiler_params=pltpu.CompilerParams(vmem_limit_bytes=24 * MIB),
        cost_estimate=pl.CostEstimate(
            flops=2 * rows * half * block_ff * len(v_blocks),
            bytes_accessed=2 * half * block_ff * len(v_blocks),
            transcendentals=0,
        ),
        name="expert_middle",
    )(g, *v_blocks)


def late_kernel(n, base, extra, blocks, w_layout, v_layout, *refs):
    w_pieces, refs = refs[: len(w_layout)], refs[len(w_layout) :]
    v_pieces, refs = refs[: len(v_layout)], refs[len(v_layout) :]
    slope, partial, g, folded, half_hid, refs = refs[0], refs[1], refs[2], refs[3], refs[4], refs[5:]
    outs, (act, ext32) = refs[:n], refs[n:]
    width = g.shape[1]
    half, block_ff = width // 2, v_layout[0][3]
    core = lax.axis_index("expert") % 2
    ext32[...] = folded[...]

    def work(here):
        for block in range(blocks):
            for at in range(0, block_ff, TILE):
                cols = slice(block * block_ff + at, block * block_ff + at + TILE)
                hid = half_hid[:, cols]
                for ref, (of, other, row, _) in zip(v_pieces, v_layout):
                    if of == block:
                        first = (1 - here if other else here) * half + row
                        hid = hid + jnp.dot(
                            g[:, first : first + ref.shape[0]],
                            ref[:, at : at + TILE],
                            preferred_element_type=F32,
                        )
                act[:, cols] = (hid * slope[:, cols]).astype(BF16)
        places = {}
        for ref, (of, other, row, _) in zip(w_pieces, w_layout):
            for at in range(0, ref.shape[0], TILE):
                size = min(TILE, ref.shape[0] - at)
                first = (1 - here if other else here) * half + row + at
                places.setdefault((first, size), []).append((of, ref, at))
        for (first, size), terms in sorted(places.items()):
            cols = slice(first, first + size)
            back = partial[:, cols]
            for of, ref, at in terms:
                back = back + lax.dot_general(
                    act[:, of * block_ff : (of + 1) * block_ff],
                    ref[at : at + size, :],
                    (((1,), (1,)), ((), ())),
                    preferred_element_type=F32,
                )
            put_back(outs, ext32, back, first, size, n, base, extra, width)

    for here in range(2):
        pl.when(core == here)(functools.partial(work, here))
    for i in range(n):
        outs[i][:, sides_of(base) * width :] = ext32[i].astype(BF16)


def flat(columns):
    arrays, layout = [], []
    for block, cores in enumerate(columns):
        for other, pieces in enumerate(cores):
            row = 0
            for piece in pieces:
                arrays.append(piece)
                layout.append((block, other, row, piece.shape[1]))
                row += piece.shape[0]
    return arrays, layout, row


def expert_late(base, extra, w_columns, v_columns, carried):
    w_pieces, w_layout, half = flat(w_columns)
    carried = list(carried) + [expert_middle(carried[2], [own[0] for own, _ in v_columns])]
    v_pieces, v_layout, _ = flat([[[], other] for _, other in v_columns])
    width, ff = 2 * half, len(w_columns) * w_layout[0][3]
    rows, folded = carried[0].shape[0], carried[3].shape
    vmem = pl.BlockSpec(memory_space=pltpu.VMEM)
    back = jax.ShapeDtypeStruct(back_shape(base, width, extra), BF16)
    return pl.pallas_call(
        functools.partial(late_kernel, folded[0], base, extra, len(w_columns), w_layout, v_layout),
        out_shape=[back] * folded[0],
        in_specs=[vmem] * (len(w_pieces) + len(v_pieces) + len(carried)),
        out_specs=[vmem] * folded[0],
        scratch_shapes=[pltpu.VMEM((rows, ff), BF16), pltpu.VMEM(folded, F32)],
        compiler_params=pltpu.CompilerParams(vmem_limit_bytes=24 * MIB),
        cost_estimate=pl.CostEstimate(
            flops=4 * rows * width * ff,
            bytes_accessed=4 * width * ff + 8 * rows * width,
            transcendentals=0,
        ),
        name="expert_late",
    )(*w_pieces, *v_pieces, *carried)


def expert(msgs, base, extra, w_columns, v_columns, stage="whole"):
    n = len(msgs)
    lengths = [len(parts) for parts in msgs]
    most, parts = max(lengths), [part for message in msgs for part in message]
    w_pieces, w_layout, half = flat(w_columns)
    v_pieces, v_layout, _ = flat(v_columns)
    width, block_ff = 2 * half, w_layout[0][3]
    w_ff, v_ff = len(w_columns) * block_ff, len(v_columns) * block_ff
    rows = n * base + -(-n * extra // 16) * 16
    ext = fold_columns(2 * width // LANES * extra, base)
    back_rows, back_cols = back_shape(base, width, extra)
    anywhere, vmem = pl.BlockSpec(memory_space=pl.ANY), pl.BlockSpec(memory_space=pltpu.VMEM)
    spare = max(16, rows - n * base)
    kept = [((rows, width), BF16), ((n, back_rows, back_cols - sides_of(base) * width), F32)]
    if stage == "early":
        results = [((rows, w_ff - block_ff), F32), ((rows, width), F32)] + kept
    else:
        results = [((back_rows, back_cols), BF16)] * n
    return pl.pallas_call(
        functools.partial(expert_kernel, n, base, extra, stage, w_layout, v_layout, lengths),
        out_shape=[jax.ShapeDtypeStruct(*result) for result in results],
        in_specs=[anywhere] * (len(parts) + len(w_pieces) + len(v_pieces)),
        out_specs=[vmem] * len(results),
        scratch_shapes=[pltpu.VMEM(*shape) for shape in (kept if stage != "early" else [])]
        + [
            pltpu.VMEM((rows, v_ff), F32),
            pltpu.VMEM((width, w_ff), BF16),
            pltpu.VMEM((width, v_ff), BF16),
            pltpu.VMEM((rows, width), BF16),
            pltpu.VMEM((rows, v_ff), BF16),
            pltpu.VMEM((n, base, ext), BF16),
            pltpu.VMEM((spare, width), F32),
            pltpu.SemaphoreType.DMA((n, most)),
            pltpu.SemaphoreType.DMA((n, most)),
            pltpu.SemaphoreType.DMA((n, most)),
            pltpu.SemaphoreType.DMA((len(w_pieces),)),
            pltpu.SemaphoreType.DMA((len(v_pieces),)),
        ],
        compiler_params=pltpu.CompilerParams(vmem_limit_bytes=24 * MIB),
        cost_estimate=pl.CostEstimate(
            flops=0 if stage == "early" else 2 * rows * width * (w_ff + 2 * v_ff),
            bytes_accessed=0 if stage == "early" else 2 * width * (w_ff + v_ff) + 6 * rows * width,
            transcendentals=0 if stage == "early" else rows * w_ff,
        ),
        name="expert_" + stage,
    )(*parts, *w_pieces, *v_pieces)


def add_kernel(n, base, extra, start_ref, *refs):
    msgs, (out_hbm, out, rows, row32, places, sem_b, sem_o) = refs[:n], refs[n:]
    tokens, width = start_ref.shape
    pieces = width // LANES
    part, sides = msgs[0].shape[0], sides_of(base)
    rows_in = []
    for i, msg in enumerate(msgs):
        for side in range(sides):
            src = msg.at[:, pl.ds(side * width, width)]
            dst = rows.at[pl.ds(i * base + side * part, part), :]
            rows_in.append(begin(src, dst, sem_b.at[i, side]))
    ext = [msg[:, sides * width :] for msg in msgs]
    folded = jnp.zeros((tokens, 16), F32)
    at, column = place_of(pieces * extra, part)
    for i in range(n):
        holders = ext[i].astype(F32)[at : at + 1, column : column + LANES]
        token = lax.broadcasted_iota(jnp.int32, (tokens, LANES), 0) + 1
        place = jnp.where(holders == token.astype(F32), 1.0, 0.0)
        places[:, i * base : (i + 1) * base] = place[:, :base].astype(BF16)
        if extra:
            mine = lax.broadcasted_iota(jnp.int32, (tokens, 16), 1) == i
            folded = folded + jnp.where(mine, place[:, base : base + 1], 0.0)
    if extra:
        places[:, n * base :] = folded.astype(BF16)
        put_extra(rows, row32, ext, n, base, 0)
    place = places[...]
    finish(rows_in)
    step = width // PIECES
    sent = []
    for h in range(PIECES):
        for at in range(h * step, (h + 1) * step, TILE):
            cols = slice(at, min(at + TILE, (h + 1) * step))
            back = jnp.dot(place, rows[:, cols], preferred_element_type=F32)
            out[:, cols] = (start_ref[:, cols].astype(F32) + back).astype(out.dtype)
        cols = pl.ds(h * step, step)
        sent.append(begin(out.at[:, cols], out_hbm.at[:, cols], sem_o.at[h]))
    finish(sent)


def add_returned(start, msgs, base, extra, kind, name):
    tokens, width = start.shape
    n = len(msgs)
    slots = n * base + 16 * extra
    sides = sides_of(base)
    anywhere, vmem = pl.BlockSpec(memory_space=pl.ANY), pl.BlockSpec(memory_space=pltpu.VMEM)
    return pl.pallas_call(
        functools.partial(add_kernel, n, base, extra),
        out_shape=jax.ShapeDtypeStruct((tokens, width), kind),
        in_specs=[vmem] * (1 + n),
        out_specs=anywhere,
        scratch_shapes=[
            pltpu.VMEM((tokens, width), kind),
            pltpu.VMEM((slots, width), BF16),
            pltpu.VMEM((16, width), F32),
            pltpu.VMEM((tokens, slots), BF16),
            pltpu.SemaphoreType.DMA((n, sides)),
            pltpu.SemaphoreType.DMA((PIECES,)),
        ],
        compiler_params=pltpu.CompilerParams(vmem_limit_bytes=24 * MIB),
        cost_estimate=pl.CostEstimate(
            flops=2 * slots * tokens * width,
            bytes_accessed=2 * slots * width + 6 * tokens * width,
            transcendentals=0,
        ),
        name=name,
    )(start, *msgs)


def swap(value, axis, apart):
    return lax.ppermute(value, axis, [(i, i ^ apart) for i in range(lax.axis_size(axis))])


def swap_back(value, apart):
    sections, places = lax.axis_size("section"), lax.axis_size("expert")
    pairs = [
        (s * places + i, (s ^ 1) * places + (i ^ apart)) for s in range(sections) for i in range(places)
    ]
    return lax.ppermute(value, ("section", "expert"), pairs)


def after(*values):
    return lax.optimization_barrier(values)


def cut(weight):
    step = -(-weight.shape[0] // (LANES * CUTS)) * LANES
    return [weight[at : at + step] for at in range(0, weight.shape[0], step)]


def groups_of(experts):
    if experts == 4:
        return [[2], [1, 0], [3]], [[1, 2], [0, 3]]
    order = list(range(experts - 1, -1, -1))
    size = -(-experts // 4)
    groups = [order[i : i + size] for i in range(0, experts, size)]
    return groups, groups


def body(tokens, grad_out, expert_ids, gate_values, w_in, w_out_t):
    tok, grad = tokens[0], grad_out[0]
    ids_t, gates_t = expert_ids[0].T, gate_values[0].T
    experts = lax.axis_size("expert") // 2
    base, extra = slots_of(tok.shape[0], ids_t.shape[0], experts)
    sends, works = groups_of(experts)
    others = range(1, lax.axis_size("dp"))
    w_own, v_own = w_in[0, 0], w_out_t[0, 0]
    sent = [
        dispatch(group, base, extra, ids_t, gates_t, tok, grad, 24 if i else LIMIT, i < len(sends) - 1)
        for i, group in enumerate(sends)
    ]
    w_far = [swap(w_own, "dp", apart) for apart in others]
    w_other, v_other = swap(w_own, "expert", 1), swap(v_own, "expert", 1)
    other_grad = swap(grad, "section", 1)
    v_late, w_other, v_other = after(v_own, w_other, v_other)
    v_far = [swap(v_late, "dp", apart) for apart in others]
    sent[-1], other_grad = after(sent[-1], other_grad)
    got = {}
    for group, msgs in zip(sends, sent):
        for dist, msg in zip(group, msgs):
            got[dist] = tuple(swap(part, "expert", 2 * dist) for part in msg) if dist else msg
    first, last = [dist for group in sends[:-1] for dist in group], sends[-1]

    w_far, heads = after(w_far, [got[dist] for dist in first])
    got.update(zip(first, heads))
    w_columns = [[[w_own], [w_other]]]
    w_columns += [[[block], [swap(piece, "expert", 1) for piece in cut(block)]] for block in w_far]
    v_columns = [[[v_own], [v_other]]]
    carried = expert([got[dist] for dist in works[0]], base, extra, w_columns, v_columns, "early")
    v_far, tails, carried = after(v_far, [got[dist][0] for dist in last], carried)
    got.update((dist, (tail,) + got[dist][1:]) for dist, tail in zip(last, tails))
    v_columns += [[[block], [swap(block, "expert", 1)]] for block in v_far]

    total = other_grad
    for i, group in enumerate(works):
        msgs = [got[dist] for dist in group]
        if i == 0:
            backs = expert_late(base, extra, w_columns[1:], v_columns[1:], carried)
            backs, heads = after(backs, {dist: parts[:1] for dist, parts in got.items()})
            got = {dist: heads[dist] + parts[1:] for dist, parts in got.items()}
        else:
            backs = expert(msgs, base, extra, w_columns, v_columns)
        returned = [swap_back(back, 2 * dist) for dist, back in zip(group, backs)]
        ends = i == len(works) - 1
        total = add_returned(total, returned, base, extra, BF16 if ends else F32, "finish" if ends else "settle")
    return total[None]


def solution(mesh):
    rows = P("section", ("expert", "dp"), None)
    weights = P("section", "expert", None, "dp")
    return jax.shard_map(
        body,
        mesh=mesh,
        in_specs=(rows, rows, rows, rows, weights, weights),
        out_specs=rows,
        check_vma=False,
    )
```
